32 devices in a mesh: dp: 8 (over z, y), seq: 4 (over x, core).
Axes of the slice: x: 2, y: 2, z: 4, core: 2. Of those that a mesh axis runs over, the one named last changes fastest.
Arguments:
- cells: bfloat16 [16, 1280, 1120], P('dp', 'seq'), may hold values from -6 to 6
- prefix_len: int32 [16], P('dp'), may hold values from 0 to 4
- ln1_gain: float32 [1120], replicated, may hold values from 0.5 to 1.5
- ln1_bias: float32 [1120], replicated, may hold values from -1.5 to 1.5
- w_qkv: bfloat16 [1120, 3360], replicated, may hold values from -0.1875 to 0.1875
- bias_q: float32 [1120], replicated, may hold values from -1.5 to 1.5
- bias_v: float32 [1120], replicated, may hold values from -1.5 to 1.5
- w_out: bfloat16 [1120, 1120], replicated, may hold values from -3 to 3
- bias_out: float32 [1120], replicated, may hold values from -1.5 to 1.5
- ln2_gain: float32 [1120], replicated, may hold values from 0.5 to 1.5
- ln2_bias: float32 [1120], replicated, may hold values from -1.5 to 1.5
- w_up: bfloat16 [1120, 4480], replicated, may hold values from -0.1875 to 0.1875
- bias_up: float32 [4480], replicated, may hold values from -1.5 to 1.5
- w_down: bfloat16 [4480, 1120], replicated, may hold values from -0.09375 to 0.09375
- bias_down: float32 [1120], replicated, may hold values from -1.5 to 1.5
- cotangent: bfloat16 [16, 1280, 1120], P('dp', 'seq'), may hold values from -6 to 6
Outputs:
- block_out: bfloat16 [16, 1280, 1120], P('dp', 'seq')
- grad_cells: bfloat16 [16, 1280, 1120], P('dp', 'seq')
- grad_ln1_gain: float32 [1120], replicated
- grad_ln1_bias: float32 [1120], replicated
- grad_w_qkv: float32 [1120, 3360], P('seq')
- grad_bias_q: float32 [1120], replicated
- grad_bias_v: float32 [1120], replicated
- grad_w_out: float32 [1120, 1120], P('seq')
- grad_bias_out: float32 [1120], replicated
- grad_ln2_gain: float32 [1120], replicated
- grad_ln2_bias: float32 [1120], replicated
- grad_w_up: float32 [1120, 4480], P('seq', 'dp')
- grad_bias_up: float32 [4480], replicated
- grad_w_down: float32 [4480, 1120], P('dp', 'seq')
- grad_bias_down: float32 [1120], replicated
The draws below stay inside these ranges and needn't reach their ends.
All inputs are finite; a program needn't handle non-finite values.
Results may differ from the reference program's by a relative error of at most 0.012.
Values may be sent and summed in bfloat16 or wider, within the bound.
A program may use at most 320 MiB of HBM per device.

```python
import jax
import jax.numpy as jnp
from jax import lax

D = 1120
H = 20
HD = 56
FF = 4480
LEN = 1280
CELLS = 16


def touch_ends(values, rng, least, largest):
    shape = values.shape
    spot = [jax.random.randint(jax.random.fold_in(rng, axis), (), 0, shape[axis]) for axis in range(len(shape))]
    values = values.at[tuple(spot)].set(least)
    longest = shape.index(max(shape))
    spot[longest] = (spot[longest] + 1) % shape[longest]
    return values.at[tuple(spot)].set(largest)


def block_levels(stream_key, shape, shards, low, largest):
    factor_of = 1.0
    for dim, parts in shards:
        draws = jax.random.uniform(jax.random.fold_in(jax.random.fold_in(stream_key, 6), dim), (parts,), jnp.float32, low / len(shards), largest / len(shards))
        factor_of = factor_of * jnp.repeat(jnp.exp(draws), shape[dim] // parts).reshape((-1,) + (1,) * (len(shape) - 1 - dim))
    return factor_of


def scatter_about(key, dims, scale, bound, split=(), kind=jnp.bfloat16):
    values = jax.random.normal(key, dims, jnp.float32) * scale
    if len(split) > 0:
        values = block_levels(key, dims, split, -0.22, 0.18) * values
    return jnp.clip(values, min=-bound, max=bound).astype(kind)


def setup_inputs(seed: int = 0) -> dict:
    splits = jax.random.split(jax.random.key(seed), 17)
    return {
        "cells": scatter_about(splits[0], (CELLS, LEN, D), 1.0, 6.0, ((0, 8), (1, 4))),
        "prefix_len": touch_ends(jax.random.randint(splits[1], (CELLS,), 0, 5), jax.random.fold_in(splits[1], 1), 0, 4).astype(jnp.int32),
        "ln1_gain": jnp.clip(1.0 + 0.1 * jax.random.normal(splits[2], (D,), jnp.float32), 0.5, 1.5),
        "ln1_bias": scatter_about(splits[3], (D,), 0.3, 1.5, (), jnp.float32),
        "w_qkv": scatter_about(splits[4], (D, 3 * D), D ** -0.5, 0.1875),
        "bias_q": scatter_about(splits[5], (D,), 0.3, 1.5, (), jnp.float32),
        "bias_v": scatter_about(splits[6], (D,), 0.3, 1.5, (), jnp.float32),
        "w_out": scatter_about(splits[7], (D, D), (max(D // 256, 1)) ** -0.5, 3.0),
        "bias_out": scatter_about(splits[8], (D,), 0.3, 1.5, (), jnp.float32),
        "ln2_gain": jnp.clip(1.0 + 0.1 * jax.random.normal(splits[9], (D,), jnp.float32), 0.5, 1.5),
        "ln2_bias": scatter_about(splits[10], (D,), 0.3, 1.5, (), jnp.float32),
        "w_up": scatter_about(splits[11], (D, FF), D ** -0.5, 0.1875),
        "bias_up": scatter_about(splits[12], (FF,), 0.3, 1.5, (), jnp.float32),
        "w_down": scatter_about(splits[13], (FF, D), FF ** -0.5, 0.09375),
        "bias_down": scatter_about(splits[14], (D,), 0.3, 1.5, (), jnp.float32),
        "cotangent": scatter_about(splits[15], (CELLS, LEN, D), 1.0, 6.0, ((0, 8), (1, 4))),
    }


@jax.custom_vjp
def low(v):
    return lax.optimization_barrier(v.astype(jnp.bfloat16)).astype(jnp.float32)

@jax.custom_vjp
def low_back(v):
    return v

def low_keep(v):
    return (low(v), None)

def low_pass(kept, grad):
    return (grad,)

def back_keep(v):
    return (v, None)

def back_low(kept, grad):
    return (low(grad),)
low.defvjp(low_keep, low_pass)
low_back.defvjp(back_keep, back_low)
epsilon = 1e-05
highest = lax.Precision.HIGHEST

def layer_norm(values_in, norm_gain, norm_shift):
    row_mean = lax.optimization_barrier(jnp.mean(values_in, axis=-1, keepdims=True))
    centred = values_in - row_mean
    variance = lax.optimization_barrier(jnp.mean(centred * centred, axis=-1, keepdims=True))
    return centred * lax.rsqrt(variance + epsilon) * norm_gain + norm_shift

def matmul(left_side, right_side):
    return jnp.dot(left_side, right_side, precision=highest)

def attend(queries, key_heads, values, prefix):
    length = queries.shape[0]
    row_index = jnp.arange(length)[:, None]
    col_index = jnp.arange(length)[None, :]
    allowed = (col_index <= row_index) | (col_index < prefix) & (row_index < prefix)
    scores = low_back(jnp.einsum('qhd,khd->hqk', queries, key_heads, precision=highest) * HD ** (-0.5))
    scores = jnp.where(allowed[None], scores, -1e+30)
    softmax_val = jax.nn.softmax(scores, axis=-1)
    return jnp.einsum('hqk,khd->qhd', low(softmax_val), values, precision=highest)

def cell_forward(params, one_cell, prefix):
    ln1_gain, ln1_bias, w_qkv, bias_q, bias_v, w_out, bias_out, ln2_gain, ln2_bias, w_up, bias_up, w_down, bias_down = params
    length = one_cell.shape[0]
    normed = low(layer_norm(one_cell, ln1_gain, ln1_bias))
    projected = matmul(normed, w_qkv)
    queries = low(low_back(projected[:, :D] + bias_q))
    key_heads = low(low_back(projected[:, D:2 * D]))
    values = low(low_back(projected[:, 2 * D:] + bias_v))
    head_shape = (length, H, HD)
    head_out = attend(queries.reshape(head_shape), key_heads.reshape(head_shape), values.reshape(head_shape), prefix)
    head_out = low(low_back(head_out.reshape(length, D)))
    branch = low_back(matmul(head_out, w_out) + bias_out)
    middle = one_cell + branch
    second = low(layer_norm(middle, ln2_gain, ln2_bias))
    hidden_pre = low_back(matmul(second, w_up) + bias_up)
    hidden = low(jax.nn.gelu(hidden_pre))
    return middle + low_back(matmul(hidden, w_down) + bias_down)

def reference(cells, prefix_len, ln1_gain, ln1_bias, w_qkv, bias_q, bias_v, w_out, bias_out, ln2_gain, ln2_bias, w_up, bias_up, w_down, bias_down, cotangent):
    params = tuple((item.astype(jnp.float32) for item in (ln1_gain, ln1_bias, w_qkv, bias_q, bias_v, w_out, bias_out, ln2_gain, ln2_bias, w_up, bias_up, w_down, bias_down)))

    def scan_step(totals, packed):
        one_cell, prefix, one_cot = packed

        def forward_fn(prm_all, cell_in):
            return cell_forward(prm_all, cell_in, prefix)
        result, pullback = jax.vjp(forward_fn, params, one_cell.astype(jnp.float32))
        grad_parts, grad_cell = pullback(one_cot.astype(jnp.float32))
        totals = jax.tree.map(lambda total_val, new_val: total_val + new_val, totals, grad_parts)
        return (totals, (result.astype(jnp.bfloat16), grad_cell.astype(jnp.bfloat16)))
    zero_grads = jax.tree.map(jnp.zeros_like, params)
    totals, (block_out, grad_cells) = lax.scan(scan_step, zero_grads, (cells, prefix_len, cotangent))
    return (block_out, grad_cells, totals[0], totals[1], totals[2], totals[3], totals[4], totals[5], totals[6], totals[7], totals[8], totals[9], totals[10], totals[11], totals[12])
```

```python
import functools
import math
import jax
import jax.numpy as jnp
from jax import lax
from jax.experimental import pallas as pl
from jax.experimental.pallas import tpu as pltpu
from jax.sharding import PartitionSpec as P

H = 20
HD=56
F32=jnp.float32; BF=jnp.bfloat16
LOG2=math.log2(math.e)
NEG=-1e30
def nt(a,b): return lax.dot_general(a,b,(((1,),(1,)),((),())),preferred_element_type=F32)
def nn(a,b): return lax.dot_general(a,b,(((1,),(0,)),((),())),preferred_element_type=F32)
def tn(a,b): return lax.dot_general(a,b,(((0,),(0,)),((),())),preferred_element_type=F32)

def split3(v):
    a=v.astype(BF); r=v-a.astype(F32); b=r.astype(BF); r=r-b.astype(F32)
    return a.astype(F32),b.astype(F32),r

def dup(k):
    low=lax.broadcasted_iota(jnp.int32,k.shape,1)<64
    r=pltpu.roll(k,64,1)
    return jnp.where(low,k,r).astype(BF), jnp.where(low,r,k).astype(BF)

def fwd_kernel(B, prefix_ref, q_ref,k_ref,v_ref,o_ref,qa_ref):
    T=q_ref.shape[1]
    p=prefix_ref[pl.program_id(0)]
    lane=lax.broadcasted_iota(jnp.int32,(T,128),1); low=lane<64
    q=q_ref[0].astype(F32)*(HD**-0.5*LOG2)
    hi=q.astype(BF).astype(F32); res=pltpu.roll(q-hi,64,1)
    qa=[jnp.where(low,hi,res),jnp.where(low,res,hi)]
    qab=[x.astype(BF) for x in qa]
    ka=dup(k_ref[0].astype(F32))
    lane_b=lane[:B]
    row=lax.broadcasted_iota(jnp.int32,(B,B),0); col=lax.broadcasted_iota(jnp.int32,(B,B),1)
    tri=col<=row
    first=tri|((col<p)&(row<p))
    for i in range(T//B):
        n=(i+1)*B; rows=slice(i*B,n)
        outs=[]
        for h in range(2):
            s=nt(qab[h][rows],ka[h][:n])
            d=jnp.where(first if i==0 else tri,s[:,n-B:],NEG)
            if i: s=jnp.concatenate([s[:,:n-B],d],1)
            else: s=d
            m=jnp.max(s,axis=1,keepdims=True)
            e=jnp.exp2(s-m).astype(BF)
            o=nn(e,v_ref[0,:n])
            l=o[:,56+64*h:57+64*h]
            outs.append(o*(1.0/l))
            lse=-(m+jnp.log2(l))
            a,b,c=split3(lse)
            z=64*h+56
            x=jnp.where(lane_b==z,a,jnp.where(lane_b==z+1,b,jnp.where(lane_b==z+2,c,qa[h][rows])))
            qa_ref[0,rows,128*h:128*h+128]=x.astype(BF)
        o_ref[0,rows]=jnp.where(low[:B],outs[0],outs[1]).astype(BF)

def attention_forward(qkv,prefix,B=256):
    C,T,W=qkv.shape; NP=W//384
    spec=lambda off: pl.BlockSpec((1,T,128),lambda c,p,pr: (c,0,off+p))
    return pl.pallas_call(functools.partial(fwd_kernel,B),
        grid_spec=pltpu.PrefetchScalarGridSpec(num_scalar_prefetch=1,grid=(C,NP),
            in_specs=[spec(0),spec(NP),spec(2*NP)],
            out_specs=[pl.BlockSpec((1,T,128),lambda c,p,pr:(c,0,p)),pl.BlockSpec((1,T,256),lambda c,p,pr:(c,0,p))]),
        out_shape=[jax.ShapeDtypeStruct((C,T,128*NP),BF),jax.ShapeDtypeStruct((C,T,256*NP),BF)],
        compiler_params=pltpu.CompilerParams(vmem_limit_bytes=24<<20),
        cost_estimate=pl.CostEstimate(flops=C*NP*2*2*2*T*T*64,bytes_accessed=C*T*128*NP*12,transcendentals=C*NP*T*T),
        name="attention_forward",
    )(prefix,qkv,qkv,qkv)

def bwd_kernel(B, prefix_ref, qa_ref,q_ref,k_ref,v_ref,do_ref,o_ref,out_ref,dk_ref,dv_ref):
    T=q_ref.shape[1]; NP=pl.num_programs(1); W=out_ref.shape[2]
    pr=pl.program_id(1)
    p=prefix_ref[pl.program_id(0)]
    lane=lax.broadcasted_iota(jnp.int32,(T,128),1); low=lane<64
    k32=k_ref[0].astype(F32); q32=q_ref[0].astype(F32); do32=do_ref[0].astype(F32)
    ka=dup(k32)
    zero=jnp.zeros_like(k32)
    km=[jnp.where(low,k32,zero).astype(BF),jnp.where(low,zero,k32).astype(BF)]
    qm=[jnp.where(low,q32,zero).astype(BF),jnp.where(low,zero,q32).astype(BF)]
    dom=[jnp.where(low,do32,zero),jnp.where(low,zero,do32)]
    o32=o_ref[0].astype(F32)
    doa=[]
    for h in range(2):
        dl=-jnp.sum(dom[h]*o32,axis=1,keepdims=True)
        a,b,c=split3(dl); z=64*h+56
        doa.append(jnp.where(lane==z,a,jnp.where(lane==z+1,b,jnp.where(lane==z+2,c,dom[h]))).astype(BF))
    dom=[x.astype(BF) for x in dom]
    key=lax.broadcasted_iota(jnp.int32,(B,B),0); qry=lax.broadcasted_iota(jnp.int32,(B,B),1)
    tri=key<=qry
    first=tri|((key<p)&(qry<p))
    sc=HD**-0.5
    for i in reversed(range(T//B)):
        n=(i+1)*B; rows=slice(i*B,n)
        pbs=[];dss=[]
        for h in range(2):
            s=nt(ka[h][:n],qa_ref[0,rows,128*h:128*h+128])
            d=jnp.where(first if i==0 else tri,s[n-B:],NEG)
            s=jnp.concatenate([s[:n-B],d],0) if i else d
            e=jnp.exp2(s)
            dp=nt(v_ref[0,:n],doa[h][rows])
            dss.append((e*dp).astype(BF)); pbs.append(e.astype(BF))
        dq=tn(dss[0],km[0][:n])+tn(dss[1],km[1][:n])
        out_ref[0,rows,pl.ds(pl.multiple_of(pr*128,128),128)]=(dq*sc).astype(BF)
        dv=nn(pbs[0],dom[0][rows])+nn(pbs[1],dom[1][rows])
        dk=nn(dss[0],qm[0][rows])+nn(dss[1],qm[1][rows])
        if i==T//B-1:
            dv_ref[...]=dv; dk_ref[...]=dk
        else:
            dv_ref[:n]+=dv; dk_ref[:n]+=dk
    out_ref[0,:,pl.ds(pl.multiple_of((NP+pr)*128,128),128)]=(dk_ref[...]*sc).astype(BF)
    out_ref[0,:,pl.ds(pl.multiple_of((2*NP+pr)*128,128),128)]=dv_ref[...].astype(BF)
    if W>384*(W//384):
        @pl.when(pr==0)
        def _():
            out_ref[0,:,384*(W//384):]=jnp.zeros((T,W-384*(W//384)),BF)

def attention_backward(qkv,qa,do,o,prefix,width,B=256):
    C,T,W=qkv.shape; NP=W//384
    spec=lambda off: pl.BlockSpec((1,T,128),lambda c,p,pr: (c,0,off+p))
    return pl.pallas_call(functools.partial(bwd_kernel,B),
        grid_spec=pltpu.PrefetchScalarGridSpec(num_scalar_prefetch=1,grid=(C,NP),
            in_specs=[pl.BlockSpec((1,T,256),lambda c,p,pr:(c,0,p)),spec(0),spec(NP),spec(2*NP),spec(0),spec(0)],
            out_specs=pl.BlockSpec((1,T,width),lambda c,p,pr:(c,0,0)),
            scratch_shapes=[pltpu.VMEM((T,128),F32)]*2),
        out_shape=jax.ShapeDtypeStruct((C,T,width),BF),
        compiler_params=pltpu.CompilerParams(vmem_limit_bytes=40<<20),
        cost_estimate=pl.CostEstimate(flops=C*NP*2*5*2*T*T*64,bytes_accessed=C*T*128*NP*20,transcendentals=C*NP*T*T),
        name="attention_backward",
    )(prefix,qa,qkv,qkv,qkv,do,o)


epsilon = 1e-05


def rows_call(kernel, steps, row_ins, whole_ins, row_outs, sum_outs, flops, name, vmem=48):
    def row_spec(block_rows, width, first=0):
        return pl.BlockSpec((block_rows, width), lambda i: (i + first, 0))

    in_specs, args = [], []
    for array, block_rows, first in row_ins:
        in_specs.append(row_spec(block_rows, array.shape[1], first))
        args.append(array)
    for array in whole_ins:
        in_specs.append(pl.BlockSpec(array.shape, lambda i: (0, 0), pipeline_mode=pl.Buffered(1)))
        args.append(array)
    out_specs, out_shape = [], []
    for shape, dtype in row_outs:
        out_specs.append(row_spec(shape[0] // steps, shape[1]))
        out_shape.append(jax.ShapeDtypeStruct(shape, dtype))
    for shape in sum_outs:
        out_specs.append(pl.BlockSpec(shape, lambda i: (0, 0)))
        out_shape.append(jax.ShapeDtypeStruct(shape, F32))
    moved = sum(a.size * a.dtype.itemsize for a in args) + sum(o.size * o.dtype.itemsize for o in out_shape)
    return pl.pallas_call(
        kernel,
        grid=(steps,),
        in_specs=in_specs,
        out_specs=out_specs,
        out_shape=out_shape,
        compiler_params=pltpu.CompilerParams(vmem_limit_bytes=vmem << 20),
        cost_estimate=pl.CostEstimate(flops=flops, bytes_accessed=moved, transcendentals=0),
        name=name,
    )(*args)


def block_norm(rows):
    width = rows.shape[1]
    mean = jnp.sum(rows, axis=1, keepdims=True) * (1.0 / width)
    centred = rows - mean
    rstd = lax.rsqrt(jnp.sum(centred * centred, axis=1, keepdims=True) * (1.0 / width) + epsilon)
    return centred * rstd, rstd


def block_norm_back(grad, normed, rstd, gain):
    inv = 1.0 / grad.shape[1]
    dn = grad * gain
    a = jnp.sum(dn, axis=1, keepdims=True) * inv
    b = jnp.sum(dn * normed, axis=1, keepdims=True) * inv
    return rstd * (dn - a - normed * b)


def add_sums(ref, *rows):
    first = pl.program_id(0) == 0
    for k, v in enumerate(rows):
        total = jnp.sum(v, axis=0, keepdims=True)
        ref[k : k + 1] = jnp.where(first, total, ref[k : k + 1] + total)


def project_kernel(x_ref, g_ref, b_ref, w_ref, c_ref, first_ref, out_ref):
    n, _ = block_norm(x_ref[...].astype(F32))
    first = (n * g_ref[...] + b_ref[...]).astype(BF)
    first_ref[...] = first
    width = w_ref.shape[1]
    for lo in range(0, width, 640):
        cols = slice(lo, min(lo + 640, width))
        out_ref[:, cols] = (nn(first, w_ref[:, cols]) + c_ref[:, cols]).astype(BF)


def project(x, gain, shift, w, bias, steps):
    rows, d = x.shape
    m = rows // steps
    return rows_call(
        project_kernel, steps, [(x, m, 0)], [gain, shift, w, bias],
        [((rows, d), BF), ((rows, w.shape[1]), BF)], [], 2 * rows * w.size, "norm_project")


def middle_kernel(own_ref, got_ref, x_ref, w_ref, c_ref, g_ref, b_ref, middle_ref, second_ref):
    half = own_ref.shape[1]
    out = nn(own_ref[...], w_ref[:half]) + nn(got_ref[...], w_ref[half:])
    middle = x_ref[...].astype(F32) + out + c_ref[...]
    middle_ref[...] = middle
    n, _ = block_norm(middle)
    second_ref[...] = (n * g_ref[...] + b_ref[...]).astype(BF)


def attention_output(own, got, x, w, bias, gain, shift, steps):
    rows, d = x.shape
    m = rows // steps
    return rows_call(
        middle_kernel, steps, [(own, m, 0), (got, m, 0), (x, m, 0)], [w, bias, gain, shift],
        [((rows, d), F32), ((rows, d), BF)], [], 2 * rows * w.size, "attention_output")


def hidden_kernel(s_ref, cot_ref, wu_ref, bu_ref, wd_ref, act_ref, gpre_ref, out_ref, gsec_ref, sum_ref):
    width = wu_ref.shape[1]
    second, cot = s_ref[...], cot_ref[...]
    out = gsec = None
    a, b = 0.7978845608, 0.044715
    for lo in range(0, width, 640):
        cols = slice(lo, min(lo + 640, width))
        u = nn(second, wu_ref[:, cols]) + bu_ref[:, cols]
        gact = nt(cot, wd_ref[cols])
        u2 = u * u
        t = jnp.tanh(u * (a + a * b * u2))
        h = 0.5 + 0.5 * t
        act = (u * h).astype(BF)
        gpre = (gact * (h + u * (0.5 - 0.5 * t * t) * (a + 3 * a * b * u2))).astype(BF)
        act_ref[:, cols] = act
        gpre_ref[:, cols] = gpre
        total = jnp.sum(gpre.astype(F32), axis=0, keepdims=True)
        sum_ref[:, cols] = jnp.where(pl.program_id(0) == 0, total, sum_ref[:, cols] + total)
        o, g = nn(act, wd_ref[cols]), nt(gpre, wu_ref[:, cols])
        out, gsec = (o, g) if out is None else (out + o, gsec + g)
    out_ref[...] = out.astype(BF)
    gsec_ref[...] = gsec.astype(BF)


def hidden_layer(second, cot, wu, bu, wd, steps):
    rows, d = second.shape
    ff = wu.shape[1]
    m = rows // steps
    return rows_call(
        hidden_kernel, steps, [(second, m, 0), (cot, m, 0)], [wu, bu, wd],
        [((rows, ff), BF), ((rows, ff), BF), ((rows, d), BF), ((rows, d), BF)], [(1, ff)], 8 * rows * wu.size,
        "hidden_layer", 56)


def middle_back_kernel(
    gs_ref, gs_got_ref, o_ref, o_got_ref, middle_ref, cot_ref, w_ref, g_ref, c_ref,
    gm_ref, gb_ref, gatt_ref, block_ref, sum_ref,
):
    middle, gy = middle_ref[...], cot_ref[...].astype(F32)
    gsecond = gs_ref[...].astype(F32) + gs_got_ref[...].astype(F32)
    n, rstd = block_norm(middle)
    gmiddle = gy + block_norm_back(gsecond, n, rstd, g_ref[...])
    gm_ref[...] = gmiddle
    gbranch = gmiddle.astype(BF)
    gb_ref[...] = gbranch
    gatt_ref[...] = nt(gbranch, w_ref[...]).astype(BF)
    block_ref[...] = (middle + (o_ref[...].astype(F32) + o_got_ref[...].astype(F32)) + c_ref[...]).astype(BF)
    add_sums(sum_ref, gbranch.astype(F32), gsecond * n, gsecond, gy)


def middle_back(gsec, gsec_got, out, out_got, middle, cot, w, gain, bias, steps):
    rows, d = middle.shape
    m = rows // steps
    return rows_call(
        middle_back_kernel, steps,
        [(a, m, 0) for a in (gsec, gsec_got, out, out_got, middle, cot)], [w, gain, bias],
        [((rows, d), F32), ((rows, d), BF), ((rows, w.shape[0]), BF), ((rows, d), BF)], [(4, d)], 2 * rows * w.size,
        "middle_back")


def project_back_kernel(g_ref, w_ref, out_ref, sum_ref):
    g = g_ref[:, : w_ref.shape[1]]
    out_ref[...] = nt(g, w_ref[...]).astype(BF)
    add_sums(sum_ref, g.astype(F32))


def project_back(g, w, steps):
    rows = g.shape[0]
    return rows_call(
        project_back_kernel, steps, [(g, rows // steps, 0)], [w], [((rows, w.shape[0]), BF)], [(1, w.shape[1])],
        2 * rows * w.size, "project_back")


def cells_back_kernel(g_ref, got_ref, x_ref, gm_ref, gain_ref, out_ref, sum_ref):
    g = g_ref[...].astype(F32) + got_ref[...].astype(F32)
    n, rstd = block_norm(x_ref[...].astype(F32))
    out_ref[...] = (gm_ref[...] + block_norm_back(g, n, rstd, gain_ref[...])).astype(BF)
    add_sums(sum_ref, g * n, g)


def cells_back(g, got, x, gmiddle, gain, steps):
    rows, d = x.shape
    m = rows // steps
    return rows_call(
        cells_back_kernel, steps, [(a, m, 0) for a in (g, got, x, gmiddle)], [gain],
        [((rows, d), BF)], [(2, d)], 0, "cells_back")


def low(value):
    return lax.optimization_barrier(value.astype(BF))


def perm_bit(axis, bit):
    n = lax.axis_size(axis)
    return [(i, i ^ bit) for i in range(n)]


def swap(value, axis, bit):
    return lax.ppermute(value, axis, perm_bit(axis, bit))


def device_pairs(steps):
    ndp, nseq = lax.axis_size("dp"), lax.axis_size("seq")
    pairs = []
    for d in range(ndp):
        for s in range(nseq):
            axis, bit = steps[s % 2]
            e, t = (d, s ^ bit) if axis == "seq" else (d ^ bit, s)
            pairs.append((d * nseq + s, e * nseq + t))
    return pairs


def pick(array, index, axis):
    return lax.dynamic_index_in_dim(array, index, axis, keepdims=False)


def one_hot(rows, cols, source):
    r = lax.broadcasted_iota(jnp.int32, (rows, cols), 0)
    return (r == source[None, :]).astype(BF)


def halving_orders():
    nb = lax.axis_size("dp").bit_length() - 1
    dps = [("dp", 1 << b) for b in range(nb)]
    x = ("seq", 2)
    return [x] + dps, dps[:2] + [x] + dps[2:], dps[1:2] + [x] + dps[:1] + dps[2:]


def arrange(blocks, order_pair, me, core):
    n = blocks.shape[0]
    ndp = lax.axis_size("dp")

    def value(step):
        axis, bit = step
        return ndp if axis == "seq" else bit

    k = len(order_pair[0])
    out = []
    for j in range(n):
        rel = [0, 0]
        for c in (0, 1):
            for pos, step in enumerate(order_pair[c]):
                if j & (1 << (k - 1 - pos)):
                    rel[c] |= value(step)
        out.append(lax.dynamic_slice_in_dim(blocks, me ^ jnp.where(core == 0, rel[0], rel[1]), 1, 0))
    return jnp.concatenate(out[n // 2 :], 0), jnp.concatenate(out[: n // 2], 0)


def reduce_blocks(sent, kept, order_pair):
    k = len(order_pair[0])
    for step in range(k):
        got = lax.ppermute(sent, ("dp", "seq"), device_pairs((order_pair[0][step], order_pair[1][step])))
        if step == k - 1:
            return kept[0].astype(F32) + got[0].astype(F32)
        half = kept.shape[0] // 2
        sent = low(kept[half:].astype(F32) + got[half:].astype(F32))
        kept = low(kept[:half].astype(F32) + got[:half].astype(F32))


def gather_dp(piece, mydp):
    ndp = lax.axis_size("dp")
    held = piece[None]
    order = [0]
    bits = [1 << b for b in range(ndp.bit_length() - 1)]
    for bit in bits[::-1]:
        got = swap(held, "dp", bit)
        held = jnp.concatenate([held, got], 0)
        order = order + [o ^ bit for o in order]
    where = {o: i for i, o in enumerate(order)}
    table = jnp.array([where[o] for o in range(ndp)], jnp.int32)
    return jnp.concatenate(
        [lax.dynamic_slice_in_dim(held, table[mydp ^ d], 1, 0) for d in range(ndp)], 0
    )


def all_sum(value):
    value = swap(value, "seq", 1) + value
    value = swap(value, "seq", 2) + value
    bit = 1
    while bit < lax.axis_size("dp"):
        value = swap(value, "dp", bit) + value
        bit *= 2
    return value


def per_device(
    cells, prefix_len, ln1_gain, ln1_bias, w_qkv, bias_q, bias_v, w_out, bias_out,
    ln2_gain, ln2_bias, w_up, bias_up, w_down, bias_down, cotangent,
):
    seq, ndp = lax.axis_size("seq"), lax.axis_size("dp")
    s, dp = lax.axis_index("seq"), lax.axis_index("dp")
    core, xi = s % 2, s // 2
    assert seq == 4
    pairs, block, D = cells.shape
    C = pairs // 2
    T = block * seq
    HH = H // 2
    WH = HH * 64
    half = D // 2
    quarter = D // 4
    FF = w_up.shape[1]
    FH = FF // 2
    FB = FH // ndp
    R = 2 * C * block
    me = xi * ndp + dp

    def to_chip(a):
        mine = lax.dynamic_slice_in_dim(a, xi * C, C, 0)
        other = lax.dynamic_slice_in_dim(a, (1 - xi) * C, C, 0)
        return jnp.stack([mine, swap(other, "seq", 2)], 0)

    def place(own, partner):
        w = own.shape[-1]
        out = jnp.zeros((C, T, w), own.dtype)
        for piece, place_of in ((own[0], s), (own[1], s ^ 2), (partner[0], s ^ 1), (partner[1], s ^ 3)):
            out = lax.dynamic_update_slice(out, piece, (0, place_of * block, 0))
        return out

    def take_rows(a, first):
        return jnp.stack([
            lax.dynamic_slice_in_dim(a, first * block, block, 1),
            lax.dynamic_slice_in_dim(a, (first ^ 2) * block, block, 1),
        ], 0)

    def from_chip(own):
        got = swap(own[1], "seq", 2)
        lo = jnp.where(xi == 0, own[0], got)
        hi = jnp.where(xi == 0, got, own[0])
        return jnp.concatenate([lo, hi], 0)

    x_own = to_chip(cells)
    x_partner = swap(x_own, "seq", 1)
    cot_own = to_chip(cotangent)
    cot_partner = swap(cot_own, "seq", 1)
    prefix = lax.dynamic_slice_in_dim(prefix_len, xi * C, C, 0)

    col = jnp.arange(WH)
    head_col = jnp.where(col % 64 < HD, core * half + (col // 64) * HD + col % 64, -1)
    w_parts = []
    for j in range(3):
        lo = j * D // 128 * 128
        hi = min(-(-(j + 1) * D // 128) * 128, 3 * D)
        e = one_hot(hi - lo, WH, jnp.where(head_col >= 0, head_col + j * D - lo, -1))
        w_parts.append(jnp.dot(w_qkv[:, lo:hi], e, preferred_element_type=F32).astype(BF))
    w_own = jnp.concatenate(w_parts, 1)

    def pad_heads(v, ones):
        v = lax.dynamic_slice_in_dim(v, core * half, half, 0).reshape(HH, HD)
        return jnp.concatenate([v, jnp.full((HH, 3), ones, F32), jnp.zeros((HH, 5), F32)], 1).reshape(WH)

    bias_own = jnp.concatenate([pad_heads(bias_q, 0.0), pad_heads(jnp.zeros_like(bias_q), 1.0), pad_heads(bias_v, 1.0)])
    wo = w_out.reshape(2, HH, HD, D)
    wo = jnp.concatenate([wo, jnp.zeros((2, HH, 64 - HD, D), BF)], 2).reshape(2, WH, D)
    wo = jnp.where(core == 0, wo, wo[::-1]).reshape(2 * WH, D)
    wu = pick(w_up.reshape(D, ndp, 2, FB), core, 2).reshape(D, FH)
    bu = pick(bias_up.reshape(ndp, 2, FB), core, 1).reshape(FH)
    wd = pick(w_down.reshape(ndp, 2, FB, D), core, 1).reshape(FH, D)

    row = lambda v: v.reshape(1, -1)
    steps = R // block
    x_all = place(x_own, x_partner).reshape(C * T, D)
    first, qkv = project(x_all, row(ln1_gain), row(ln1_bias), w_own, row(bias_own), 2 * steps)
    qkv = qkv.reshape(C, T, 3 * WH)
    att, q_aug = attention_forward(qkv, prefix)
    att_own = take_rows(att, s).reshape(R, WH)
    att_got = swap(take_rows(att, s ^ 1), "seq", 1).reshape(R, WH)

    x_rows = x_own.reshape(R, D)
    middle, second_own = attention_output(
        att_own, att_got, x_rows, wo, row(bias_out), row(ln2_gain), row(ln2_bias), steps)
    second = jnp.concatenate([second_own, swap(second_own, "seq", 1)], 0)
    cot_rows = cot_own.reshape(R, D)
    cot = jnp.concatenate([cot_rows, cot_partner.reshape(R, D)], 0)

    act, gpre, out_part, gsec_part, bias_up_sum = hidden_layer(second, cot, wu, row(bu), wd, 2 * steps)
    gsec_got = swap(gsec_part[R:], "seq", 1)
    out_got = swap(out_part[R:], "seq", 1)

    def pad_model(v):
        z = jnp.zeros((v.shape[0], 640 - half), BF)
        return jnp.concatenate([v[:, :half], z, v[:, half:], z], 1)

    def weight_blocks(rows, cols):
        cols = pad_model(cols)
        parts = [
            low(lax.dot_general(rows, cols[:, 640 * i : 640 * i + 640], (((0,), (0,)), ((), ())), preferred_element_type=F32))
            for i in (0, 1)
        ]
        return jnp.stack(parts, 0).reshape(2 * ndp, FB, 640)

    order_a, order_b, order_c = halving_orders()
    down_pair, up_pair, att_pair = (order_a, order_b), (order_c, order_a), (order_b, order_c)
    down_sent, down_kept = arrange(weight_blocks(act, cot), down_pair, me, core)
    down_sum = reduce_blocks(down_sent, down_kept, down_pair)
    up_sent, up_kept = arrange(weight_blocks(gpre, second), up_pair, me, core)
    up_sum = reduce_blocks(up_sent, up_kept, up_pair)

    gmiddle, gbranch, gatt_rows, block_rows, sums2 = middle_back(
        gsec_part, gsec_got, out_part, out_got, middle, cot_rows, wo, row(ln2_gain), row(bias_down), steps)
    block_out = from_chip(block_rows.reshape(2, C, block, D))
    gatt_recv = swap(gatt_rows[:, WH:], "seq", 1)
    gatt = place(gatt_rows[:, :WH].reshape(2, C, block, WH), gatt_recv.reshape(2, C, block, WH))

    att_rows = jnp.concatenate([att_own, att_got], 1)
    g_out = low(lax.dot_general(att_rows, gbranch, (((0,), (0,)), ((), ())), preferred_element_type=F32))
    g_out = g_out.reshape(2, 2, WH // 2, D)
    g_out_own = pick(g_out, core, 1)
    g_out_recv = swap(pick(g_out, 1 - core, 1), "seq", 1)
    g_out = low(g_out_own.astype(F32) + g_out_recv[::-1].astype(F32))
    g_out = jnp.where(core == 0, g_out, g_out[::-1]).reshape(2 * ndp, WH // 2 // ndp, D)
    out_sent, out_kept = arrange(g_out, att_pair, me, core)
    out_sum = reduce_blocks(out_sent, out_kept, att_pair)

    gqkv = attention_backward(qkv, q_aug, gatt, att, prefix, -(-3 * WH // 256) * 256).reshape(C * T, -1)
    WP = gqkv.shape[1]
    g_qkv = low(lax.dot_general(first, gqkv, (((0,), (0,)), ((), ())), preferred_element_type=F32))
    g_qkv = g_qkv.reshape(2, half, ndp, WP // ndp).transpose(0, 2, 1, 3).reshape(2 * ndp, half, WP // ndp)
    qkv_sent, qkv_kept = arrange(g_qkv, down_pair, me, core)
    qkv_sum = reduce_blocks(qkv_sent, qkv_kept, down_pair)

    gfirst_part, sums_qkv = project_back(gqkv, w_own, 2 * steps)
    gfirst_part = gfirst_part.reshape(C, T, D)
    gfirst_own = take_rows(gfirst_part, s).reshape(R, D)
    gfirst_got = swap(take_rows(gfirst_part, s ^ 1), "seq", 1).reshape(R, D)
    gcells, sums1 = cells_back(gfirst_own, gfirst_got, x_rows, gmiddle, row(ln1_gain), steps)
    grad_cells = from_chip(gcells.reshape(2, C, block, D))

    unpad = lambda v: v.reshape(HH, 64)[:, :HD].reshape(half)
    own_half = lambda v: jnp.where(core == 0, jnp.concatenate([v, jnp.zeros_like(v)]), jnp.concatenate([jnp.zeros_like(v), v]))
    sums = sums_qkv[0]
    g_bias_up = bias_up_sum.reshape(ndp, 1, FB)
    zero_up = jnp.zeros_like(g_bias_up)
    g_bias_up = jnp.where(core == 0, jnp.concatenate([g_bias_up, zero_up], 1), jnp.concatenate([zero_up, g_bias_up], 1)).reshape(FF)
    terms = [
        sums1[0], sums1[1], own_half(unpad(sums[:WH])), own_half(unpad(sums[2 * WH : 3 * WH])),
        sums2[0], sums2[1], sums2[2], sums2[3], g_bias_up,
    ]
    packed = jnp.concatenate(terms)
    packed = all_sum(packed.reshape(-1, 128)).reshape(-1)
    shared = [packed[i * D : (i + 1) * D] for i in range(8)] + [packed[8 * D :]]

    down = down_sum[:, :half].reshape(FB, 2, quarter)
    up = up_sum[:, :half].reshape(FB, 2, quarter)
    pair = jnp.stack([down, up], 0)
    theirs = low(swap(low(pick(pair, 1 - core, 2)), "seq", 1)).astype(F32)
    ours = pick(pair, core, 2)
    both = jnp.where(core == 0, jnp.concatenate([ours, theirs], 1), jnp.concatenate([theirs, ours], 1))
    final_down = both[0]
    final_up = both[1].T

    q2 = low(qkv_sum).reshape(2, quarter, WP // ndp)
    q_theirs = swap(pick(q2, 1 - core, 0), "seq", 1)
    q_ours = pick(q2, core, 0)
    q_both = jnp.where(core == 0, jnp.stack([q_ours, q_theirs]), jnp.stack([q_theirs, q_ours]))
    q_full = gather_dp(q_both, dp)
    q_full = q_full.transpose(2, 1, 0, 3).reshape(quarter, 2, WP)[:, :, : 3 * WH].reshape(quarter, 2, 3, WH)
    e_out = one_hot(D, 2 * WH, jnp.where(jnp.arange(2 * WH) % 64 < HD, jnp.arange(2 * WH) // 64 * HD + jnp.arange(2 * WH) % 64, -1))
    final_qkv = jnp.concatenate(
        [
            lax.dot_general(q_full[:, :, j].reshape(quarter, 2 * WH), e_out, (((1,), (1,)), ((), ())), preferred_element_type=F32)
            for j in range(3)
        ],
        1,
    )
    o_full = gather_dp(low(out_sum), dp).reshape(HH // 2, 64, D)
    final_out = o_full[:, :HD].reshape(quarter, D).astype(F32)

    return (
        block_out, grad_cells, shared[0], shared[1], final_qkv, shared[2], shared[3], final_out,
        shared[4], shared[5], shared[6], final_up, shared[8], final_down, shared[7],
    )


def solution(mesh):
    rows = P("dp", "seq", None)
    return jax.shard_map(
        per_device,
        mesh=mesh,
        in_specs=(rows, P("dp")) + (P(),) * 13 + (rows,),
        out_specs=(rows, rows, P(), P(), P("seq", None), P(), P(), P("seq", None), P(), P(), P(), P("seq", "dp"), P(), P("dp", "seq"), P()),
        check_vma=False,
    )
```

```python
import functools
import math
import jax
import jax.numpy as jnp
from jax import lax
from jax.experimental import pallas as pl
from jax.experimental.pallas import tpu as pltpu
from jax.sharding import PartitionSpec as P

H = 20
HD=56
F32=jnp.float32; BF=jnp.bfloat16
LOG2=math.log2(math.e)
NEG=-1e30
def nt(a,b): return lax.dot_general(a,b,(((1,),(1,)),((),())),preferred_element_type=F32)
def nn(a,b): return lax.dot_general(a,b,(((1,),(0,)),((),())),preferred_element_type=F32)
def tn(a,b): return lax.dot_general(a,b,(((0,),(0,)),((),())),preferred_element_type=F32)

def split3(v):
    a=v.astype(BF); r=v-a.astype(F32); b=r.astype(BF); r=r-b.astype(F32)
    return a.astype(F32),b.astype(F32),r

def dup(k):
    low=lax.broadcasted_iota(jnp.int32,k.shape,1)<64
    r=pltpu.roll(k,64,1)
    return jnp.where(low,k,r).astype(BF), jnp.where(low,r,k).astype(BF)

def fwd_kernel(B, prefix_ref, q_ref,k_ref,v_ref,o_ref,qa_ref):
    T=q_ref.shape[1]
    p=prefix_ref[pl.program_id(0)]
    lane=lax.broadcasted_iota(jnp.int32,(T,128),1); low=lane<64
    q=q_ref[0].astype(F32)*(HD**-0.5*LOG2)
    hi=q.astype(BF).astype(F32); res=pltpu.roll(q-hi,64,1)
    qa=[jnp.where(low,hi,res),jnp.where(low,res,hi)]
    qab=[x.astype(BF) for x in qa]
    ka=dup(k_ref[0].astype(F32))
    lane_b=lane[:B]
    row=lax.broadcasted_iota(jnp.int32,(B,B),0); col=lax.broadcasted_iota(jnp.int32,(B,B),1)
    tri=col<=row
    first=tri|((col<p)&(row<p))
    for i in range(T//B):
        n=(i+1)*B; rows=slice(i*B,n)
        outs=[]
        for h in range(2):
            s=nt(qab[h][rows],ka[h][:n])
            d=jnp.where(first if i==0 else tri,s[:,n-B:],NEG)
            if i: s=jnp.concatenate([s[:,:n-B],d],1)
            else: s=d
            m=jnp.max(s,axis=1,keepdims=True)
            e=jnp.exp2(s-m).astype(BF)
            o=nn(e,v_ref[0,:n])
            l=o[:,56+64*h:57+64*h]
            outs.append(o*(1.0/l))
            lse=-(m+jnp.log2(l))
            a,b,c=split3(lse)
            z=64*h+56
            x=jnp.where(lane_b==z,a,jnp.where(lane_b==z+1,b,jnp.where(lane_b==z+2,c,qa[h][rows])))
            qa_ref[0,rows,128*h:128*h+128]=x.astype(BF)
        o_ref[0,rows]=jnp.where(low[:B],outs[0],outs[1]).astype(BF)

def attention_forward(qkv,prefix,B=256):
    C,T,W=qkv.shape; NP=W//384
    spec=lambda off: pl.BlockSpec((1,T,128),lambda c,p,pr: (c,0,off+p))
    return pl.pallas_call(functools.partial(fwd_kernel,B),
        grid_spec=pltpu.PrefetchScalarGridSpec(num_scalar_prefetch=1,grid=(C,NP),
            in_specs=[spec(0),spec(NP),spec(2*NP)],
            out_specs=[pl.BlockSpec((1,T,128),lambda c,p,pr:(c,0,p)),pl.BlockSpec((1,T,256),lambda c,p,pr:(c,0,p))]),
        out_shape=[jax.ShapeDtypeStruct((C,T,128*NP),BF),jax.ShapeDtypeStruct((C,T,256*NP),BF)],
        compiler_params=pltpu.CompilerParams(vmem_limit_bytes=24<<20),
        cost_estimate=pl.CostEstimate(flops=C*NP*2*2*2*T*T*64,bytes_accessed=C*T*128*NP*12,transcendentals=C*NP*T*T),
        name="attention_forward",
    )(prefix,qkv,qkv,qkv)

def bwd_kernel(B, prefix_ref, qa_ref,q_ref,k_ref,v_ref,go_ref,gg_ref,o_ref,out_ref,dk_ref,dv_ref,do_ref):
    T=q_ref.shape[1]; NP=pl.num_programs(1); W=out_ref.shape[2]
    block=T//4
    s=lax.axis_index("seq")
    for k,piece in enumerate((go_ref[0,0],go_ref[1,0],gg_ref[0,0],gg_ref[1,0])):
        place=s^(2*(k%2)+k//2)
        do_ref[pl.ds(pl.multiple_of(place*block,block),block)]=piece
    pr=pl.program_id(1)
    p=prefix_ref[pl.program_id(0)]
    lane=lax.broadcasted_iota(jnp.int32,(T,128),1); low=lane<64
    k32=k_ref[0].astype(F32); q32=q_ref[0].astype(F32); do32=do_ref[...].astype(F32)
    ka=dup(k32)
    zero=jnp.zeros_like(k32)
    km=[jnp.where(low,k32,zero).astype(BF),jnp.where(low,zero,k32).astype(BF)]
    qm=[jnp.where(low,q32,zero).astype(BF),jnp.where(low,zero,q32).astype(BF)]
    dom=[jnp.where(low,do32,zero),jnp.where(low,zero,do32)]
    o32=o_ref[0].astype(F32)
    doa=[]
    for h in range(2):
        dl=-jnp.sum(dom[h]*o32,axis=1,keepdims=True)
        a,b,c=split3(dl); z=64*h+56
        doa.append(jnp.where(lane==z,a,jnp.where(lane==z+1,b,jnp.where(lane==z+2,c,dom[h]))).astype(BF))
    dom=[x.astype(BF) for x in dom]
    key=lax.broadcasted_iota(jnp.int32,(B,B),0); qry=lax.broadcasted_iota(jnp.int32,(B,B),1)
    tri=key<=qry
    first=tri|((key<p)&(qry<p))
    sc=HD**-0.5
    for i in reversed(range(T//B)):
        n=(i+1)*B; rows=slice(i*B,n)
        pbs=[];dss=[]
        for h in range(2):
            s=nt(ka[h][:n],qa_ref[0,rows,128*h:128*h+128])
            d=jnp.where(first if i==0 else tri,s[n-B:],NEG)
            s=jnp.concatenate([s[:n-B],d],0) if i else d
            e=jnp.exp2(s)
            dp=nt(v_ref[0,:n],doa[h][rows])
            dss.append((e*dp).astype(BF)); pbs.append(e.astype(BF))
        dq=tn(dss[0],km[0][:n])+tn(dss[1],km[1][:n])
        out_ref[0,rows,pl.ds(pl.multiple_of(pr*128,128),128)]=(dq*sc).astype(BF)
        dv=nn(pbs[0],dom[0][rows])+nn(pbs[1],dom[1][rows])
        dk=nn(dss[0],qm[0][rows])+nn(dss[1],qm[1][rows])
        if i==T//B-1:
            dv_ref[...]=dv; dk_ref[...]=dk
        else:
            dv_ref[:n]+=dv; dk_ref[:n]+=dk
    out_ref[0,:,pl.ds(pl.multiple_of((NP+pr)*128,128),128)]=(dk_ref[...]*sc).astype(BF)
    out_ref[0,:,pl.ds(pl.multiple_of((2*NP+pr)*128,128),128)]=dv_ref[...].astype(BF)
    if W>384*(W//384):
        @pl.when(pr==0)
        def _():
            out_ref[0,:,384*(W//384):]=jnp.zeros((T,W-384*(W//384)),BF)

def attention_backward(qkv,qa,do,do_got,o,prefix,width,B=256):
    C,T,W=qkv.shape; NP=W//384
    spec=lambda off: pl.BlockSpec((1,T,128),lambda c,p,pr: (c,0,off+p))
    return pl.pallas_call(functools.partial(bwd_kernel,B),
        grid_spec=pltpu.PrefetchScalarGridSpec(num_scalar_prefetch=1,grid=(C,NP),
            in_specs=[pl.BlockSpec((1,T,256),lambda c,p,pr:(c,0,p)),spec(0),spec(NP),spec(2*NP),
                pl.BlockSpec((2,1,T//4,128),lambda c,p,pr:(0,c,0,p)),pl.BlockSpec((2,1,T//4,128),lambda c,p,pr:(0,c,0,NP+p)),spec(0)],
            out_specs=pl.BlockSpec((1,T,width),lambda c,p,pr:(c,0,0)),
            scratch_shapes=[pltpu.VMEM((T,128),F32)]*2+[pltpu.VMEM((T,128),BF)]),
        out_shape=jax.ShapeDtypeStruct((C,T,width),BF),
        compiler_params=pltpu.CompilerParams(vmem_limit_bytes=40<<20),
        cost_estimate=pl.CostEstimate(flops=C*NP*2*5*2*T*T*64,bytes_accessed=C*T*128*NP*20,transcendentals=C*NP*T*T),
        name="attention_backward",
    )(prefix,qa,qkv,qkv,qkv,do,do_got,o)


epsilon = 1e-05


def vmem(megabytes):
    return pltpu.CompilerParams(vmem_limit_bytes=megabytes << 20)


def whole(array):
    return pl.BlockSpec(array.shape, lambda *_: (0,) * array.ndim, pipeline_mode=pl.Buffered(1))


def cost(flops, *arrays):
    return pl.CostEstimate(
        flops=flops, bytes_accessed=sum(math.prod(a.shape) * a.dtype.itemsize for a in arrays), transcendentals=0)


def block_norm(rows):
    width = rows.shape[1]
    mean = jnp.sum(rows, axis=1, keepdims=True) * (1.0 / width)
    centred = rows - mean
    rstd = lax.rsqrt(jnp.sum(centred * centred, axis=1, keepdims=True) * (1.0 / width) + epsilon)
    return centred * rstd, rstd


def block_norm_back(grad, normed, rstd, gain):
    inv = 1.0 / grad.shape[1]
    dn = grad * gain
    a = jnp.sum(dn, axis=1, keepdims=True) * inv
    b = jnp.sum(dn * normed, axis=1, keepdims=True) * inv
    return rstd * (dn - a - normed * b)


def add_sums(ref, start, *rows):
    for k, v in enumerate(rows):
        total = jnp.sum(v, axis=0, keepdims=True)
        ref[k : k + 1] = jnp.where(start, total, ref[k : k + 1] + total)


def project_kernel(s_ref, a_ref, b_ref, c_ref, d_ref, g_ref, h_ref, w_ref, bias_ref, first_ref, out_ref):
    k = pl.program_id(1)
    x = jnp.where(k < 2, jnp.where(k == 0, a_ref[0].astype(F32), b_ref[0].astype(F32)),
                  jnp.where(k == 2, c_ref[0].astype(F32), d_ref[0].astype(F32)))
    n, _ = block_norm(x)
    first = (n * g_ref[...] + h_ref[...]).astype(BF)
    first_ref[0] = first
    width = w_ref.shape[1]
    for lo in range(0, width, 640):
        cols = slice(lo, min(lo + 640, width))
        out_ref[0, :, cols] = (nn(first, w_ref[:, cols]) + bias_ref[:, cols]).astype(BF)


def project(place, pieces, gain, shift, w, bias):
    cells, rows, d = pieces[0].shape
    width = w.shape[1]
    piece = pl.BlockSpec((1, rows, d), lambda c, k, s: (c, 0, 0))
    at = lambda c, k, s: (c, s[0] ^ k, 0)
    ins = (gain, shift, w, bias)
    outs = [jax.ShapeDtypeStruct((cells, 4 * rows, n), BF) for n in (d, width)]
    return pl.pallas_call(
        project_kernel,
        grid_spec=pltpu.PrefetchScalarGridSpec(
            num_scalar_prefetch=1, grid=(cells, 4), in_specs=[piece] * 4 + [whole(a) for a in ins],
            out_specs=[pl.BlockSpec((1, rows, n), at) for n in (d, width)]),
        out_shape=outs,
        compiler_params=vmem(40),
        cost_estimate=cost(8 * cells * rows * w.size, *pieces, *ins, *outs),
        name="norm_project",
    )(place, *pieces, *ins)


def middle_kernel(s_ref, own_ref, got_ref, a_ref, b_ref, w_ref, c_ref, g_ref, h_ref, middle_ref, second_ref):
    half = own_ref.shape[2]
    out = nn(own_ref[0], w_ref[:half]) + nn(got_ref[0], w_ref[half:])
    x = jnp.where(pl.program_id(0) == 0, a_ref[0].astype(F32), b_ref[0].astype(F32))
    middle = x + out + c_ref[...]
    middle_ref[...] = middle
    n, _ = block_norm(middle)
    second_ref[...] = (n * g_ref[...] + h_ref[...]).astype(BF)


def attention_output(place, own, got, x0, x1, w, bias, gain, shift):
    cells, rows, d = x0.shape
    half = own.shape[2]
    at = pl.BlockSpec((1, rows, half), lambda k, c, s: (c, s[0] ^ (2 * k), 0))
    piece = pl.BlockSpec((1, rows, d), lambda k, c, s: (c, 0, 0))
    ins = (w, bias, gain, shift)
    outs = [jax.ShapeDtypeStruct((2 * cells * rows, d), t) for t in (F32, BF)]
    return pl.pallas_call(
        middle_kernel,
        grid_spec=pltpu.PrefetchScalarGridSpec(
            num_scalar_prefetch=1, grid=(2, cells), in_specs=[at, at, piece, piece] + [whole(a) for a in ins],
            out_specs=[pl.BlockSpec((rows, d), lambda k, c, s: (k * cells + c, 0))] * 2),
        out_shape=outs,
        compiler_params=vmem(32),
        cost_estimate=cost(4 * cells * rows * w.size, x0, x0, *ins, *outs),
        name="attention_output",
    )(place, own, got, x0, x1, *ins)


CHUNK = 768


def hidden_window(core, ff):
    width = -(-(ff // 2) // CHUNK) * CHUNK
    return core * (ff - width), width, core * (width - ff // 2)


def hidden_kernel(
    ff, s0_ref, s1_ref, c0_ref, c1_ref, bu_ref, wu_hbm, wd_hbm,
    act_ref, gpre_ref, out0_ref, out1_ref, gs0_ref, gs1_ref, sum_ref, wu_ref, wd_ref, sem,
):
    i, n = pl.program_id(0), pl.num_programs(0) // 2
    core = lax.rem(lax.axis_index("seq"), 2)
    start, width, skip = hidden_window(core, ff)
    chunks = width // CHUNK

    def copies(k):
        at = pl.multiple_of(start + k * CHUNK, 128)
        cols = pl.ds(k * CHUNK, CHUNK)
        return (
            pltpu.make_async_copy(wu_hbm.at[:, pl.ds(at, CHUNK)], wu_ref.at[:, cols], sem.at[2 * k]),
            pltpu.make_async_copy(wd_hbm.at[:, pl.ds(at, CHUNK)], wd_ref.at[:, cols], sem.at[2 * k + 1]),
        )

    @pl.when(i == 0)
    def _():
        for k in range(chunks):
            for c in copies(k):
                c.start()

    second = jnp.where(i < n, s0_ref[...].astype(F32), s1_ref[...].astype(F32)).astype(BF)
    cot = jnp.where(i < n, c0_ref[...].astype(F32), c1_ref[...].astype(F32)).astype(BF)
    out = gsec = None
    a, b = 0.7978845608, 0.044715
    for k in range(chunks):
        cols = slice(k * CHUNK, (k + 1) * CHUNK)

        @pl.when(i == 0)
        def _():
            for c in copies(k):
                c.wait()

        u = nn(second, wu_ref[:, cols]) + bu_ref[:, pl.ds(pl.multiple_of(start + k * CHUNK, 128), CHUNK)]
        gact = nn(cot, wd_ref[:, cols])
        u2 = u * u
        t = jnp.tanh(u * (a + a * b * u2))
        h = 0.5 + 0.5 * t
        act = u * h
        gpre = gact * (h + u * (0.5 - 0.5 * t * t) * (a + 3 * a * b * u2))
        if k in (0, chunks - 1):
            col = lax.broadcasted_iota(jnp.int32, (1, CHUNK), 1) + k * CHUNK
            mine = (col >= skip) & (col < skip + ff // 2)
            act, gpre = jnp.where(mine, act, 0.0), jnp.where(mine, gpre, 0.0)
        act, gpre = act.astype(BF), gpre.astype(BF)
        act_ref[:, cols] = act
        gpre_ref[:, cols] = gpre
        total = jnp.sum(gpre.astype(F32), axis=0, keepdims=True)
        sum_ref[:, cols] = jnp.where(i == 0, total, sum_ref[:, cols] + total)
        o, g = nt(act, wd_ref[:, cols]), nt(gpre, wu_ref[:, cols])
        out, gsec = (o, g) if out is None else (out + o, gsec + g)

    @pl.when(i < n)
    def _():
        out0_ref[...] = out.astype(BF)
        gs0_ref[...] = gsec.astype(BF)

    @pl.when(i >= n)
    def _():
        out1_ref[...] = out.astype(BF)
        gs1_ref[...] = gsec.astype(BF)


def hidden_layer(second, second_got, cot, cot_got, w_up, bias_up, w_down_t, m):
    rows, d = second.shape
    ff = w_up.shape[1]
    n = rows // m
    width = hidden_window(0, ff)[1]
    lo = pl.BlockSpec((m, d), lambda i: (jnp.minimum(i, n - 1), 0))
    hi = pl.BlockSpec((m, d), lambda i: (jnp.maximum(i - n, 0), 0))
    row = pl.BlockSpec((m, width), lambda i: (i, 0))
    hbm = pl.BlockSpec(memory_space=pl.ANY)
    shape = jax.ShapeDtypeStruct
    outs = [shape((2 * rows, width), BF)] * 2 + [shape((rows, d), BF)] * 4 + [shape((1, width), F32)]
    return pl.pallas_call(
        functools.partial(hidden_kernel, ff),
        grid=(2 * n,),
        in_specs=[lo, hi, lo, hi, whole(bias_up), hbm, hbm],
        out_specs=[row, row, lo, hi, lo, hi, pl.BlockSpec((1, width), lambda i: (0, 0))],
        out_shape=outs,
        scratch_shapes=[pltpu.VMEM((d, width), BF), pltpu.VMEM((d, width), BF), pltpu.SemaphoreType.DMA((2 * (width // CHUNK),))],
        compiler_params=vmem(56),
        cost_estimate=cost(16 * rows * d * width, second, second, cot, cot, w_up, *outs),
        name="hidden_layer",
    )(second, second_got, cot, cot_got, bias_up, w_up, w_down_t)


def middle_back_kernel(
    gs_ref, gs_got_ref, o_ref, o_got_ref, middle_ref, cot_ref, w_ref, g_ref, c_ref,
    gm_ref, gb_ref, gatt_ref, block_ref, sum_ref,
):
    middle, gy = middle_ref[...], cot_ref[...].astype(F32)
    gsecond = gs_ref[...].astype(F32) + gs_got_ref[...].astype(F32)
    n, rstd = block_norm(middle)
    gmiddle = gy + block_norm_back(gsecond, n, rstd, g_ref[...])
    gm_ref[...] = gmiddle
    gbranch = gmiddle.astype(BF)
    gb_ref[...] = gbranch
    gatt_ref[...] = nt(gbranch, w_ref[...]).astype(BF)
    block_ref[...] = (middle + (o_ref[...].astype(F32) + o_got_ref[...].astype(F32)) + c_ref[...]).astype(BF)
    add_sums(sum_ref, pl.program_id(0) == 0, gbranch.astype(F32), gsecond * n, gsecond, gy)


def middle_back(gsec, gsec_got, out, out_got, middle, cot, w, gain, bias, m):
    rows, d = middle.shape
    row = lambda n: pl.BlockSpec((m, n), lambda i: (i, 0))
    ins = (gsec, gsec_got, out, out_got, middle, cot, w, gain, bias)
    shape = jax.ShapeDtypeStruct
    heads = w.shape[0]
    outs = [shape((rows, d), F32), shape((rows, d), BF), shape((rows, heads), BF), shape((rows, d), BF), shape((4, d), F32)]
    return pl.pallas_call(
        middle_back_kernel,
        grid=(rows // m,),
        in_specs=[row(d)] * 6 + [whole(a) for a in ins[6:]],
        out_specs=[row(d), row(d), row(heads), row(d), pl.BlockSpec((4, d), lambda i: (0, 0))],
        out_shape=outs,
        compiler_params=vmem(40),
        cost_estimate=cost(2 * rows * w.size, *ins, *outs),
        name="middle_back",
    )(*ins)


def project_back_kernel(g_ref, w_ref, out_ref, sum_ref):
    g = g_ref[:, : w_ref.shape[1]]
    out_ref[...] = nt(g, w_ref[...]).astype(BF)
    add_sums(sum_ref, pl.program_id(0) == 0, g.astype(F32))


def project_back(g, w, m):
    rows = g.shape[0]
    d, width = w.shape
    outs = [jax.ShapeDtypeStruct((rows, d), BF), jax.ShapeDtypeStruct((1, width), F32)]
    return pl.pallas_call(
        project_back_kernel,
        grid=(rows // m,),
        in_specs=[pl.BlockSpec((m, g.shape[1]), lambda i: (i, 0)), whole(w)],
        out_specs=[pl.BlockSpec((m, d), lambda i: (i, 0)), pl.BlockSpec((1, width), lambda i: (0, 0))],
        out_shape=outs,
        compiler_params=vmem(32),
        cost_estimate=cost(2 * rows * w.size, g, w, *outs),
        name="project_back",
    )(g, w)


def cells_back_kernel(s_ref, g_ref, got_ref, a_ref, b_ref, gm_ref, gain_ref, out_ref, sum_ref):
    k = pl.program_id(0)
    g = g_ref[0].astype(F32) + got_ref[0].astype(F32)
    n, rstd = block_norm(jnp.where(k == 0, a_ref[0].astype(F32), b_ref[0].astype(F32)))
    out_ref[0, 0] = (gm_ref[...] + block_norm_back(g, n, rstd, gain_ref[...])).astype(BF)
    add_sums(sum_ref, (k == 0) & (pl.program_id(1) == 0), g * n, g)


def cells_back(place, g, got, x0, x1, gmiddle, gain):
    cells, rows, d = x0.shape
    at = pl.BlockSpec((1, rows, d), lambda k, c, s: (c, s[0] ^ (2 * k), 0))
    piece = pl.BlockSpec((1, rows, d), lambda k, c, s: (c, 0, 0))
    outs = [jax.ShapeDtypeStruct((2, cells, rows, d), BF), jax.ShapeDtypeStruct((2, d), F32)]
    return pl.pallas_call(
        cells_back_kernel,
        grid_spec=pltpu.PrefetchScalarGridSpec(
            num_scalar_prefetch=1, grid=(2, cells),
            in_specs=[at, at, piece, piece, pl.BlockSpec((rows, d), lambda k, c, s: (k * cells + c, 0)), whole(gain)],
            out_specs=[pl.BlockSpec((1, 1, rows, d), lambda k, c, s: (k, c, 0, 0)), pl.BlockSpec((2, d), lambda k, c, s: (0, 0))]),
        out_shape=outs,
        compiler_params=vmem(32),
        cost_estimate=cost(0, x0, x0, x0, x0, x0, x0, gmiddle, *outs),
        name="cells_back",
    )(place, g, got, x0, x1, gmiddle, gain)


def store_block(orders, rel, value, sent_ref, kept_ref):
    core = lax.rem(lax.axis_index("seq"), 2)
    half = kept_ref.shape[0]
    places = [
        sum(jnp.where(rel & step != 0, half >> k, 0) for k, step in enumerate(steps)) for steps in orders
    ]
    pos = jnp.where(core == 0, places[0], places[1])

    @pl.when(pos >= half)
    def _():
        sent_ref[pos - half] = value

    @pl.when(pos < half)
    def _():
        kept_ref[pos] = value


def hidden_weights_kernel(orders, ff, nj, lhs_ref, own_ref, got_ref, sent_ref, kept_ref, rhs_ref, acc_ref):
    rows, d = own_ref.shape
    pad = rhs_ref.shape[1]
    seq, dp = lax.axis_index("seq"), lax.axis_index("dp")
    core, xi = lax.rem(seq, 2), lax.div(seq, 2)
    width = lhs_ref.shape[1]
    base = pad - d
    rhs_ref[:rows, :d] = own_ref[...]
    rhs_ref[rows:, :d] = got_ref[...]
    rhs_ref[:, d:] = jnp.zeros((2 * rows, base), BF)
    depth = ff // 2 // nj
    for x in (0, 1):
        rhs = rhs_ref[:, x * (pad - 640) : x * (pad - 640) + 640]
        for lo in range(0, width, 256):
            acc_ref[lo : lo + 256] = tn(lhs_ref[:, lo : lo + 256], rhs)
        for c in (0, 1):

            @pl.when(core == c)
            def _():
                for j in range(nj):
                    at = hidden_window(c, ff)[2] + j * depth
                    rel = (x ^ xi) * nj + (j ^ lax.rem(dp, nj))
                    store_block(orders, rel, acc_ref[at : at + depth].astype(BF), sent_ref, kept_ref)


def hidden_weights(lhs, own, got, ff, nj, orders):
    rows, d = own.shape
    width = lhs.shape[1]
    pad = -(-d // 128) * 128
    depth = ff // 2 // nj
    outs = [jax.ShapeDtypeStruct((nj, depth, 640), BF)] * 2
    full = lambda: pl.BlockSpec((nj, depth, 640), lambda *_: (0, 0, 0), pipeline_mode=pl.Buffered(1))
    return pl.pallas_call(
        functools.partial(hidden_weights_kernel, orders, ff, nj),
        grid=(1,),
        in_specs=[whole(lhs), whole(own), whole(got)],
        out_specs=[full(), full()],
        out_shape=outs,
        scratch_shapes=[pltpu.VMEM((2 * rows, pad), BF), pltpu.VMEM((width, 640), F32)],
        compiler_params=vmem(48),
        cost_estimate=cost(4 * rows * width * 1280, lhs, own, got, *outs),
        name="hidden_weights",
    )(lhs, own, got)


def project_weights_kernel(orders, ndp, lhs_ref, rhs_ref, out_ref, sent_ref, kept_ref, acc_ref, block_ref):
    d = lhs_ref.shape[1]
    half = d // 2
    wide = rhs_ref.shape[1] // ndp
    tall = out_ref.shape[1] // ndp
    rows = block_ref.shape[0]
    seq, dp = lax.axis_index("seq"), lax.axis_index("dp")
    xi, core = lax.div(seq, 2), lax.rem(seq, 2)
    for lo in range(0, d, 256):
        hi = min(lo + 256, d)
        acc_ref[lo:hi] = tn(lhs_ref[:, lo:hi], rhs_ref[...])
    block_ref[half:] = jnp.zeros((rows - half, wide), F32)
    for x in (0, 1):
        for j in range(ndp):
            block_ref[:half] = acc_ref[x * half : (x + 1) * half, j * wide : (j + 1) * wide]
            strip = out_ref[x ^ core, j * tall : (j + 1) * tall]
            for t, lo in enumerate(range(0, d, wide)):
                hi = min(lo + wide, d)
                block_ref[half + t * tall : half + (t + 1) * tall, : hi - lo] = strip[:, lo:hi]
            store_block(orders, (x ^ xi) * ndp + (j ^ dp), block_ref[...].astype(BF), sent_ref, kept_ref)


def project_rows(d, tall, wide):
    return -(-(d // 2 + -(-d // wide) * tall) // 16) * 16


def project_weights(lhs, rhs, out, ndp, orders):
    d, width = lhs.shape[1], rhs.shape[1]
    wide = width // ndp
    rows = project_rows(d, out.shape[1] // ndp, wide)
    block = (ndp, rows, wide)
    outs = [jax.ShapeDtypeStruct(block, BF)] * 2
    full = lambda: pl.BlockSpec(block, lambda *_: (0, 0, 0), pipeline_mode=pl.Buffered(1))
    return pl.pallas_call(
        functools.partial(project_weights_kernel, orders, ndp),
        grid=(1,),
        in_specs=[whole(lhs), whole(rhs), whole(out)],
        out_specs=[full(), full()],
        out_shape=outs,
        scratch_shapes=[pltpu.VMEM((d, width), F32), pltpu.VMEM((rows, wide), F32)],
        compiler_params=vmem(48),
        cost_estimate=cost(2 * lhs.shape[0] * d * width, lhs, rhs, out, *outs),
        name="project_weights",
    )(lhs, rhs, out)


def assemble_kernel(bits, held_ref, e_ref, qkv_ref, out_ref, q_ref, o_ref):
    ndp, _, wide = held_ref.shape
    quarter, d = out_ref.shape
    heads, head = e_ref.shape
    tall = o_ref.shape[0] // ndp
    dp = lax.axis_index("dp")
    for j in range(ndp):
        rel = dp ^ j
        slot = sum(jnp.where(rel & b != 0, 1 << k, 0) for k, b in enumerate(bits))
        block = held_ref[slot].astype(F32)
        for c in (0, 1):
            q_ref[c, :, j * wide : (j + 1) * wide] = block[c * quarter : (c + 1) * quarter]
        for t, lo in enumerate(range(0, d, wide)):
            hi = min(lo + wide, d)
            at = 2 * quarter + t * tall
            o_ref[j * tall : (j + 1) * tall, lo:hi] = block[at : at + tall, : hi - lo]
    for part in range(3):
        for c in (0, 1):
            lo = part * d + c * head
            qkv_ref[:, lo : lo + head] = nn(q_ref[c, :, part * heads : (part + 1) * heads].astype(BF), e_ref[...])
    for h in range(o_ref.shape[0] // 64):
        out_ref[h * HD : (h + 1) * HD] = o_ref[h * 64 : h * 64 + HD]


def assemble(held, e, quarter, d, bits):
    ndp, rows, wide = held.shape
    heads = e.shape[0]
    outs = [jax.ShapeDtypeStruct((quarter, 3 * d), F32), jax.ShapeDtypeStruct((quarter, d), F32)]
    return pl.pallas_call(
        functools.partial(assemble_kernel, bits),
        in_specs=[pl.BlockSpec(memory_space=pltpu.VMEM)] * 2,
        out_specs=[pl.BlockSpec(memory_space=pltpu.VMEM)] * 2,
        out_shape=outs,
        scratch_shapes=[pltpu.VMEM((2, quarter, ndp * wide), F32), pltpu.VMEM((quarter // HD * 64, d), F32)],
        compiler_params=vmem(40),
        cost_estimate=cost(6 * 2 * quarter * e.size, held, e, *outs),
        name="assemble",
    )(held, e)


def low(value):
    return lax.optimization_barrier(value.astype(BF))


def after(value, *first):
    return lax.optimization_barrier((value, *first))[0]


def swap(value, axis, bit):
    return lax.ppermute(value, axis, [(i, i ^ bit) for i in range(lax.axis_size(axis))])


def swap_by_core(value, steps):
    ndp, nseq = lax.axis_size("dp"), lax.axis_size("seq")
    pairs = []
    for d in range(ndp):
        for s in range(nseq):
            axis, bit = steps[s % 2]
            e, t = (d, s ^ bit) if axis == "seq" else (d ^ bit, s)
            pairs.append((d * nseq + s, e * nseq + t))
    return lax.ppermute(value, ("dp", "seq"), pairs)


def pick(array, index, axis):
    return lax.dynamic_index_in_dim(array, index, axis, keepdims=False)


def one_hot(rows, cols, source):
    r = lax.broadcasted_iota(jnp.int32, (rows, cols), 0)
    return (r == source[None, :]).astype(BF)


def halve(kept, got):
    half = kept.shape[0] // 2
    total = kept.astype(F32) + got.astype(F32)
    return low(total[half:]), low(total[:half])


def all_sum(value):
    value = swap(value, "seq", 1) + value
    value = swap(value, "seq", 2) + value
    bit = 1
    while bit < lax.axis_size("dp"):
        value = swap(value, "dp", bit) + value
        bit *= 2
    return value


def gather_dp(piece):
    held = piece[None]
    bits = [1 << b for b in range(lax.axis_size("dp").bit_length() - 1)][::-1]
    for bit in bits:
        held = jnp.concatenate([held, swap(held, "dp", bit)], 0)
    return held, bits


def per_device(
    cells, prefix_len, ln1_gain, ln1_bias, w_qkv, bias_q, bias_v, w_out, bias_out,
    ln2_gain, ln2_bias, w_up, bias_up, w_down, bias_down, cotangent,
):
    seq, ndp = lax.axis_size("seq"), lax.axis_size("dp")
    s, dp = lax.axis_index("seq"), lax.axis_index("dp")
    core, xi = s % 2, s // 2
    assert seq == 4
    pairs, block, D = cells.shape
    C = pairs // 2
    T = block * seq
    HH = H // 2
    WH = HH * 64
    half = D // 2
    quarter = D // 4
    FF = w_up.shape[1]
    nj = ndp // 2
    R = 2 * C * block
    row = lambda v: v.reshape(1, -1)
    place = s.reshape(1).astype(jnp.int32)

    def split_cells(a):
        return lax.dynamic_slice_in_dim(a, xi * C, C, 0), lax.dynamic_slice_in_dim(a, (1 - xi) * C, C, 0)

    def from_chip(own):
        got = swap(own[1], "seq", 2)
        return jnp.concatenate([jnp.where(xi == 0, own[0], got), jnp.where(xi == 0, got, own[0])], 0)

    x0, x_other = split_cells(cells)
    x1 = swap(x_other, "seq", 2)
    x0_got = swap(x0, "seq", 1)
    prefix = lax.dynamic_slice_in_dim(prefix_len, xi * C, C, 0)

    col = jnp.arange(WH)
    head_col = jnp.where(col % 64 < HD, core * half + (col // 64) * HD + col % 64, -1)
    w_parts = []
    for j in range(3):
        lo = j * D // 128 * 128
        hi = min(-(-(j + 1) * D // 128) * 128, 3 * D)
        e = one_hot(hi - lo, WH, jnp.where(head_col >= 0, head_col + j * D - lo, -1))
        w_parts.append(jnp.dot(w_qkv[:, lo:hi], e, preferred_element_type=F32).astype(BF))
    w_own = jnp.concatenate(w_parts, 1)

    def pad_heads(v, ones):
        v = lax.dynamic_slice_in_dim(v, core * half, half, 0).reshape(HH, HD)
        return jnp.concatenate([v, jnp.full((HH, 3), ones, F32), jnp.zeros((HH, 5), F32)], 1).reshape(WH)

    bias_own = jnp.concatenate([pad_heads(bias_q, 0.0), pad_heads(jnp.zeros_like(bias_q), 1.0), pad_heads(bias_v, 1.0)])
    wo = w_out.reshape(2, HH, HD, D)
    wo = jnp.concatenate([wo, jnp.zeros((2, HH, 64 - HD, D), BF)], 2).reshape(2, WH, D)
    wo = jnp.where(core == 0, wo, wo[::-1]).reshape(2 * WH, D)

    x1 = after(x1, wo, w_own)
    x1_got = swap(x1, "seq", 1)
    first, qkv = project(place, (x0, x0_got, x1, x1_got), row(ln1_gain), row(ln1_bias), w_own, row(bias_own))
    c0, c_other = split_cells(cotangent)
    c1 = swap(after(c_other, x1), "seq", 2)
    qkv, c1 = lax.optimization_barrier((qkv, c1))
    c_pair = jnp.concatenate([c0, c1], 0)
    c_got = swap(c_pair, "seq", 1)
    att, q_aug = attention_forward(qkv, prefix)
    att_got = swap(att, "seq", 1)
    middle, second = attention_output(place, att, att_got, x0, x1, wo, row(bias_out), row(ln2_gain), row(ln2_bias))
    blocks = lambda v: v.reshape(-1, block, v.shape[-1])
    rows_of = lambda v: v.reshape(-1, v.shape[-1])
    second_got = rows_of(swap(blocks(second), "seq", 1))
    cot, cot_got = rows_of(c_pair), rows_of(c_got)

    act, gpre, out_own, out_send, gs_own, gs_send, bias_up_sum = hidden_layer(
        second, second_got, cot, cot_got, w_up, row(bias_up), w_down.T, block)
    gs_got = rows_of(swap(blocks(gs_send), "seq", 1))
    out_got = rows_of(swap(blocks(out_send), "seq", 1))

    low_bits = [1 << b for b in range(nj.bit_length() - 1)]
    rest = low_bits[2:]

    def order(*names):
        n = {"x": ("seq", 2), "y": ("dp", 1), "z": ("dp", 2)}
        return [n[k] for k in names] + [("dp", b) for b in rest]

    def codes(steps, n):
        return [n if axis == "seq" else bit for axis, bit in steps]

    down_orders = (order("x", "y", "z"), order("y", "z", "x"))
    up_orders = (order("z", "x", "y"), order("x", "z", "y"))
    d_sent, d_kept = hidden_weights(act, cot, cot_got, FF, nj, [codes(o, nj) for o in down_orders])
    d_got = swap_by_core(d_sent, (down_orders[0][0], down_orders[1][0]))
    u_sent, u_kept = hidden_weights(gpre, second, second_got, FF, nj, [codes(o, nj) for o in up_orders])
    u_got = swap_by_core(u_sent, (up_orders[0][0], up_orders[1][0]))

    gmiddle, gbranch, gatt, block_rows, sums2 = middle_back(
        gs_own, gs_got, out_own, out_got, middle, cot, wo, row(ln2_gain), row(bias_down), block)
    gatt_got = swap(gatt, "seq", 1)
    block_out = from_chip(block_rows.reshape(2, C, block, D))

    att_rows = [
        jnp.concatenate([lax.dynamic_slice_in_dim(a, (s ^ (2 * k)) * block, block, 1) for k in (0, 1)], 0).reshape(R, WH)
        for a in (att, att_got)
    ]
    g_out = jnp.stack([
        lax.dot_general(a, gbranch, (((0,), (0,)), ((), ())), preferred_element_type=F32).astype(BF) for a in att_rows
    ]).reshape(2, 2, WH // 2, D)
    g_out = low(g_out)
    o_got = swap(pick(g_out, 1 - core, 1), "seq", 1)
    g_out = pick(g_out, core, 1).astype(F32) + o_got[::-1].astype(F32)
    shape = (2, C, block, 2 * WH)
    gqkv = attention_backward(
        qkv, q_aug, gatt.reshape(shape), gatt_got.reshape(shape), att, prefix, -(-3 * WH // 256) * 256).reshape(C * T, -1)

    d_sent, d_kept = halve(d_kept, d_got)
    d_got = swap_by_core(d_sent, (down_orders[0][1], down_orders[1][1]))
    u_sent, u_kept = halve(u_kept, u_got)
    u_got = swap_by_core(u_sent, (up_orders[0][1], up_orders[1][1]))

    WP = gqkv.shape[1]
    gqkv, block_out = lax.optimization_barrier((gqkv, block_out))
    q_orders = (order("z", "x", "y") + [("dp", nj)], order("y", "z", "x") + [("dp", nj)])
    q_sent, q_kept = project_weights(first.reshape(C * T, D), gqkv, g_out, ndp, [codes(o, ndp) for o in q_orders])
    q_got = swap_by_core(q_sent, (q_orders[0][0], q_orders[1][0]))
    gfirst, sums_qkv = project_back(gqkv, w_own, block)
    gfirst_got = rows_of(swap(blocks(gfirst), "seq", 1)).reshape(C, T, D)
    gfirst = gfirst.reshape(C, T, D)
    gcells, sums1 = cells_back(place, gfirst, gfirst_got, x0, x1, gmiddle, row(ln1_gain))
    grad_cells = from_chip(gcells)

    unpad = lambda v: v.reshape(HH, 64)[:, :HD].reshape(half)
    own_half = lambda v: jnp.where(core == 0, jnp.concatenate([v, jnp.zeros_like(v)]), jnp.concatenate([jnp.zeros_like(v), v]))
    ff_width = bias_up_sum.shape[1]
    pad_up = FF - ff_width
    g_bias_up = jnp.where(core == 0, jnp.pad(bias_up_sum[0], (0, pad_up)), jnp.pad(bias_up_sum[0], (pad_up, 0)))
    terms = [
        sums1[0], sums1[1], own_half(unpad(sums_qkv[0, :WH])), own_half(unpad(sums_qkv[0, 2 * WH : 3 * WH])),
        sums2[0], sums2[1], sums2[2], sums2[3], g_bias_up,
    ]
    packed = jnp.concatenate(terms)
    packed = all_sum(packed.reshape(-1, 128)).reshape(-1)
    shared = [packed[i * D : (i + 1) * D] for i in range(8)] + [packed[8 * D :]]

    for k in range(1, len(q_orders[0])):
        q_sent, q_kept = halve(q_kept, q_got)
        q_got = swap_by_core(q_sent, (q_orders[0][k], q_orders[1][k]))
    q_sum = low(q_kept.astype(F32) + q_got.astype(F32))[0]
    q_half = q_sum[: 2 * quarter].reshape(2, quarter, WP // ndp)
    q_theirs = swap(pick(q_half, 1 - core, 0), "seq", 1)
    q_ours = pick(q_half, core, 0)
    piece = jnp.concatenate([jnp.where(core == 0, q_ours, q_theirs), jnp.where(core == 0, q_theirs, q_ours), q_sum[2 * quarter :]], 0)
    held, bits = gather_dp(piece)
    head_of = jnp.arange(half)
    e_out = (jnp.arange(WH)[:, None] == (head_of // HD * 64 + head_of % HD)[None, :]).astype(BF)
    final_qkv, final_out = assemble(held, e_out, quarter, D, bits)

    for k in range(1, len(down_orders[0])):
        if k > 1:
            d_got = swap_by_core(d_sent, (down_orders[0][k], down_orders[1][k]))
            u_got = swap_by_core(u_sent, (up_orders[0][k], up_orders[1][k]))
        if k < len(down_orders[0]) - 1:
            d_sent, d_kept = halve(d_kept, d_got)
            u_sent, u_kept = halve(u_kept, u_got)
    pair = low(jnp.concatenate([d_kept, u_kept], 0).astype(F32) + jnp.concatenate([d_got, u_got], 0).astype(F32))
    across = []
    for d in range(ndp):
        for t in range(seq):
            if d // nj != t % 2:
                across.append((d * seq + t, (d ^ nj) * seq + t))
    pair_got = lax.ppermute(pair, ("dp", "seq"), across)
    pair = pair.astype(F32) + pair_got.astype(F32)
    shift = -(-D // 128) * 128 - 640
    def part(c):
        lo0, lo1 = c * quarter, half - shift + c * quarter
        return jnp.where(xi == 0, pair[:, :, lo0 : lo0 + quarter], pair[:, :, lo1 : lo1 + quarter])
    p0, p1 = part(0), part(1)
    theirs = swap(low(jnp.where(core == 0, p1, p0)), "seq", 1).astype(F32)
    both = jnp.where(core == dp // nj, jnp.where(core == 0, p0, p1), theirs)
    final_down = both[0]
    final_up = both[1].T

    return (
        block_out, grad_cells, shared[0], shared[1], final_qkv, shared[2], shared[3], final_out,
        shared[4], shared[5], shared[6], final_up, shared[8], final_down, shared[7],
    )


def solution(mesh):
    rows = P("dp", "seq", None)
    return jax.shard_map(
        per_device,
        mesh=mesh,
        in_specs=(rows, P("dp")) + (P(),) * 13 + (rows,),
        out_specs=(rows, rows, P(), P(), P("seq", None), P(), P(), P("seq", None), P(), P(), P(), P("seq", "dp"), P(), P("dp", "seq"), P()),
        check_vma=False,
    )
```

```python
import functools
import math
import jax
import jax.numpy as jnp
from jax import lax
from jax.experimental import pallas as pl
from jax.experimental.pallas import tpu as pltpu
from jax.sharding import PartitionSpec as P

H = 20
HD=56
F32=jnp.float32; BF=jnp.bfloat16
LOG2=math.log2(math.e)
NEG=-1e30
def nt(a,b): return lax.dot_general(a,b,(((1,),(1,)),((),())),preferred_element_type=F32)
def nn(a,b): return lax.dot_general(a,b,(((1,),(0,)),((),())),preferred_element_type=F32)
def tn(a,b): return lax.dot_general(a,b,(((0,),(0,)),((),())),preferred_element_type=F32)

def split3(v):
    a=v.astype(BF); r=v-a.astype(F32); b=r.astype(BF); r=r-b.astype(F32)
    return a.astype(F32),b.astype(F32),r

def dup(k):
    low=lax.broadcasted_iota(jnp.int32,k.shape,1)<64
    r=pltpu.roll(k,64,1)
    return jnp.where(low,k,r).astype(BF), jnp.where(low,r,k).astype(BF)

def fwd_kernel(B, prefix_ref, q_ref,k_ref,v_ref,o_ref,qa_ref):
    T=q_ref.shape[1]
    p=prefix_ref[pl.program_id(0)]
    lane=lax.broadcasted_iota(jnp.int32,(T,128),1); low=lane<64
    q=q_ref[0].astype(F32)*(HD**-0.5*LOG2)
    hi=q.astype(BF).astype(F32); res=pltpu.roll(q-hi,64,1)
    qa=[jnp.where(low,hi,res),jnp.where(low,res,hi)]
    qab=[x.astype(BF) for x in qa]
    ka=dup(k_ref[0].astype(F32))
    lane_b=lane[:B]
    row=lax.broadcasted_iota(jnp.int32,(B,B),0); col=lax.broadcasted_iota(jnp.int32,(B,B),1)
    tri=col<=row
    first=tri|((col<p)&(row<p))
    for i in range(T//B):
        n=(i+1)*B; rows=slice(i*B,n)
        outs=[]
        for h in range(2):
            s=nt(qab[h][rows],ka[h][:n])
            d=jnp.where(first if i==0 else tri,s[:,n-B:],NEG)
            if i: s=jnp.concatenate([s[:,:n-B],d],1)
            else: s=d
            m=jnp.max(s,axis=1,keepdims=True)
            e=jnp.exp2(s-m).astype(BF)
            o=nn(e,v_ref[0,:n])
            l=o[:,56+64*h:57+64*h]
            outs.append(o*(1.0/l))
            lse=-(m+jnp.log2(l))
            a,b,c=split3(lse)
            z=64*h+56
            x=jnp.where(lane_b==z,a,jnp.where(lane_b==z+1,b,jnp.where(lane_b==z+2,c,qa[h][rows])))
            qa_ref[0,rows,128*h:128*h+128]=x.astype(BF)
        o_ref[0,rows]=jnp.where(low[:B],outs[0],outs[1]).astype(BF)

FIRST=3


def tile_of(part,p,pairs):
    if isinstance(p,int):
        return part*FIRST+p if p<FIRST else 3*FIRST+part*(pairs-FIRST)+p-FIRST
    return jnp.where(p<FIRST,part*FIRST+p,3*FIRST+part*(pairs-FIRST)+p-FIRST)


def attention_forward(qkv,prefix,B=256):
    C,T,W=qkv.shape; NP=W//384
    spec=lambda part: pl.BlockSpec((1,T,128),lambda c,p,pr: (c,0,tile_of(part,p,NP)))
    return pl.pallas_call(functools.partial(fwd_kernel,B),
        grid_spec=pltpu.PrefetchScalarGridSpec(num_scalar_prefetch=1,grid=(C,NP),
            in_specs=[spec(0),spec(1),spec(2)],
            out_specs=[pl.BlockSpec((1,T,128),lambda c,p,pr:(c,0,p)),pl.BlockSpec((1,T,256),lambda c,p,pr:(c,0,p))]),
        out_shape=[jax.ShapeDtypeStruct((C,T,128*NP),BF),jax.ShapeDtypeStruct((C,T,256*NP),BF)],
        compiler_params=pltpu.CompilerParams(vmem_limit_bytes=24<<20),
        cost_estimate=pl.CostEstimate(flops=C*NP*2*2*2*T*T*64,bytes_accessed=C*T*128*NP*12,transcendentals=C*NP*T*T),
        name="attention_forward",
    )(prefix,qkv,qkv,qkv)

def bwd_kernel(B, prefix_ref, qa_ref,q_ref,k_ref,v_ref,go_ref,gg_ref,o_ref,out_ref,dk_ref,dv_ref,do_ref):
    T=q_ref.shape[1]; NP=pl.num_programs(1); W=out_ref.shape[2]
    block=T//4
    s=lax.axis_index("seq")
    for k,piece in enumerate((go_ref[0,0],go_ref[1,0],gg_ref[0,0],gg_ref[1,0])):
        place=s^(2*(k%2)+k//2)
        do_ref[pl.ds(pl.multiple_of(place*block,block),block)]=piece
    pr=pl.program_id(1)
    p=prefix_ref[pl.program_id(0)]
    lane=lax.broadcasted_iota(jnp.int32,(T,128),1); low=lane<64
    k32=k_ref[0].astype(F32); q32=q_ref[0].astype(F32); do32=do_ref[...].astype(F32)
    ka=dup(k32)
    zero=jnp.zeros_like(k32)
    km=[jnp.where(low,k32,zero).astype(BF),jnp.where(low,zero,k32).astype(BF)]
    qm=[jnp.where(low,q32,zero).astype(BF),jnp.where(low,zero,q32).astype(BF)]
    dom=[jnp.where(low,do32,zero),jnp.where(low,zero,do32)]
    o32=o_ref[0].astype(F32)
    doa=[]
    for h in range(2):
        dl=-jnp.sum(dom[h]*o32,axis=1,keepdims=True)
        a,b,c=split3(dl); z=64*h+56
        doa.append(jnp.where(lane==z,a,jnp.where(lane==z+1,b,jnp.where(lane==z+2,c,dom[h]))).astype(BF))
    dom=[x.astype(BF) for x in dom]
    key=lax.broadcasted_iota(jnp.int32,(B,B),0); qry=lax.broadcasted_iota(jnp.int32,(B,B),1)
    tri=key<=qry
    first=tri|((key<p)&(qry<p))
    sc=HD**-0.5
    for i in reversed(range(T//B)):
        n=(i+1)*B; rows=slice(i*B,n)
        pbs=[];dss=[]
        for h in range(2):
            s=nt(ka[h][:n],qa_ref[0,rows,128*h:128*h+128])
            d=jnp.where(first if i==0 else tri,s[n-B:],NEG)
            s=jnp.concatenate([s[:n-B],d],0) if i else d
            e=jnp.exp2(s)
            dp=nt(v_ref[0,:n],doa[h][rows])
            dss.append((e*dp).astype(BF)); pbs.append(e.astype(BF))
        dq=tn(dss[0],km[0][:n])+tn(dss[1],km[1][:n])
        out_ref[0,rows,pl.ds(pl.multiple_of(pr*128,128),128)]=(dq*sc).astype(BF)
        dv=nn(pbs[0],dom[0][rows])+nn(pbs[1],dom[1][rows])
        dk=nn(dss[0],qm[0][rows])+nn(dss[1],qm[1][rows])
        if i==T//B-1:
            dv_ref[...]=dv; dk_ref[...]=dk
        else:
            dv_ref[:n]+=dv; dk_ref[:n]+=dk
    out_ref[0,:,pl.ds(pl.multiple_of((NP+pr)*128,128),128)]=(dk_ref[...]*sc).astype(BF)
    out_ref[0,:,pl.ds(pl.multiple_of((2*NP+pr)*128,128),128)]=dv_ref[...].astype(BF)

def attention_backward(qkv,qa,do,do_got,o,prefix,p0,p1,B=256):
    C,T,W=qkv.shape; NP=W//384
    width=384*(p1-p0)
    spec=lambda part: pl.BlockSpec((1,T,128),lambda c,p,pr: (c,0,tile_of(part,p0,NP)+p))
    return pl.pallas_call(functools.partial(bwd_kernel,B),
        grid_spec=pltpu.PrefetchScalarGridSpec(num_scalar_prefetch=1,grid=(C,p1-p0),
            in_specs=[pl.BlockSpec((1,T,256),lambda c,p,pr:(c,0,p0+p)),spec(0),spec(1),spec(2),
                pl.BlockSpec((2,1,T//4,128),lambda c,p,pr:(0,c,0,p0+p)),pl.BlockSpec((2,1,T//4,128),lambda c,p,pr:(0,c,0,NP+p0+p)),
                pl.BlockSpec((1,T,128),lambda c,p,pr:(c,0,p0+p))],
            out_specs=pl.BlockSpec((1,T,width),lambda c,p,pr:(c,0,0)),
            scratch_shapes=[pltpu.VMEM((T,128),F32)]*2+[pltpu.VMEM((T,128),BF)]),
        out_shape=jax.ShapeDtypeStruct((C,T,width),BF),
        compiler_params=pltpu.CompilerParams(vmem_limit_bytes=40<<20),
        cost_estimate=pl.CostEstimate(flops=C*(p1-p0)*2*5*2*T*T*64,bytes_accessed=C*T*128*(p1-p0)*20,transcendentals=C*(p1-p0)*T*T),
        name="attention_backward",
    )(prefix,qa,qkv,qkv,qkv,do,do_got,o)


epsilon = 1e-05


def vmem(megabytes):
    return pltpu.CompilerParams(vmem_limit_bytes=megabytes << 20)


def whole(array):
    return pl.BlockSpec(array.shape, lambda *_: (0,) * array.ndim, pipeline_mode=pl.Buffered(1))


def cost(flops, *arrays):
    return pl.CostEstimate(
        flops=flops, bytes_accessed=sum(math.prod(a.shape) * a.dtype.itemsize for a in arrays), transcendentals=0)


def block_norm(rows):
    width = rows.shape[1]
    mean = jnp.sum(rows, axis=1, keepdims=True) * (1.0 / width)
    centred = rows - mean
    rstd = lax.rsqrt(jnp.sum(centred * centred, axis=1, keepdims=True) * (1.0 / width) + epsilon)
    return centred * rstd, rstd


def block_norm_back(grad, normed, rstd, gain):
    inv = 1.0 / grad.shape[1]
    dn = grad * gain
    a = jnp.sum(dn, axis=1, keepdims=True) * inv
    b = jnp.sum(dn * normed, axis=1, keepdims=True) * inv
    return rstd * (dn - a - normed * b)


def add_sums(ref, start, *rows):
    for k, v in enumerate(rows):
        total = jnp.sum(v, axis=0, keepdims=True)
        ref[k : k + 1] = jnp.where(start, total, ref[k : k + 1] + total)


def project_kernel(s_ref, a_ref, b_ref, c_ref, d_ref, g_ref, h_ref, w_ref, bias_ref, first_ref, out_ref):
    k = pl.program_id(1)
    x = jnp.where(k < 2, jnp.where(k == 0, a_ref[0].astype(F32), b_ref[0].astype(F32)),
                  jnp.where(k == 2, c_ref[0].astype(F32), d_ref[0].astype(F32)))
    n, _ = block_norm(x)
    first = (n * g_ref[...] + h_ref[...]).astype(BF)
    first_ref[0] = first
    width = w_ref.shape[1]
    for lo in range(0, width, 640):
        cols = slice(lo, min(lo + 640, width))
        out_ref[0, :, cols] = (nn(first, w_ref[:, cols]) + bias_ref[:, cols]).astype(BF)


def project(place, pieces, gain, shift, w, bias):
    cells, rows, d = pieces[0].shape
    width = w.shape[1]
    piece = pl.BlockSpec((1, rows, d), lambda c, k, s: (c, 0, 0))
    at = lambda c, k, s: (c, s[0] ^ k, 0)
    ins = (gain, shift, w, bias)
    outs = [jax.ShapeDtypeStruct((cells, 4 * rows, n), BF) for n in (d, width)]
    return pl.pallas_call(
        project_kernel,
        grid_spec=pltpu.PrefetchScalarGridSpec(
            num_scalar_prefetch=1, grid=(cells, 4), in_specs=[piece] * 4 + [whole(a) for a in ins],
            out_specs=[pl.BlockSpec((1, rows, n), at) for n in (d, width)]),
        out_shape=outs,
        compiler_params=vmem(40),
        cost_estimate=cost(8 * cells * rows * w.size, *pieces, *ins, *outs),
        name="norm_project",
    )(place, *pieces, *ins)


def middle_kernel(s_ref, own_ref, got_ref, a_ref, b_ref, w_ref, c_ref, g_ref, h_ref, middle_ref, second_ref):
    half = own_ref.shape[2]
    out = nn(own_ref[0], w_ref[:half]) + nn(got_ref[0], w_ref[half:])
    x = jnp.where(pl.program_id(0) == 0, a_ref[0].astype(F32), b_ref[0].astype(F32))
    middle = x + out + c_ref[...]
    middle_ref[...] = middle
    n, _ = block_norm(middle)
    second_ref[...] = (n * g_ref[...] + h_ref[...]).astype(BF)


def attention_output(place, own, got, x0, x1, w, bias, gain, shift):
    cells, rows, d = x0.shape
    half = own.shape[2]
    at = pl.BlockSpec((1, rows, half), lambda k, c, s: (c, s[0] ^ (2 * k), 0))
    piece = pl.BlockSpec((1, rows, d), lambda k, c, s: (c, 0, 0))
    ins = (w, bias, gain, shift)
    outs = [jax.ShapeDtypeStruct((2 * cells * rows, d), t) for t in (F32, BF)]
    return pl.pallas_call(
        middle_kernel,
        grid_spec=pltpu.PrefetchScalarGridSpec(
            num_scalar_prefetch=1, grid=(2, cells), in_specs=[at, at, piece, piece] + [whole(a) for a in ins],
            out_specs=[pl.BlockSpec((rows, d), lambda k, c, s: (k * cells + c, 0))] * 2),
        out_shape=outs,
        compiler_params=vmem(32),
        cost_estimate=cost(4 * cells * rows * w.size, x0, x0, *ins, *outs),
        name="attention_output",
    )(place, own, got, x0, x1, *ins)


CHUNK = 768


def hidden_window(core, ff):
    width = -(-(ff // 2) // CHUNK) * CHUNK
    return core * (ff - width), width, core * (width - ff // 2)


def hidden_kernel(
    ff, s0_ref, s1_ref, c0_ref, c1_ref, bu_ref, wu_hbm, wd_hbm,
    act_ref, gpre_ref, out0_ref, out1_ref, gs0_ref, gs1_ref, sum_ref, wu_ref, wd_ref, sem,
):
    i, n = pl.program_id(0), pl.num_programs(0) // 2
    core = lax.rem(lax.axis_index("seq"), 2)
    start, width, skip = hidden_window(core, ff)
    chunks = width // CHUNK

    def copies(k):
        at = pl.multiple_of(start + k * CHUNK, 128)
        cols = pl.ds(k * CHUNK, CHUNK)
        return (
            pltpu.make_async_copy(wu_hbm.at[:, pl.ds(at, CHUNK)], wu_ref.at[:, cols], sem.at[2 * k]),
            pltpu.make_async_copy(wd_hbm.at[:, pl.ds(at, CHUNK)], wd_ref.at[:, cols], sem.at[2 * k + 1]),
        )

    @pl.when(i == 0)
    def _():
        for k in range(chunks):
            for c in copies(k):
                c.start()

    second = jnp.where(i < n, s0_ref[...].astype(F32), s1_ref[...].astype(F32)).astype(BF)
    cot = jnp.where(i < n, c0_ref[...].astype(F32), c1_ref[...].astype(F32)).astype(BF)
    out = gsec = None
    a, b = 0.7978845608, 0.044715
    for k in range(chunks):
        cols = slice(k * CHUNK, (k + 1) * CHUNK)

        @pl.when(i == 0)
        def _():
            for c in copies(k):
                c.wait()

        u = nn(second, wu_ref[:, cols]) + bu_ref[:, pl.ds(pl.multiple_of(start + k * CHUNK, 128), CHUNK)]
        gact = nn(cot, wd_ref[:, cols])
        u2 = u * u
        t = jnp.tanh(u * (a + a * b * u2))
        h = 0.5 + 0.5 * t
        act = u * h
        gpre = gact * (h + u * (0.5 - 0.5 * t * t) * (a + 3 * a * b * u2))
        if k in (0, chunks - 1):
            col = lax.broadcasted_iota(jnp.int32, (1, CHUNK), 1) + k * CHUNK
            mine = (col >= skip) & (col < skip + ff // 2)
            act, gpre = jnp.where(mine, act, 0.0), jnp.where(mine, gpre, 0.0)
        act, gpre = act.astype(BF), gpre.astype(BF)
        act_ref[:, cols] = act
        gpre_ref[:, cols] = gpre
        total = jnp.sum(gpre.astype(F32), axis=0, keepdims=True)
        sum_ref[:, cols] = jnp.where(i == 0, total, sum_ref[:, cols] + total)
        o, g = nt(act, wd_ref[:, cols]), nt(gpre, wu_ref[:, cols])
        out, gsec = (o, g) if out is None else (out + o, gsec + g)

    @pl.when(i < n)
    def _():
        out0_ref[...] = out.astype(BF)
        gs0_ref[...] = gsec.astype(BF)

    @pl.when(i >= n)
    def _():
        out1_ref[...] = out.astype(BF)
        gs1_ref[...] = gsec.astype(BF)


def hidden_layer(second, second_got, cot, cot_got, w_up, bias_up, w_down_t, m):
    rows, d = second.shape
    ff = w_up.shape[1]
    n = rows // m
    width = hidden_window(0, ff)[1]
    lo = pl.BlockSpec((m, d), lambda i: (jnp.minimum(i, n - 1), 0))
    hi = pl.BlockSpec((m, d), lambda i: (jnp.maximum(i - n, 0), 0))
    row = pl.BlockSpec((m, width), lambda i: (i, 0))
    hbm = pl.BlockSpec(memory_space=pl.ANY)
    shape = jax.ShapeDtypeStruct
    outs = [shape((2 * rows, width), BF)] * 2 + [shape((rows, d), BF)] * 4 + [shape((1, width), F32)]
    return pl.pallas_call(
        functools.partial(hidden_kernel, ff),
        grid=(2 * n,),
        in_specs=[lo, hi, lo, hi, whole(bias_up), hbm, hbm],
        out_specs=[row, row, lo, hi, lo, hi, pl.BlockSpec((1, width), lambda i: (0, 0))],
        out_shape=outs,
        scratch_shapes=[pltpu.VMEM((d, width), BF), pltpu.VMEM((d, width), BF), pltpu.SemaphoreType.DMA((2 * (width // CHUNK),))],
        compiler_params=vmem(56),
        cost_estimate=cost(16 * rows * d * width, second, second, cot, cot, w_up, *outs),
        name="hidden_layer",
    )(second, second_got, cot, cot_got, bias_up, w_up, w_down_t)


def middle_back_kernel(
    gs_ref, gs_got_ref, o_ref, o_got_ref, middle_ref, cot_ref, w_ref, g_ref, c_ref,
    gm_ref, gb_ref, gatt_ref, block_ref, sum_ref,
):
    middle, gy = middle_ref[...], cot_ref[...].astype(F32)
    gsecond = gs_ref[...].astype(F32) + gs_got_ref[...].astype(F32)
    n, rstd = block_norm(middle)
    gmiddle = gy + block_norm_back(gsecond, n, rstd, g_ref[...])
    gm_ref[...] = gmiddle
    gbranch = gmiddle.astype(BF)
    gb_ref[...] = gbranch
    gatt_ref[...] = nt(gbranch, w_ref[...]).astype(BF)
    block_ref[...] = (middle + (o_ref[...].astype(F32) + o_got_ref[...].astype(F32)) + c_ref[...]).astype(BF)
    add_sums(sum_ref, pl.program_id(0) == 0, gbranch.astype(F32), gsecond * n, gsecond, gy)


def middle_back(gsec, gsec_got, out, out_got, middle, cot, w, gain, bias, m):
    rows, d = middle.shape
    row = lambda n: pl.BlockSpec((m, n), lambda i: (i, 0))
    ins = (gsec, gsec_got, out, out_got, middle, cot, w, gain, bias)
    shape = jax.ShapeDtypeStruct
    heads = w.shape[0]
    outs = [shape((rows, d), F32), shape((rows, d), BF), shape((rows, heads), BF), shape((rows, d), BF), shape((4, d), F32)]
    return pl.pallas_call(
        middle_back_kernel,
        grid=(rows // m,),
        in_specs=[row(d)] * 6 + [whole(a) for a in ins[6:]],
        out_specs=[row(d), row(d), row(heads), row(d), pl.BlockSpec((4, d), lambda i: (0, 0))],
        out_shape=outs,
        compiler_params=vmem(40),
        cost_estimate=cost(2 * rows * w.size, *ins, *outs),
        name="middle_back",
    )(*ins)


def project_back_kernel(a_ref, b_ref, w_ref, out_ref, sum_ref):
    split = a_ref.shape[1]
    out_ref[...] = (nt(a_ref[...], w_ref[:, :split]) + nt(b_ref[...], w_ref[:, split:])).astype(BF)
    start = pl.program_id(0) == 0
    for ref, cols in ((a_ref, slice(0, split)), (b_ref, slice(split, None))):
        total = jnp.sum(ref[...].astype(F32), axis=0, keepdims=True)
        sum_ref[:, cols] = jnp.where(start, total, sum_ref[:, cols] + total)


def project_back(a, b, w, m):
    rows = a.shape[0]
    d, width = w.shape
    outs = [jax.ShapeDtypeStruct((rows, d), BF), jax.ShapeDtypeStruct((1, width), F32)]
    return pl.pallas_call(
        project_back_kernel,
        grid=(rows // m,),
        in_specs=[pl.BlockSpec((m, a.shape[1]), lambda i: (i, 0)), pl.BlockSpec((m, b.shape[1]), lambda i: (i, 0)), whole(w)],
        out_specs=[pl.BlockSpec((m, d), lambda i: (i, 0)), pl.BlockSpec((1, width), lambda i: (0, 0))],
        out_shape=outs,
        compiler_params=vmem(32),
        cost_estimate=cost(2 * rows * w.size, a, b, w, *outs),
        name="project_back",
    )(a, b, w)


def cells_back_kernel(s_ref, g_ref, got_ref, a_ref, b_ref, gm_ref, gain_ref, out_ref, sum_ref):
    k = pl.program_id(0)
    g = g_ref[0].astype(F32) + got_ref[0].astype(F32)
    n, rstd = block_norm(jnp.where(k == 0, a_ref[0].astype(F32), b_ref[0].astype(F32)))
    out_ref[0, 0] = (gm_ref[...] + block_norm_back(g, n, rstd, gain_ref[...])).astype(BF)
    add_sums(sum_ref, (k == 0) & (pl.program_id(1) == 0), g * n, g)


def cells_back(place, g, got, x0, x1, gmiddle, gain):
    cells, rows, d = x0.shape
    at = pl.BlockSpec((1, rows, d), lambda k, c, s: (c, s[0] ^ (2 * k), 0))
    piece = pl.BlockSpec((1, rows, d), lambda k, c, s: (c, 0, 0))
    outs = [jax.ShapeDtypeStruct((2, cells, rows, d), BF), jax.ShapeDtypeStruct((2, d), F32)]
    return pl.pallas_call(
        cells_back_kernel,
        grid_spec=pltpu.PrefetchScalarGridSpec(
            num_scalar_prefetch=1, grid=(2, cells),
            in_specs=[at, at, piece, piece, pl.BlockSpec((rows, d), lambda k, c, s: (k * cells + c, 0)), whole(gain)],
            out_specs=[pl.BlockSpec((1, 1, rows, d), lambda k, c, s: (k, c, 0, 0)), pl.BlockSpec((2, d), lambda k, c, s: (0, 0))]),
        out_shape=outs,
        compiler_params=vmem(32),
        cost_estimate=cost(0, x0, x0, x0, x0, x0, x0, gmiddle, *outs),
        name="cells_back",
    )(place, g, got, x0, x1, gmiddle, gain)


def store_block(orders, rel, value, sent_ref, kept_ref):
    core = lax.rem(lax.axis_index("seq"), 2)
    half = kept_ref.shape[0]
    places = [
        sum(jnp.where(rel & step != 0, half >> k, 0) for k, step in enumerate(steps)) for steps in orders
    ]
    pos = jnp.where(core == 0, places[0], places[1])

    @pl.when(pos >= half)
    def _():
        sent_ref[pos - half] = value

    @pl.when(pos < half)
    def _():
        kept_ref[pos] = value


def hidden_weights_kernel(orders, ff, nj, lhs_ref, own_ref, got_ref, sent_ref, kept_ref, rhs_ref, acc_ref):
    rows, d = own_ref.shape
    pad = rhs_ref.shape[1]
    step, steps = pl.program_id(0), pl.num_programs(0)
    seq, dp = lax.axis_index("seq"), lax.axis_index("dp")
    core, xi = lax.rem(seq, 2), lax.div(seq, 2)
    depth = ff // 2 // nj

    @pl.when(step == 0)
    def _():
        rhs_ref[:rows, :d] = own_ref[...]
        rhs_ref[rows:, :d] = got_ref[...]
        rhs_ref[:, d:] = jnp.zeros((2 * rows, pad - d), BF)

    wide = lhs_ref.shape[1]
    acc_ref[pl.ds(pl.multiple_of(step * wide, wide), wide)] = tn(lhs_ref[...], rhs_ref[...])
    for c in (0, 1):

        @pl.when((core == c) & (step == steps - 1))
        def _():
            for x in (0, 1):
                for j in range(nj):
                    at = hidden_window(c, ff)[2] + j * depth
                    rel = (x ^ xi) * nj + (j ^ lax.rem(dp, nj))
                    value = acc_ref[at : at + depth, x * (pad - 640) : x * (pad - 640) + 640]
                    store_block(orders, rel, value.astype(BF), sent_ref, kept_ref)


def hidden_weights(lhs, own, got, ff, nj, orders):
    rows, d = own.shape
    width = lhs.shape[1]
    pad = -(-d // 128) * 128
    depth = ff // 2 // nj
    outs = [jax.ShapeDtypeStruct((nj, depth, 640), BF)] * 2
    full = lambda: pl.BlockSpec((nj, depth, 640), lambda *_: (0, 0, 0), pipeline_mode=pl.Buffered(1))
    return pl.pallas_call(
        functools.partial(hidden_weights_kernel, orders, ff, nj),
        grid=(width // 256,),
        in_specs=[pl.BlockSpec((2 * rows, 256), lambda i: (0, i)), whole(own), whole(got)],
        out_specs=[full(), full()],
        out_shape=outs,
        scratch_shapes=[pltpu.VMEM((2 * rows, pad), BF), pltpu.VMEM((width, pad), F32)],
        compiler_params=vmem(48),
        cost_estimate=cost(4 * rows * width * pad, lhs, own, got, *outs),
        name="hidden_weights",
    )(lhs, own, got)


def output_weights_kernel(s_ref, own_ref, got_ref, g_ref, send_ref, keep_ref, acc_ref):
    k, c = pl.program_id(0), pl.program_id(1)
    start = (k == 0) & (c == 0)
    for h, ref in enumerate((own_ref, got_ref)):
        total = tn(ref[0], g_ref[...])
        acc_ref[h] = jnp.where(start, total, acc_ref[h] + total)
    core = lax.rem(lax.axis_index("seq"), 2)
    half = keep_ref.shape[1]
    for mine in (0, 1):

        @pl.when((k == 1) & (c == pl.num_programs(1) - 1) & (core == mine))
        def _():
            for h in (0, 1):
                keep_ref[h] = acc_ref[h, mine * half : (mine + 1) * half]
                send_ref[h] = acc_ref[h, (1 - mine) * half : (2 - mine) * half].astype(BF)


def output_weights(place, own, got, g, rows):
    cells, _, width = own.shape
    d = g.shape[1]
    at = pl.BlockSpec((1, rows, width), lambda k, c, s: (c, s[0] ^ (2 * k), 0))
    shape = (2, width // 2, d)
    outs = [jax.ShapeDtypeStruct(shape, BF), jax.ShapeDtypeStruct(shape, F32)]
    return pl.pallas_call(
        output_weights_kernel,
        grid_spec=pltpu.PrefetchScalarGridSpec(
            num_scalar_prefetch=1, grid=(2, cells),
            in_specs=[at, at, pl.BlockSpec((rows, d), lambda k, c, s: (k * cells + c, 0))],
            out_specs=[pl.BlockSpec(shape, lambda *_: (0, 0, 0), pipeline_mode=pl.Buffered(1))] * 2,
            scratch_shapes=[pltpu.VMEM((2, width, d), F32)]),
        out_shape=outs,
        compiler_params=vmem(32),
        cost_estimate=cost(8 * cells * rows * width * d, own, got, g, *outs),
        name="output_weights",
    )(place, own, got, g)


def place_in(steps, rel, count):
    return sum(jnp.where(rel & step != 0, count >> (k + 1), 0) for k, step in enumerate(steps))


def project_weights_kernel(orders, ndp, half, lhs_ref, rhs_refs, out_ref, blocks_ref, acc_ref, block_ref):
    step, steps = pl.program_id(0), pl.num_programs(0)
    seq, dp = lax.axis_index("seq"), lax.axis_index("dp")
    xi, core = lax.div(seq, 2), lax.rem(seq, 2)
    m = lhs_ref.shape[1]
    lo = 0
    rows = pl.ds(pl.multiple_of(step * m, m), m)
    for ref in rhs_refs:
        wide = ref.shape[1]
        acc_ref[rows, lo : lo + wide] = tn(lhs_ref[...], ref[...])
        lo += wide
    acc_ref[rows, lo:] = jnp.zeros((m, acc_ref.shape[1] - lo), F32)

    @pl.when(step == steps - 1)
    def _():
        wide = acc_ref.shape[1] // ndp
        third = block_ref.shape[0] // 3
        block_ref[half:] = jnp.zeros((3 * third - half, wide), F32)
        tall = out_ref.shape[1] // ndp
        for x in (0, 1):
            for j in range(ndp):
                block_ref[:half] = acc_ref[x * half : (x + 1) * half, j * wide : (j + 1) * wide]
                strip = out_ref[x ^ core, j * tall : (j + 1) * tall]
                for t, lo in enumerate(range(0, 2 * half, wide)):
                    hi = min(lo + wide, 2 * half)
                    block_ref[half + t * tall : half + (t + 1) * tall, : hi - lo] = strip[:, lo:hi]
                rel = (x ^ xi) * ndp + (j ^ dp)
                for i in range(3):
                    blocks_ref[i, place_in(orders[i], rel, 2 * ndp)] = block_ref[i * third : (i + 1) * third].astype(BF)


def project_weights(lhs, parts, width, out, ndp, orders):
    rows_in, d = lhs.shape
    m = 256
    steps = -(-d // m)
    wide = width // ndp
    third = -(-(d // 2 + -(-d // wide) * (out.shape[1] // ndp)) // 48) * 16
    block = (3, 2 * ndp, third, wide)
    n = len(parts)

    def kernel(lhs_ref, *refs):
        project_weights_kernel(orders, ndp, d // 2, lhs_ref, refs[:n], *refs[n:])

    return pl.pallas_call(
        kernel,
        grid=(steps,),
        in_specs=[pl.BlockSpec((rows_in, m), lambda i: (0, i))] + [whole(a) for a in (*parts, out)],
        out_specs=pl.BlockSpec(block, lambda *_: (0, 0, 0, 0), pipeline_mode=pl.Buffered(1)),
        out_shape=jax.ShapeDtypeStruct(block, BF),
        scratch_shapes=[pltpu.VMEM((steps * m, width), F32), pltpu.VMEM((3 * third, wide), F32)],
        compiler_params=vmem(48),
        cost_estimate=cost(2 * rows_in * d * width, lhs, out),
        name="project_weights",
    )(lhs, *parts, out)


def flip(index, bit):
    return index + bit - 2 * bit * lax.rem(lax.div(index, bit), 2)


def quarter_of(pair, x, c, quarter, shift):
    lo = x * shift + c * quarter
    return pair[:, :, lo : lo + quarter]


def sum_kernel(
    ndp, orders, quarter, shift, in_ref, pair_ref, terms_ref, block_ref, cells_ref,
    held_ref, shared_ref, hidden_ref, block_got, cells_got,
    acc, got, piece, core_out, core_in, pair_got, part_out, part_in, sums, sums_got, out_sem, in_sem,
):
    seq, dp = lax.axis_index("seq"), lax.axis_index("dp")
    core, xi = lax.rem(seq, 2), lax.div(seq, 2)
    count, third = in_ref.shape[1], in_ref.shape[2]
    dims = [1 << b for b in range(ndp.bit_length() - 1)]

    def to(axis, bit):
        return {"dp": flip(dp, bit) if axis == "dp" else dp, "seq": flip(seq, bit) if axis == "seq" else seq}

    partners = [to("seq", 1), to("seq", 2)] + [to("dp", b) for b in dims]
    barrier = pltpu.get_barrier_semaphore()
    for p in partners:
        pl.semaphore_signal(barrier, inc=1, device_id=p, device_id_type=pl.DeviceIdType.MESH)
    pl.semaphore_wait(barrier, len(partners))
    used = []

    def copy(src, dst, target, always=True):
        n = len(used)
        c = pltpu.make_async_remote_copy(
            src_ref=src, dst_ref=dst, send_sem=out_sem.at[n], recv_sem=in_sem.at[n], device_id=target,
            device_id_type=pl.DeviceIdType.MESH)
        used.append((c, always))
        return c

    flying = []
    for i in range(3):
        c = copy(in_ref.at[i, pl.ds(count // 2, count // 2)], got.at[i, pl.ds(0, count // 2)], to(*orders[i][0]))
        c.start()
        flying.append(c)
    mine = core == lax.div(dp, ndp // 2)
    over_dp = copy(pair_ref, pair_got, to("dp", ndp // 2), False)
    over_core = copy(part_out, part_in, to("seq", 1), False)

    @pl.when(jnp.logical_not(mine))
    def _():
        over_dp.start()

    small = []

    def small_step():
        n = len(small)
        if n:
            small[-1].wait_recv()
            sums[n] = sums[n - 1] + sums_got[n - 1]
        else:
            sums[0] = terms_ref[...]
        if n < 2 + len(dims):
            c = copy(sums.at[n], sums_got.at[n], to("seq", 1 << n) if n < 2 else to("dp", dims[n - 2]))
            c.start()
            small.append(c)
        else:
            shared_ref[...] = sums[n]

    small_step()

    steps = len(orders[0])
    size, base = count // 2, 0
    for k in range(steps):
        for i in range(3):
            flying[i].wait_recv()
            for b in range(size):
                kept = in_ref[i, b] if k == 0 else acc[i, b]
                acc[i, b] = (kept.astype(F32) + got[i, base + b].astype(F32)).astype(BF)
            if k + 1 < steps:
                half = size // 2
                c = copy(acc.at[i, pl.ds(half, half)], got.at[i, pl.ds(base + size, half)], to(*orders[i][k + 1]))
                c.start()
                flying[i] = c
        small_step()
        base += size
        size //= 2

    for i in range(3):
        piece[i * third : (i + 1) * third] = acc[i, 0].astype(F32)
    for c in (0, 1):

        @pl.when(core == c)
        def _():
            core_out[...] = piece[(1 - c) * quarter : (2 - c) * quarter].astype(BF)

    swap_core = copy(core_out, core_in, to("seq", 1))
    swap_core.start()
    back = [copy(block_ref.at[1], block_got, to("seq", 2)), copy(cells_ref.at[1], cells_got, to("seq", 2))]
    for c in back:
        c.start()
    swap_core.wait_recv()
    for c in (0, 1):

        @pl.when(core == c)
        def _():
            piece[(1 - c) * quarter : (2 - c) * quarter] = core_in[...].astype(F32)

    held_ref[0] = piece[...].astype(BF)

    ends = []
    for i in range(3):
        rows = pl.ds(i * third, third)
        n = 1
        for k, bit in enumerate(dims[::-1]):
            c = copy(held_ref.at[pl.ds(0, n), rows], held_ref.at[pl.ds(n, n), rows], to("dp", bit))
            c.start()
            n *= 2
            if k + 1 < len(dims):
                c.wait_recv()
            else:
                ends.append(c)
        if i == 0:
            small_step()

    for x in (0, 1):
        for c in (0, 1):

            @pl.when(mine & (xi == x) & (core == c))
            def _():
                over_dp.wait_recv()
                total = pair_ref[...].astype(F32) + pair_got[...].astype(F32)
                hidden_ref[...] = quarter_of(total, x, c, quarter, shift)
                part_out[...] = quarter_of(total, x, 1 - c, quarter, shift).astype(BF)

    @pl.when(mine)
    def _():
        over_core.start()
        over_core.wait_send()

    @pl.when(jnp.logical_not(mine))
    def _():
        over_dp.wait_send()
        over_core.wait_recv()
        hidden_ref[...] = part_in[...].astype(F32)

    for c in ends + back:
        c.wait_recv()
    for c, always in used:
        if always:
            c.wait_send()


def sum_and_gather(blocks, pair, terms, block_rows, cell_rows, ndp, orders, quarter, shift):
    _, count, third, wide = blocks.shape
    _, depth, width = pair.shape
    in_vmem, hbm = pl.BlockSpec(memory_space=pltpu.VMEM), pl.BlockSpec(memory_space=pl.ANY)
    dims = ndp.bit_length() - 1
    copies = 3 * len(orders[0]) + 2 + (2 + dims) + 1 + 2 + 3 * dims
    shape = jax.ShapeDtypeStruct
    outs = [
        shape((ndp, 3 * third, wide), BF), shape(terms.shape, F32), shape((2, depth, quarter), F32),
        shape(block_rows.shape[1:], BF), shape(cell_rows.shape[1:], BF)]
    return pl.pallas_call(
        functools.partial(sum_kernel, ndp, orders, quarter, shift),
        in_specs=[in_vmem] * 3 + [hbm] * 2,
        out_specs=[in_vmem] * 3 + [hbm] * 2,
        out_shape=outs,
        scratch_shapes=[
            pltpu.VMEM((3, count // 2, third, wide), BF),
            pltpu.VMEM((3, count - 1, third, wide), BF),
            pltpu.VMEM((3 * third, wide), F32),
            pltpu.VMEM((quarter, wide), BF),
            pltpu.VMEM((quarter, wide), BF),
            pltpu.VMEM((2, depth, width), BF),
            pltpu.VMEM((2, depth, quarter), BF),
            pltpu.VMEM((2, depth, quarter), BF),
            pltpu.VMEM((3 + dims, *terms.shape), F32),
            pltpu.VMEM((2 + dims, *terms.shape), F32),
            pltpu.SemaphoreType.DMA((copies,)),
            pltpu.SemaphoreType.DMA((copies,)),
        ],
        compiler_params=pltpu.CompilerParams(vmem_limit_bytes=56 << 20, collective_id=0, has_side_effects=True),
        cost_estimate=cost(0, blocks),
        name="sum_and_gather",
    )(blocks, pair, terms, block_rows, cell_rows)


def sum_and_gather_by_steps(blocks, pair, terms, block_rows, cell_rows, ndp, orders, quarter, shift):
    seq, dp = lax.axis_index("seq"), lax.axis_index("dp")
    core, xi = seq % 2, seq // 2
    count = blocks.shape[1]
    thirds = []
    for i in range(3):
        sent, kept = blocks[i, count // 2 :], blocks[i, : count // 2]
        for k, (axis, bit) in enumerate(orders[i]):
            got = swap(sent, axis, bit)
            if k + 1 < len(orders[i]):
                sent, kept = halve(kept, got)
        thirds.append(low(kept.astype(F32) + got.astype(F32))[0])
    piece = jnp.concatenate(thirds, 0)
    halves = piece[: 2 * quarter].reshape(2, quarter, -1)
    ours, theirs = pick(halves, core, 0), swap(pick(halves, 1 - core, 0), "seq", 1)
    held = jnp.concatenate(
        [jnp.where(core == 0, ours, theirs), jnp.where(core == 0, theirs, ours), piece[2 * quarter :]], 0)[None]
    bits = [1 << b for b in range(ndp.bit_length() - 1)]
    for bit in bits[::-1]:
        held = jnp.concatenate([held, swap(held, "dp", bit)], 0)
    for axis, bit in [("seq", 1), ("seq", 2)] + [("dp", b) for b in bits]:
        terms = terms + swap(terms, axis, bit)
    nj = ndp // 2
    across = [(d * 4 + t, (d ^ nj) * 4 + t) for d in range(ndp) for t in range(4) if d // nj != t % 2]
    total = pair.astype(F32) + lax.ppermute(pair, ("dp", "seq"), across).astype(F32)
    parts = [
        jnp.where(xi == 0, quarter_of(total, 0, c, quarter, shift), quarter_of(total, 1, c, quarter, shift)) for c in (0, 1)]
    theirs = swap(low(jnp.where(core == 0, parts[1], parts[0])), "seq", 1).astype(F32)
    hidden = jnp.where(core == dp // nj, jnp.where(core == 0, parts[0], parts[1]), theirs)
    return held, terms, hidden, swap(block_rows[1], "seq", 2), swap(cell_rows[1], "seq", 2)


def assemble_kernel(bits, tiles, held_ref, e_ref, qkv_ref, out_ref, q_ref, o_ref):
    ndp, _, wide = held_ref.shape
    quarter, d = out_ref.shape
    heads, head = e_ref.shape
    tall = o_ref.shape[0] // ndp
    dp = lax.axis_index("dp")
    for j in range(ndp):
        rel = dp ^ j
        slot = sum(jnp.where(rel & b != 0, 1 << k, 0) for k, b in enumerate(bits))
        block = held_ref[slot].astype(F32)
        for c in (0, 1):
            q_ref[c, :, j * wide : (j + 1) * wide] = block[c * quarter : (c + 1) * quarter]
        for t, lo in enumerate(range(0, d, wide)):
            hi = min(lo + wide, d)
            at = 2 * quarter + t * tall
            o_ref[j * tall : (j + 1) * tall, lo:hi] = block[at : at + tall, : hi - lo]
    for part in range(3):
        for c in (0, 1):
            row = jnp.concatenate([q_ref[c, :, 128 * t : 128 * t + 128] for t in tiles[part]], 1)
            lo = part * d + c * head
            qkv_ref[:, lo : lo + head] = nn(row.astype(BF), e_ref[...])
    for h in range(o_ref.shape[0] // 64):
        out_ref[h * HD : (h + 1) * HD] = o_ref[h * 64 : h * 64 + HD]


def assemble(held, e, quarter, d, bits, tiles):
    ndp, _, wide = held.shape
    outs = [jax.ShapeDtypeStruct((quarter, 3 * d), F32), jax.ShapeDtypeStruct((quarter, d), F32)]
    return pl.pallas_call(
        functools.partial(assemble_kernel, bits, tiles),
        in_specs=[pl.BlockSpec(memory_space=pltpu.VMEM)] * 2,
        out_specs=[pl.BlockSpec(memory_space=pltpu.VMEM)] * 2,
        out_shape=outs,
        scratch_shapes=[pltpu.VMEM((2, quarter, ndp * wide), F32), pltpu.VMEM((quarter // HD * 64, d), F32)],
        compiler_params=vmem(40),
        cost_estimate=cost(6 * 2 * quarter * e.size, held, e, *outs),
        name="assemble",
    )(held, e)


def low(value):
    return lax.optimization_barrier(value.astype(BF))


def after(value, *first):
    return lax.optimization_barrier((value, *first))[0]


def swap(value, axis, bit):
    return lax.ppermute(value, axis, [(i, i ^ bit) for i in range(lax.axis_size(axis))])


def swap_by_core(value, steps):
    ndp, nseq = lax.axis_size("dp"), lax.axis_size("seq")
    pairs = []
    for d in range(ndp):
        for s in range(nseq):
            axis, bit = steps[s % 2]
            e, t = (d, s ^ bit) if axis == "seq" else (d ^ bit, s)
            pairs.append((d * nseq + s, e * nseq + t))
    return lax.ppermute(value, ("dp", "seq"), pairs)


def pick(array, index, axis):
    return lax.dynamic_index_in_dim(array, index, axis, keepdims=False)


def one_hot(rows, cols, source):
    r = lax.broadcasted_iota(jnp.int32, (rows, cols), 0)
    return (r == source[None, :]).astype(BF)


def halve(kept, got):
    half = kept.shape[0] // 2
    total = kept.astype(F32) + got.astype(F32)
    return low(total[half:]), low(total[:half])


def per_device(
    cells, prefix_len, ln1_gain, ln1_bias, w_qkv, bias_q, bias_v, w_out, bias_out,
    ln2_gain, ln2_bias, w_up, bias_up, w_down, bias_down, cotangent,
):
    seq, ndp = lax.axis_size("seq"), lax.axis_size("dp")
    s, dp = lax.axis_index("seq"), lax.axis_index("dp")
    core, xi = s % 2, s // 2
    assert seq == 4
    pairs, block, D = cells.shape
    C = pairs // 2
    T = block * seq
    HH = H // 2
    WH = HH * 64
    half = D // 2
    quarter = D // 4
    FF = w_up.shape[1]
    nj = ndp // 2
    R = 2 * C * block
    row = lambda v: v.reshape(1, -1)
    place = s.reshape(1).astype(jnp.int32)

    def split_cells(a):
        return lax.dynamic_slice_in_dim(a, xi * C, C, 0), lax.dynamic_slice_in_dim(a, (1 - xi) * C, C, 0)

    x0, x_other = split_cells(cells)
    x1 = swap(x_other, "seq", 2)
    x0_got = swap(x0, "seq", 1)
    prefix = lax.dynamic_slice_in_dim(prefix_len, xi * C, C, 0)

    col = jnp.arange(WH)
    head_col = jnp.where(col % 64 < HD, core * half + (col // 64) * HD + col % 64, -1)
    w_parts = []
    for j in range(3):
        lo = j * D // 128 * 128
        hi = min(-(-(j + 1) * D // 128) * 128, 3 * D)
        e = one_hot(hi - lo, WH, jnp.where(head_col >= 0, head_col + j * D - lo, -1))
        w_parts.append(jnp.dot(w_qkv[:, lo:hi], e, preferred_element_type=F32).astype(BF))
    cut = FIRST * 128
    in_order = lambda parts: [p[..., :cut] for p in parts] + [p[..., cut:] for p in parts]
    w_own = jnp.concatenate(in_order(w_parts), 1)

    def pad_heads(v, ones):
        v = lax.dynamic_slice_in_dim(v, core * half, half, 0).reshape(HH, HD)
        return jnp.concatenate([v, jnp.full((HH, 3), ones, F32), jnp.zeros((HH, 5), F32)], 1).reshape(WH)

    bias_own = jnp.concatenate(in_order([pad_heads(bias_q, 0.0), pad_heads(jnp.zeros_like(bias_q), 1.0), pad_heads(bias_v, 1.0)]))
    wo = w_out.reshape(2, HH, HD, D)
    wo = jnp.concatenate([wo, jnp.zeros((2, HH, 64 - HD, D), BF)], 2).reshape(2, WH, D)
    wo = jnp.where(core == 0, wo, wo[::-1]).reshape(2 * WH, D)

    x1 = after(x1, wo, w_own)
    x1_got = swap(x1, "seq", 1)
    first, qkv = project(place, (x0, x0_got, x1, x1_got), row(ln1_gain), row(ln1_bias), w_own, row(bias_own))
    c0, c_other = split_cells(cotangent)
    c1 = swap(after(c_other, x1), "seq", 2)
    qkv, c1 = lax.optimization_barrier((qkv, c1))
    c_pair = jnp.concatenate([c0, c1], 0)
    c_got = swap(c_pair, "seq", 1)
    att, q_aug = attention_forward(qkv, prefix)
    att_got = swap(att, "seq", 1)
    middle, second = attention_output(place, att, att_got, x0, x1, wo, row(bias_out), row(ln2_gain), row(ln2_bias))
    blocks = lambda v: v.reshape(-1, block, v.shape[-1])
    rows_of = lambda v: v.reshape(-1, v.shape[-1])
    second_got = rows_of(swap(blocks(second), "seq", 1))
    cot, cot_got = rows_of(c_pair), rows_of(c_got)

    act, gpre, out_own, out_send, gs_own, gs_send, bias_up_sum = hidden_layer(
        second, second_got, cot, cot_got, w_up, row(bias_up), w_down.T, block)
    gs_got = rows_of(swap(blocks(gs_send), "seq", 1))
    out_got = rows_of(swap(blocks(out_send), "seq", 1))

    low_bits = [1 << b for b in range(nj.bit_length() - 1)]
    rest = low_bits[2:]

    def order(*names):
        n = {"x": ("seq", 2), "y": ("dp", 1), "z": ("dp", 2)}
        return [n[k] for k in names] + [("dp", b) for b in rest]

    def codes(steps, n):
        return [n if axis == "seq" else bit for axis, bit in steps]

    down_orders = (order("x", "y", "z"), order("y", "x", "z"))
    up_orders = (order("z", "x", "y"), order("z", "y", "x"))
    top = [("dp", nj)]
    q_orders = [order("x", "y", "z") + top, order("y", "z", "x") + top, order("z", "x", "y") + top]

    def send(sent, orders, k):
        return swap_by_core(sent, (orders[0][k], orders[1][k]))

    d_sent, d_kept = hidden_weights(act, cot, cot_got, FF, nj, [codes(o, nj) for o in down_orders])
    d_got = send(d_sent, down_orders, 0)
    u_sent, u_kept = hidden_weights(gpre, second, second_got, FF, nj, [codes(o, nj) for o in up_orders])
    u_got = send(u_sent, up_orders, 0)

    gmiddle, gbranch, gatt, block_rows, sums2 = middle_back(
        after(gs_own, d_sent, u_sent), gs_got, out_own, out_got, middle, cot, wo, row(ln2_gain), row(bias_down), block)
    gatt_got = swap(gatt, "seq", 1)
    o_send, o_keep = output_weights(place, att, att_got, gbranch, block)
    o_got = swap(o_send, "seq", 1)
    g_out = o_keep + o_got[::-1].astype(F32)

    shape = (2, C, block, 2 * WH)
    gatt, gatt_got = gatt.reshape(shape), gatt_got.reshape(shape)
    d_sent, d_kept = halve(d_kept, d_got)
    d_got = send(d_sent, down_orders, 1)
    g_first = attention_backward(qkv, q_aug, after(gatt, d_sent, g_out), gatt_got, att, prefix, 0, FIRST).reshape(C * T, -1)
    d_sent, d_kept = halve(d_kept, after(d_got, g_first))
    d_got = send(d_sent, down_orders, 2)
    g_rest = attention_backward(
        qkv, q_aug, after(gatt, d_sent), gatt_got, att, prefix, FIRST, WH // 128).reshape(C * T, -1)
    u_sent, u_kept = halve(u_kept, after(u_got, g_rest))
    u_got = send(u_sent, up_orders, 1)
    q_blocks = project_weights(
        first.reshape(C * T, D), [g_first, after(g_rest, u_sent)], -(-3 * WH // (128 * 16)) * 128 * 16, g_out, ndp,
        [codes(o, ndp) for o in q_orders])
    u_sent, u_kept = halve(u_kept, after(u_got, q_blocks))
    u_got = send(u_sent, up_orders, 2)
    for k in range(3, len(down_orders[0])):
        d_sent, d_kept = halve(d_kept, d_got)
        d_got = send(d_sent, down_orders, k)
        u_sent, u_kept = halve(u_kept, u_got)
        u_got = send(u_sent, up_orders, k)
    gfirst, sums_qkv = project_back(g_first, after(g_rest, u_sent), w_own, block)
    gfirst_got = rows_of(swap(blocks(gfirst), "seq", 1)).reshape(C, T, D)
    gfirst = gfirst.reshape(C, T, D)
    pair = low(jnp.concatenate([d_kept, u_kept], 0).astype(F32) + jnp.concatenate([d_got, after(u_got, gfirst)], 0).astype(F32))
    gcells, sums1 = cells_back(place, after(gfirst, pair), gfirst_got, x0, x1, gmiddle, row(ln1_gain))

    unpad = lambda v: v.reshape(HH, 64)[:, :HD].reshape(half)
    own_half = lambda v: jnp.where(core == 0, jnp.concatenate([v, jnp.zeros_like(v)]), jnp.concatenate([jnp.zeros_like(v), v]))
    ff_width = bias_up_sum.shape[1]
    pad_up = FF - ff_width
    g_bias_up = jnp.where(core == 0, jnp.pad(bias_up_sum[0], (0, pad_up)), jnp.pad(bias_up_sum[0], (pad_up, 0)))
    rest_cut = 3 * cut
    more = WH - cut
    sums_of = lambda j: jnp.concatenate([
        sums_qkv[0, j * cut : (j + 1) * cut], sums_qkv[0, rest_cut + j * more : rest_cut + (j + 1) * more]])
    terms = [
        sums1[0], sums1[1], own_half(unpad(sums_of(0))), own_half(unpad(sums_of(2))),
        sums2[0], sums2[1], sums2[2], sums2[3], g_bias_up,
    ]
    terms = jnp.concatenate(terms).reshape(-1, 128)

    bits = [1 << b for b in range(ndp.bit_length() - 1)]
    shift = half - (-(-D // 128) * 128 - 640)
    block_rows = block_rows.reshape(2, C, block, D)
    finish = sum_and_gather if ndp <= 8 else sum_and_gather_by_steps
    held, packed, hidden, block_got, cells_got = finish(
        q_blocks, pair, terms, block_rows, gcells, ndp, q_orders, quarter, shift)
    packed = packed.reshape(-1)
    shared = [packed[i * D : (i + 1) * D] for i in range(8)] + [packed[8 * D :]]

    def both_cells(own, got):
        return jnp.concatenate([jnp.where(xi == 0, own, got), jnp.where(xi == 0, got, own)], 0)

    block_out, grad_cells = both_cells(block_rows[0], block_got), both_cells(gcells[0], cells_got)

    head_of = jnp.arange(half)
    e_out = (jnp.arange(WH)[:, None] == (head_of // HD * 64 + head_of % HD)[None, :]).astype(BF)
    n_pairs = WH // 128
    tiles = [[tile_of(part, p, n_pairs) for p in range(n_pairs)] for part in range(3)]
    final_qkv, final_out = assemble(held, e_out, quarter, D, bits[::-1], tiles)

    final_down, final_up = hidden[0], hidden[1].T

    return (
        block_out, grad_cells, shared[0], shared[1], final_qkv, shared[2], shared[3], final_out,
        shared[4], shared[5], shared[6], final_up, shared[8], final_down, shared[7],
    )


def solution(mesh):
    rows = P("dp", "seq", None)
    return jax.shard_map(
        per_device,
        mesh=mesh,
        in_specs=(rows, P("dp")) + (P(),) * 13 + (rows,),
        out_specs=(rows, rows, P(), P(), P("seq", None), P(), P(), P("seq", None), P(), P(), P(), P("seq", "dp"), P(), P("dp", "seq"), P()),
        check_vma=False,
    )
```

```python
import functools
import math
import jax
import jax.numpy as jnp
from jax import lax
from jax.experimental import pallas as pl
from jax.experimental.pallas import tpu as pltpu
from jax.sharding import PartitionSpec as P

H = 20
HD=56
F32=jnp.float32; BF=jnp.bfloat16
LOG2=math.log2(math.e)
NEG=-1e30
def nt(a,b): return lax.dot_general(a,b,(((1,),(1,)),((),())),preferred_element_type=F32)
def nn(a,b): return lax.dot_general(a,b,(((1,),(0,)),((),())),preferred_element_type=F32)
def tn(a,b): return lax.dot_general(a,b,(((0,),(0,)),((),())),preferred_element_type=F32)

def split3(v):
    a=v.astype(BF); r=v-a.astype(F32); b=r.astype(BF); r=r-b.astype(F32)
    return a.astype(F32),b.astype(F32),r

def dup(k):
    low=lax.broadcasted_iota(jnp.int32,k.shape,1)<64
    r=pltpu.roll(k,64,1)
    return jnp.where(low,k,r).astype(BF), jnp.where(low,r,k).astype(BF)

def fwd_kernel(B, prefix_ref, q_ref,k_ref,v_ref,o_ref,qa_ref):
    T=q_ref.shape[1]
    p=prefix_ref[pl.program_id(0)]
    lane=lax.broadcasted_iota(jnp.int32,(T,128),1); low=lane<64
    q=q_ref[0].astype(F32)*(HD**-0.5*LOG2)
    hi=q.astype(BF).astype(F32); res=pltpu.roll(q-hi,64,1)
    qa=[jnp.where(low,hi,res),jnp.where(low,res,hi)]
    qab=[x.astype(BF) for x in qa]
    ka=dup(k_ref[0].astype(F32))
    lane_b=lane[:B]
    row=lax.broadcasted_iota(jnp.int32,(B,B),0); col=lax.broadcasted_iota(jnp.int32,(B,B),1)
    tri=col<=row
    first=tri|((col<p)&(row<p))
    for i in range(T//B):
        n=(i+1)*B; rows=slice(i*B,n)
        outs=[]
        for h in range(2):
            s=nt(qab[h][rows],ka[h][:n])
            d=jnp.where(first if i==0 else tri,s[:,n-B:],NEG)
            if i: s=jnp.concatenate([s[:,:n-B],d],1)
            else: s=d
            m=jnp.max(s,axis=1,keepdims=True)
            e=jnp.exp2(s-m).astype(BF)
            o=nn(e,v_ref[0,:n])
            l=o[:,56+64*h:57+64*h]
            outs.append(o*(1.0/l))
            lse=-(m+jnp.log2(l))
            a,b,c=split3(lse)
            z=64*h+56
            x=jnp.where(lane_b==z,a,jnp.where(lane_b==z+1,b,jnp.where(lane_b==z+2,c,qa[h][rows])))
            qa_ref[0,rows,128*h:128*h+128]=x.astype(BF)
        o_ref[0,rows]=jnp.where(low[:B],outs[0],outs[1]).astype(BF)

FIRST=3


def tile_of(part,p,pairs):
    if isinstance(p,int):
        return part*FIRST+p if p<FIRST else 3*FIRST+part*(pairs-FIRST)+p-FIRST
    return jnp.where(p<FIRST,part*FIRST+p,3*FIRST+part*(pairs-FIRST)+p-FIRST)


def attention_forward(qkv,prefix,B=256):
    C,T,W=qkv.shape; NP=W//384
    spec=lambda part: pl.BlockSpec((1,T,128),lambda c,p,pr: (c,0,tile_of(part,p,NP)))
    return pl.pallas_call(functools.partial(fwd_kernel,B),
        grid_spec=pltpu.PrefetchScalarGridSpec(num_scalar_prefetch=1,grid=(C,NP),
            in_specs=[spec(0),spec(1),spec(2)],
            out_specs=[pl.BlockSpec((1,T,128),lambda c,p,pr:(c,0,p)),pl.BlockSpec((1,T,256),lambda c,p,pr:(c,0,p))]),
        out_shape=[jax.ShapeDtypeStruct((C,T,128*NP),BF),jax.ShapeDtypeStruct((C,T,256*NP),BF)],
        compiler_params=pltpu.CompilerParams(vmem_limit_bytes=24<<20),
        cost_estimate=pl.CostEstimate(flops=1,bytes_accessed=1,transcendentals=0),
        name="attention_forward",
    )(prefix,qkv,qkv,qkv)

def bwd_kernel(B, prefix_ref, qa_ref,q_ref,k_ref,v_ref,go_ref,gg_ref,o_ref,out_ref,dk_ref,dv_ref,do_ref):
    T=q_ref.shape[1]; NP=pl.num_programs(1); W=out_ref.shape[2]
    block=T//4
    s=lax.axis_index("seq")
    for k,piece in enumerate((go_ref[0,0],go_ref[1,0],gg_ref[0,0],gg_ref[1,0])):
        place=s^(2*(k%2)+k//2)
        do_ref[pl.ds(pl.multiple_of(place*block,block),block)]=piece
    pr=pl.program_id(1)
    p=prefix_ref[pl.program_id(0)]
    lane=lax.broadcasted_iota(jnp.int32,(T,128),1); low=lane<64
    k32=k_ref[0].astype(F32); q32=q_ref[0].astype(F32); do32=do_ref[...].astype(F32)
    ka=dup(k32)
    zero=jnp.zeros_like(k32)
    km=[jnp.where(low,k32,zero).astype(BF),jnp.where(low,zero,k32).astype(BF)]
    qm=[jnp.where(low,q32,zero).astype(BF),jnp.where(low,zero,q32).astype(BF)]
    dom=[jnp.where(low,do32,zero),jnp.where(low,zero,do32)]
    o32=o_ref[0].astype(F32)
    doa=[]
    for h in range(2):
        dl=-jnp.sum(dom[h]*o32,axis=1,keepdims=True)
        a,b,c=split3(dl); z=64*h+56
        doa.append(jnp.where(lane==z,a,jnp.where(lane==z+1,b,jnp.where(lane==z+2,c,dom[h]))).astype(BF))
    dom=[x.astype(BF) for x in dom]
    key=lax.broadcasted_iota(jnp.int32,(B,B),0); qry=lax.broadcasted_iota(jnp.int32,(B,B),1)
    tri=key<=qry
    first=tri|((key<p)&(qry<p))
    sc=HD**-0.5
    for i in reversed(range(T//B)):
        n=(i+1)*B; rows=slice(i*B,n)
        pbs=[];dss=[]
        for h in range(2):
            s=nt(ka[h][:n],qa_ref[0,rows,128*h:128*h+128])
            d=jnp.where(first if i==0 else tri,s[n-B:],NEG)
            s=jnp.concatenate([s[:n-B],d],0) if i else d
            e=jnp.exp2(s)
            dp=nt(v_ref[0,:n],doa[h][rows])
            dss.append((e*dp).astype(BF)); pbs.append(e.astype(BF))
        dq=tn(dss[0],km[0][:n])+tn(dss[1],km[1][:n])
        out_ref[0,rows,pl.ds(pl.multiple_of(pr*128,128),128)]=(dq*sc).astype(BF)
        dv=nn(pbs[0],dom[0][rows])+nn(pbs[1],dom[1][rows])
        dk=nn(dss[0],qm[0][rows])+nn(dss[1],qm[1][rows])
        if i==T//B-1:
            dv_ref[...]=dv; dk_ref[...]=dk
        else:
            dv_ref[:n]+=dv; dk_ref[:n]+=dk
    out_ref[0,:,pl.ds(pl.multiple_of((NP+pr)*128,128),128)]=(dk_ref[...]*sc).astype(BF)
    out_ref[0,:,pl.ds(pl.multiple_of((2*NP+pr)*128,128),128)]=dv_ref[...].astype(BF)

def attention_backward(qkv,qa,do,do_got,o,prefix,p0,p1,B=256):
    C,T,W=qkv.shape; NP=W//384
    width=384*(p1-p0)
    spec=lambda part: pl.BlockSpec((1,T,128),lambda c,p,pr: (c,0,tile_of(part,p0,NP)+p))
    return pl.pallas_call(functools.partial(bwd_kernel,B),
        grid_spec=pltpu.PrefetchScalarGridSpec(num_scalar_prefetch=1,grid=(C,p1-p0),
            in_specs=[pl.BlockSpec((1,T,256),lambda c,p,pr:(c,0,p0+p)),spec(0),spec(1),spec(2),
                pl.BlockSpec((2,1,T//4,128),lambda c,p,pr:(0,c,0,p0+p)),pl.BlockSpec((2,1,T//4,128),lambda c,p,pr:(0,c,0,NP+p0+p)),
                pl.BlockSpec((1,T,128),lambda c,p,pr:(c,0,p0+p))],
            out_specs=pl.BlockSpec((1,T,width),lambda c,p,pr:(c,0,0)),
            scratch_shapes=[pltpu.VMEM((T,128),F32)]*2+[pltpu.VMEM((T,128),BF)]),
        out_shape=jax.ShapeDtypeStruct((C,T,width),BF),
        compiler_params=pltpu.CompilerParams(vmem_limit_bytes=40<<20),
        cost_estimate=pl.CostEstimate(flops=1,bytes_accessed=1,transcendentals=0),
        name="attention_backward",
    )(prefix,qa,qkv,qkv,qkv,do,do_got,o)


epsilon = 1e-05


def vmem(megabytes):
    return pltpu.CompilerParams(vmem_limit_bytes=megabytes << 20)


def whole(array):
    return pl.BlockSpec(array.shape, lambda *_: (0,) * array.ndim, pipeline_mode=pl.Buffered(1))


def cost(flops, *arrays):
    return pl.CostEstimate(flops=1, bytes_accessed=1, transcendentals=0)


def block_norm(rows):
    width = rows.shape[1]
    mean = jnp.sum(rows, axis=1, keepdims=True) * (1.0 / width)
    centred = rows - mean
    rstd = lax.rsqrt(jnp.sum(centred * centred, axis=1, keepdims=True) * (1.0 / width) + epsilon)
    return centred * rstd, rstd


def block_norm_back(grad, normed, rstd, gain):
    inv = 1.0 / grad.shape[1]
    dn = grad * gain
    a = jnp.sum(dn, axis=1, keepdims=True) * inv
    b = jnp.sum(dn * normed, axis=1, keepdims=True) * inv
    return rstd * (dn - a - normed * b)


def add_sums(ref, start, *rows):
    for k, v in enumerate(rows):
        total = jnp.sum(v, axis=0, keepdims=True)
        ref[k : k + 1] = jnp.where(start, total, ref[k : k + 1] + total)


def project_kernel(s_ref, a_ref, b_ref, c_ref, d_ref, g_ref, h_ref, w_ref, bias_ref, first_ref, out_ref):
    k = pl.program_id(1)
    x = jnp.where(k < 2, jnp.where(k == 0, a_ref[0].astype(F32), b_ref[0].astype(F32)),
                  jnp.where(k == 2, c_ref[0].astype(F32), d_ref[0].astype(F32)))
    n, _ = block_norm(x)
    first = (n * g_ref[...] + h_ref[...]).astype(BF)
    first_ref[0] = first
    width = w_ref.shape[1]
    for lo in range(0, width, 640):
        cols = slice(lo, min(lo + 640, width))
        out_ref[0, :, cols] = (nn(first, w_ref[:, cols]) + bias_ref[:, cols]).astype(BF)


def project(place, pieces, gain, shift, w, bias):
    cells, rows, d = pieces[0].shape
    width = w.shape[1]
    piece = pl.BlockSpec((1, rows, d), lambda c, k, s: (c, 0, 0))
    at = lambda c, k, s: (c, s[0] ^ k, 0)
    ins = (gain, shift, w, bias)
    outs = [jax.ShapeDtypeStruct((cells, 4 * rows, n), BF) for n in (d, width)]
    return pl.pallas_call(
        project_kernel,
        grid_spec=pltpu.PrefetchScalarGridSpec(
            num_scalar_prefetch=1, grid=(cells, 4), in_specs=[piece] * 4 + [whole(a) for a in ins],
            out_specs=[pl.BlockSpec((1, rows, n), at) for n in (d, width)]),
        out_shape=outs,
        compiler_params=vmem(40),
        cost_estimate=cost(8 * cells * rows * w.size, *pieces, *ins, *outs),
        name="norm_project",
    )(place, *pieces, *ins)


def middle_kernel(s_ref, own_ref, got_ref, a_ref, b_ref, w_ref, c_ref, g_ref, h_ref, middle_ref, second_ref):
    half = own_ref.shape[2]
    out = nn(own_ref[0], w_ref[:half]) + nn(got_ref[0], w_ref[half:])
    x = jnp.where(pl.program_id(0) == 0, a_ref[0].astype(F32), b_ref[0].astype(F32))
    middle = x + out + c_ref[...]
    middle_ref[...] = middle
    n, _ = block_norm(middle)
    second_ref[...] = (n * g_ref[...] + h_ref[...]).astype(BF)


def attention_output(place, own, got, x0, x1, w, bias, gain, shift):
    cells, rows, d = x0.shape
    half = own.shape[2]
    at = pl.BlockSpec((1, rows, half), lambda k, c, s: (c, s[0] ^ (2 * k), 0))
    piece = pl.BlockSpec((1, rows, d), lambda k, c, s: (c, 0, 0))
    ins = (w, bias, gain, shift)
    outs = [jax.ShapeDtypeStruct((2 * cells * rows, d), t) for t in (F32, BF)]
    return pl.pallas_call(
        middle_kernel,
        grid_spec=pltpu.PrefetchScalarGridSpec(
            num_scalar_prefetch=1, grid=(2, cells), in_specs=[at, at, piece, piece] + [whole(a) for a in ins],
            out_specs=[pl.BlockSpec((rows, d), lambda k, c, s: (k * cells + c, 0))] * 2),
        out_shape=outs,
        compiler_params=vmem(32),
        cost_estimate=cost(4 * cells * rows * w.size, x0, x0, *ins, *outs),
        name="attention_output",
    )(place, own, got, x0, x1, *ins)


CHUNK = 768


def hidden_window(core, ff):
    width = -(-(ff // 2) // CHUNK) * CHUNK
    return core * (ff - width), width, core * (width - ff // 2)


def hidden_kernel(
    ff, s0_ref, s1_ref, c0_ref, c1_ref, bu_ref, wu_hbm, wd_hbm,
    act_ref, gpre_ref, out0_ref, out1_ref, gs0_ref, gs1_ref, sum_ref, wu_ref, wd_ref, sem,
):
    i, n = pl.program_id(0), pl.num_programs(0) // 2
    core = lax.rem(lax.axis_index("seq"), 2)
    start, width, skip = hidden_window(core, ff)
    chunks = width // CHUNK

    def copies(k):
        at = pl.multiple_of(start + k * CHUNK, 128)
        cols = pl.ds(k * CHUNK, CHUNK)
        return (
            pltpu.make_async_copy(wu_hbm.at[:, pl.ds(at, CHUNK)], wu_ref.at[:, cols], sem.at[2 * k]),
            pltpu.make_async_copy(wd_hbm.at[:, pl.ds(at, CHUNK)], wd_ref.at[:, cols], sem.at[2 * k + 1]),
        )

    @pl.when(i == 0)
    def _():
        for k in range(chunks):
            for c in copies(k):
                c.start()

    second = jnp.where(i < n, s0_ref[...].astype(F32), s1_ref[...].astype(F32)).astype(BF)
    cot = jnp.where(i < n, c0_ref[...].astype(F32), c1_ref[...].astype(F32)).astype(BF)
    out = gsec = None
    a, b = 0.7978845608, 0.044715
    for k in range(chunks):
        cols = slice(k * CHUNK, (k + 1) * CHUNK)

        @pl.when(i == 0)
        def _():
            for c in copies(k):
                c.wait()

        u = nn(second, wu_ref[:, cols]) + bu_ref[:, pl.ds(pl.multiple_of(start + k * CHUNK, 128), CHUNK)]
        gact = nn(cot, wd_ref[:, cols])
        u2 = u * u
        t = jnp.tanh(u * (a + a * b * u2))
        h = 0.5 + 0.5 * t
        act = u * h
        gpre = gact * (h + u * (0.5 - 0.5 * t * t) * (a + 3 * a * b * u2))
        if k in (0, chunks - 1):
            col = lax.broadcasted_iota(jnp.int32, (1, CHUNK), 1) + k * CHUNK
            mine = (col >= skip) & (col < skip + ff // 2)
            act, gpre = jnp.where(mine, act, 0.0), jnp.where(mine, gpre, 0.0)
        act, gpre = act.astype(BF), gpre.astype(BF)
        act_ref[:, cols] = act
        gpre_ref[:, cols] = gpre
        total = jnp.sum(gpre.astype(F32), axis=0, keepdims=True)
        sum_ref[:, cols] = jnp.where(i == 0, total, sum_ref[:, cols] + total)
        o, g = nt(act, wd_ref[:, cols]), nt(gpre, wu_ref[:, cols])
        out, gsec = (o, g) if out is None else (out + o, gsec + g)

    @pl.when(i < n)
    def _():
        out0_ref[...] = out.astype(BF)
        gs0_ref[...] = gsec.astype(BF)

    @pl.when(i >= n)
    def _():
        out1_ref[...] = out.astype(BF)
        gs1_ref[...] = gsec.astype(BF)


def hidden_layer(second, second_got, cot, cot_got, w_up, bias_up, w_down_t, m):
    rows, d = second.shape
    ff = w_up.shape[1]
    n = rows // m
    width = hidden_window(0, ff)[1]
    lo = pl.BlockSpec((m, d), lambda i: (jnp.minimum(i, n - 1), 0))
    hi = pl.BlockSpec((m, d), lambda i: (jnp.maximum(i - n, 0), 0))
    row = pl.BlockSpec((m, width), lambda i: (i, 0))
    hbm = pl.BlockSpec(memory_space=pl.ANY)
    shape = jax.ShapeDtypeStruct
    outs = [shape((2 * rows, width), BF)] * 2 + [shape((rows, d), BF)] * 4 + [shape((1, width), F32)]
    return pl.pallas_call(
        functools.partial(hidden_kernel, ff),
        grid=(2 * n,),
        in_specs=[lo, hi, lo, hi, whole(bias_up), hbm, hbm],
        out_specs=[row, row, lo, hi, lo, hi, pl.BlockSpec((1, width), lambda i: (0, 0))],
        out_shape=outs,
        scratch_shapes=[pltpu.VMEM((d, width), BF), pltpu.VMEM((d, width), BF), pltpu.SemaphoreType.DMA((2 * (width // CHUNK),))],
        compiler_params=vmem(56),
        cost_estimate=cost(16 * rows * d * width, second, second, cot, cot, w_up, *outs),
        name="hidden_layer",
    )(second, second_got, cot, cot_got, bias_up, w_up, w_down_t)


def middle_back_kernel(
    gs_ref, gs_got_ref, o_ref, o_got_ref, middle_ref, cot_ref, w_ref, g_ref, c_ref,
    gm_ref, gb_ref, gatt_ref, block_ref, sum_ref,
):
    middle, gy = middle_ref[...], cot_ref[...].astype(F32)
    gsecond = gs_ref[...].astype(F32) + gs_got_ref[...].astype(F32)
    n, rstd = block_norm(middle)
    gmiddle = gy + block_norm_back(gsecond, n, rstd, g_ref[...])
    gm_ref[...] = gmiddle
    gbranch = gmiddle.astype(BF)
    gb_ref[...] = gbranch
    gatt_ref[...] = nt(gbranch, w_ref[...]).astype(BF)
    block_ref[...] = (middle + (o_ref[...].astype(F32) + o_got_ref[...].astype(F32)) + c_ref[...]).astype(BF)
    add_sums(sum_ref, pl.program_id(0) == 0, gbranch.astype(F32), gsecond * n, gsecond, gy)


def middle_back(gsec, gsec_got, out, out_got, middle, cot, w, gain, bias, m):
    rows, d = middle.shape
    row = lambda n: pl.BlockSpec((m, n), lambda i: (i, 0))
    ins = (gsec, gsec_got, out, out_got, middle, cot, w, gain, bias)
    shape = jax.ShapeDtypeStruct
    heads = w.shape[0]
    outs = [shape((rows, d), F32), shape((rows, d), BF), shape((rows, heads), BF), shape((rows, d), BF), shape((4, d), F32)]
    return pl.pallas_call(
        middle_back_kernel,
        grid=(rows // m,),
        in_specs=[row(d)] * 6 + [whole(a) for a in ins[6:]],
        out_specs=[row(d), row(d), row(heads), row(d), pl.BlockSpec((4, d), lambda i: (0, 0))],
        out_shape=outs,
        compiler_params=vmem(40),
        cost_estimate=cost(2 * rows * w.size, *ins, *outs),
        name="middle_back",
    )(*ins)


def project_back_kernel(a_ref, b_ref, w_ref, out_ref, sum_ref):
    split = a_ref.shape[1]
    out_ref[...] = (nt(a_ref[...], w_ref[:, :split]) + nt(b_ref[...], w_ref[:, split:])).astype(BF)
    start = pl.program_id(0) == 0
    for ref, cols in ((a_ref, slice(0, split)), (b_ref, slice(split, None))):
        total = jnp.sum(ref[...].astype(F32), axis=0, keepdims=True)
        sum_ref[:, cols] = jnp.where(start, total, sum_ref[:, cols] + total)


def project_back(a, b, w, m):
    rows = a.shape[0]
    d, width = w.shape
    outs = [jax.ShapeDtypeStruct((rows, d), BF), jax.ShapeDtypeStruct((1, width), F32)]
    return pl.pallas_call(
        project_back_kernel,
        grid=(rows // m,),
        in_specs=[pl.BlockSpec((m, a.shape[1]), lambda i: (i, 0)), pl.BlockSpec((m, b.shape[1]), lambda i: (i, 0)), whole(w)],
        out_specs=[pl.BlockSpec((m, d), lambda i: (i, 0)), pl.BlockSpec((1, width), lambda i: (0, 0))],
        out_shape=outs,
        compiler_params=vmem(32),
        cost_estimate=cost(2 * rows * w.size, a, b, w, *outs),
        name="project_back",
    )(a, b, w)


def cells_back_kernel(s_ref, g_ref, got_ref, a_ref, b_ref, gm_ref, gain_ref, out_ref, sum_ref):
    k = pl.program_id(0)
    g = g_ref[0].astype(F32) + got_ref[0].astype(F32)
    n, rstd = block_norm(jnp.where(k == 0, a_ref[0].astype(F32), b_ref[0].astype(F32)))
    out_ref[0, 0] = (gm_ref[...] + block_norm_back(g, n, rstd, gain_ref[...])).astype(BF)
    add_sums(sum_ref, (k == 0) & (pl.program_id(1) == 0), g * n, g)


def cells_back(place, g, got, x0, x1, gmiddle, gain):
    cells, rows, d = x0.shape
    at = pl.BlockSpec((1, rows, d), lambda k, c, s: (c, s[0] ^ (2 * k), 0))
    piece = pl.BlockSpec((1, rows, d), lambda k, c, s: (c, 0, 0))
    outs = [jax.ShapeDtypeStruct((2, cells, rows, d), BF), jax.ShapeDtypeStruct((2, d), F32)]
    return pl.pallas_call(
        cells_back_kernel,
        grid_spec=pltpu.PrefetchScalarGridSpec(
            num_scalar_prefetch=1, grid=(2, cells),
            in_specs=[at, at, piece, piece, pl.BlockSpec((rows, d), lambda k, c, s: (k * cells + c, 0)), whole(gain)],
            out_specs=[pl.BlockSpec((1, 1, rows, d), lambda k, c, s: (k, c, 0, 0)), pl.BlockSpec((2, d), lambda k, c, s: (0, 0))]),
        out_shape=outs,
        compiler_params=vmem(32),
        cost_estimate=cost(0, x0, x0, x0, x0, x0, x0, gmiddle, *outs),
        name="cells_back",
    )(place, g, got, x0, x1, gmiddle, gain)


def store_block(orders, rel, value, sent_ref, kept_ref):
    core = lax.rem(lax.axis_index("seq"), 2)
    half = kept_ref.shape[0]
    places = [
        sum(jnp.where(rel & step != 0, half >> k, 0) for k, step in enumerate(steps)) for steps in orders
    ]
    pos = jnp.where(core == 0, places[0], places[1])

    @pl.when(pos >= half)
    def _():
        sent_ref[pos - half] = value

    @pl.when(pos < half)
    def _():
        kept_ref[pos] = value


def hidden_weights_kernel(orders, ff, nj, lhs_ref, own_ref, got_ref, sent_ref, kept_ref, rhs_ref, acc_ref):
    rows, d = own_ref.shape
    pad = rhs_ref.shape[1]
    step, steps = pl.program_id(0), pl.num_programs(0)
    seq, dp = lax.axis_index("seq"), lax.axis_index("dp")
    core, xi = lax.rem(seq, 2), lax.div(seq, 2)
    depth = ff // 2 // nj

    @pl.when(step == 0)
    def _():
        rhs_ref[:rows, :d] = own_ref[...]
        rhs_ref[rows:, :d] = got_ref[...]
        rhs_ref[:, d:] = jnp.zeros((2 * rows, pad - d), BF)

    wide = lhs_ref.shape[1]
    acc_ref[pl.ds(pl.multiple_of(step * wide, wide), wide)] = tn(lhs_ref[...], rhs_ref[...])
    for c in (0, 1):

        @pl.when((core == c) & (step == steps - 1))
        def _():
            for x in (0, 1):
                for j in range(nj):
                    at = hidden_window(c, ff)[2] + j * depth
                    rel = (x ^ xi) * nj + (j ^ lax.rem(dp, nj))
                    value = acc_ref[at : at + depth, x * (pad - 640) : x * (pad - 640) + 640]
                    store_block(orders, rel, value.astype(BF), sent_ref, kept_ref)


def hidden_weights(lhs, own, got, ff, nj, orders):
    rows, d = own.shape
    width = lhs.shape[1]
    pad = -(-d // 128) * 128
    depth = ff // 2 // nj
    outs = [jax.ShapeDtypeStruct((nj, depth, 640), BF)] * 2
    full = lambda: pl.BlockSpec((nj, depth, 640), lambda *_: (0, 0, 0), pipeline_mode=pl.Buffered(1))
    return pl.pallas_call(
        functools.partial(hidden_weights_kernel, orders, ff, nj),
        grid=(width // 256,),
        in_specs=[pl.BlockSpec((2 * rows, 256), lambda i: (0, i)), whole(own), whole(got)],
        out_specs=[full(), full()],
        out_shape=outs,
        scratch_shapes=[pltpu.VMEM((2 * rows, pad), BF), pltpu.VMEM((width, pad), F32)],
        compiler_params=vmem(48),
        cost_estimate=cost(4 * rows * width * pad, lhs, own, got, *outs),
        name="hidden_weights",
    )(lhs, own, got)


def output_weights_kernel(s_ref, own_ref, got_ref, g_ref, send_ref, keep_ref, acc_ref):
    k, c = pl.program_id(0), pl.program_id(1)
    start = (k == 0) & (c == 0)
    for h, ref in enumerate((own_ref, got_ref)):
        total = tn(ref[0], g_ref[...])
        acc_ref[h] = jnp.where(start, total, acc_ref[h] + total)
    core = lax.rem(lax.axis_index("seq"), 2)
    half = keep_ref.shape[1]
    for mine in (0, 1):

        @pl.when((k == 1) & (c == pl.num_programs(1) - 1) & (core == mine))
        def _():
            for h in (0, 1):
                keep_ref[h] = acc_ref[h, mine * half : (mine + 1) * half]
                send_ref[h] = acc_ref[h, (1 - mine) * half : (2 - mine) * half].astype(BF)


def output_weights(place, own, got, g, rows):
    cells, _, width = own.shape
    d = g.shape[1]
    at = pl.BlockSpec((1, rows, width), lambda k, c, s: (c, s[0] ^ (2 * k), 0))
    shape = (2, width // 2, d)
    outs = [jax.ShapeDtypeStruct(shape, BF), jax.ShapeDtypeStruct(shape, F32)]
    return pl.pallas_call(
        output_weights_kernel,
        grid_spec=pltpu.PrefetchScalarGridSpec(
            num_scalar_prefetch=1, grid=(2, cells),
            in_specs=[at, at, pl.BlockSpec((rows, d), lambda k, c, s: (k * cells + c, 0))],
            out_specs=[pl.BlockSpec(shape, lambda *_: (0, 0, 0), pipeline_mode=pl.Buffered(1))] * 2,
            scratch_shapes=[pltpu.VMEM((2, width, d), F32)]),
        out_shape=outs,
        compiler_params=vmem(32),
        cost_estimate=cost(8 * cells * rows * width * d, own, got, g, *outs),
        name="output_weights",
    )(place, own, got, g)


def place_in(steps, rel, count):
    return sum(jnp.where(rel & step != 0, count >> (k + 1), 0) for k, step in enumerate(steps))


def project_weights_kernel(orders, ndp, half, lhs_ref, rhs_refs, out_ref, blocks_ref, acc_ref, block_ref):
    step, steps = pl.program_id(0), pl.num_programs(0)
    seq, dp = lax.axis_index("seq"), lax.axis_index("dp")
    xi, core = lax.div(seq, 2), lax.rem(seq, 2)
    m = lhs_ref.shape[1]
    lo = 0
    rows = pl.ds(pl.multiple_of(step * m, m), m)
    for ref in rhs_refs:
        wide = ref.shape[1]
        acc_ref[rows, lo : lo + wide] = tn(lhs_ref[...], ref[...])
        lo += wide
    acc_ref[rows, lo:] = jnp.zeros((m, acc_ref.shape[1] - lo), F32)

    @pl.when(step == steps - 1)
    def _():
        wide = acc_ref.shape[1] // ndp
        third = block_ref.shape[0] // 3
        block_ref[half:] = jnp.zeros((3 * third - half, wide), F32)
        tall = out_ref.shape[1] // ndp
        for x in (0, 1):
            for j in range(ndp):
                block_ref[:half] = acc_ref[x * half : (x + 1) * half, j * wide : (j + 1) * wide]
                strip = out_ref[x ^ core, j * tall : (j + 1) * tall]
                for t, lo in enumerate(range(0, 2 * half, wide)):
                    hi = min(lo + wide, 2 * half)
                    block_ref[half + t * tall : half + (t + 1) * tall, : hi - lo] = strip[:, lo:hi]
                rel = (x ^ xi) * ndp + (j ^ dp)
                for i in range(3):
                    blocks_ref[i, place_in(orders[i], rel, 2 * ndp)] = block_ref[i * third : (i + 1) * third].astype(BF)


def project_weights(lhs, parts, width, out, ndp, orders):
    rows_in, d = lhs.shape
    m = 256
    steps = -(-d // m)
    wide = width // ndp
    third = -(-(d // 2 + -(-d // wide) * (out.shape[1] // ndp)) // 48) * 16
    block = (3, 2 * ndp, third, wide)
    n = len(parts)

    def kernel(lhs_ref, *refs):
        project_weights_kernel(orders, ndp, d // 2, lhs_ref, refs[:n], *refs[n:])

    return pl.pallas_call(
        kernel,
        grid=(steps,),
        in_specs=[pl.BlockSpec((rows_in, m), lambda i: (0, i))] + [whole(a) for a in (*parts, out)],
        out_specs=pl.BlockSpec(block, lambda *_: (0, 0, 0, 0), pipeline_mode=pl.Buffered(1)),
        out_shape=jax.ShapeDtypeStruct(block, BF),
        scratch_shapes=[pltpu.VMEM((steps * m, width), F32), pltpu.VMEM((3 * third, wide), F32)],
        compiler_params=vmem(48),
        cost_estimate=cost(2 * rows_in * d * width, lhs, out),
        name="project_weights",
    )(lhs, *parts, out)


def flip(index, bit):
    return index + bit - 2 * bit * lax.rem(lax.div(index, bit), 2)


def quarter_of(pair, x, c, quarter, shift):
    lo = x * shift + c * quarter
    return pair[:, :, lo : lo + quarter]


def sum_kernel(
    ndp, orders, quarter, shift, in_ref, pair_ref, terms_ref, block_ref, cells_ref,
    held_ref, shared_ref, hidden_ref, block_got, cells_got,
    acc, got, piece, core_out, core_in, pair_got, part_out, part_in, sums, sums_got, out_sem, in_sem,
):
    seq, dp = lax.axis_index("seq"), lax.axis_index("dp")
    core, xi = lax.rem(seq, 2), lax.div(seq, 2)
    count, third = in_ref.shape[1], in_ref.shape[2]
    dims = [1 << b for b in range(ndp.bit_length() - 1)]

    def to(axis, bit):
        return {"dp": flip(dp, bit) if axis == "dp" else dp, "seq": flip(seq, bit) if axis == "seq" else seq}

    partners = [to("seq", 1), to("seq", 2)] + [to("dp", b) for b in dims]
    barrier = pltpu.get_barrier_semaphore()
    for p in partners:
        pl.semaphore_signal(barrier, inc=1, device_id=p, device_id_type=pl.DeviceIdType.MESH)
    pl.semaphore_wait(barrier, len(partners))
    used = []

    def copy(src, dst, target, always=True):
        n = len(used)
        c = pltpu.make_async_remote_copy(
            src_ref=src, dst_ref=dst, send_sem=out_sem.at[n], recv_sem=in_sem.at[n], device_id=target,
            device_id_type=pl.DeviceIdType.MESH)
        used.append((c, always))
        return c

    part = third // 2
    steps = len(orders[0])
    flying = {}

    def start(i, h, k):
        half = count >> (k + 1)
        rows = pl.ds(h * part, part)
        src = (in_ref if k == 0 else acc).at[i, pl.ds(half, half), rows]
        c = copy(src, got.at[i, pl.ds(count - 2 * half, half), rows], to(*orders[i][k]))
        c.start()
        flying[i, h] = c

    def finish(i, h, k):
        flying[i, h].wait_recv()
        half = count >> (k + 1)
        rows = slice(h * part, (h + 1) * part)
        for b in range(half):
            kept = in_ref[i, b, rows] if k == 0 else acc[i, b, rows]
            acc[i, b, rows] = (kept.astype(F32) + got[i, count - 2 * half + b, rows].astype(F32)).astype(BF)
        if k + 1 < steps:
            start(i, h, k + 1)

    for i in range(3):
        start(i, 0, 0)
    mine = core == lax.div(dp, ndp // 2)
    over_dp = copy(pair_ref, pair_got, to("dp", ndp // 2), False)
    over_core = copy(part_out, part_in, to("seq", 1), False)

    @pl.when(jnp.logical_not(mine))
    def _():
        over_dp.start()

    small = []

    def small_step():
        n = len(small)
        if n:
            small[-1].wait_recv()
            sums[n] = sums[n - 1] + sums_got[n - 1]
        else:
            sums[0] = terms_ref[...]
        if n < 2 + len(dims):
            c = copy(sums.at[n], sums_got.at[n], to("seq", 1 << n) if n < 2 else to("dp", dims[n - 2]))
            c.start()
            small.append(c)
        else:
            shared_ref[...] = sums[n]

    small_step()

    for i in range(3):
        finish(i, 0, 0)
        start(i, 1, 0)
    small_step()
    for k in range(1, steps):
        for h in (0, 1):
            for i in range(3):
                finish(i, h, k - h)
        if k < 4:
            small_step()
    for i in range(3):
        finish(i, 1, steps - 1)

    for i in range(3):
        piece[i * third : (i + 1) * third] = acc[i, 0].astype(F32)
    for c in (0, 1):

        @pl.when(core == c)
        def _():
            core_out[...] = piece[(1 - c) * quarter : (2 - c) * quarter].astype(BF)

    swap_core = copy(core_out, core_in, to("seq", 1))
    swap_core.start()
    back = [copy(block_ref.at[1], block_got, to("seq", 2)), copy(cells_ref.at[1], cells_got, to("seq", 2))]
    for c in back:
        c.start()
    swap_core.wait_recv()
    for c in (0, 1):

        @pl.when(core == c)
        def _():
            piece[(1 - c) * quarter : (2 - c) * quarter] = core_in[...].astype(F32)

    held_ref[0] = piece[...].astype(BF)

    ends = []
    far = dims[::-1]
    parts = 6
    rows_of = [pl.ds(i * (3 * third // parts), 3 * third // parts) for i in range(parts)]

    def share(i, k):
        n = 1 << k
        c = copy(held_ref.at[pl.ds(0, n), rows_of[i]], held_ref.at[pl.ds(n, n), rows_of[i]], to("dp", far[k]))
        c.start()
        return c

    first = share(0, 0)
    for i in range(parts):
        first.wait_recv()
        c = share(i, 1)
        if i + 1 < parts:
            first = share(i + 1, 0)
        for k in range(2, len(far)):
            c.wait_recv()
            c = share(i, k)
        ends.append(c)
        if i == 0:
            small_step()

    for x in (0, 1):
        for c in (0, 1):

            @pl.when(mine & (xi == x) & (core == c))
            def _():
                over_dp.wait_recv()
                total = pair_ref[...].astype(F32) + pair_got[...].astype(F32)
                hidden_ref[...] = quarter_of(total, x, c, quarter, shift)
                part_out[...] = quarter_of(total, x, 1 - c, quarter, shift).astype(BF)

    @pl.when(mine)
    def _():
        over_core.start()
        over_core.wait_send()

    @pl.when(jnp.logical_not(mine))
    def _():
        over_dp.wait_send()
        over_core.wait_recv()
        hidden_ref[...] = part_in[...].astype(F32)

    for c in ends + back:
        c.wait_recv()
    for c, always in used:
        if always:
            c.wait_send()


def sum_and_gather(blocks, pair, terms, block_rows, cell_rows, ndp, orders, quarter, shift):
    _, count, third, wide = blocks.shape
    _, depth, width = pair.shape
    in_vmem, hbm = pl.BlockSpec(memory_space=pltpu.VMEM), pl.BlockSpec(memory_space=pl.ANY)
    dims = ndp.bit_length() - 1
    copies = 6 * len(orders[0]) + 2 + (2 + dims) + 1 + 2 + 6 * dims
    shape = jax.ShapeDtypeStruct
    outs = [
        shape((ndp, 3 * third, wide), BF), shape(terms.shape, F32), shape((2, depth, quarter), F32),
        shape(block_rows.shape[1:], BF), shape(cell_rows.shape[1:], BF)]
    return pl.pallas_call(
        functools.partial(sum_kernel, ndp, orders, quarter, shift),
        in_specs=[in_vmem] * 3 + [hbm] * 2,
        out_specs=[in_vmem] * 3 + [hbm] * 2,
        out_shape=outs,
        scratch_shapes=[
            pltpu.VMEM((3, count // 2, third, wide), BF),
            pltpu.VMEM((3, count - 1, third, wide), BF),
            pltpu.VMEM((3 * third, wide), F32),
            pltpu.VMEM((quarter, wide), BF),
            pltpu.VMEM((quarter, wide), BF),
            pltpu.VMEM((2, depth, width), BF),
            pltpu.VMEM((2, depth, quarter), BF),
            pltpu.VMEM((2, depth, quarter), BF),
            pltpu.VMEM((3 + dims, *terms.shape), F32),
            pltpu.VMEM((2 + dims, *terms.shape), F32),
            pltpu.SemaphoreType.DMA((copies,)),
            pltpu.SemaphoreType.DMA((copies,)),
        ],
        compiler_params=pltpu.CompilerParams(vmem_limit_bytes=56 << 20, collective_id=0, has_side_effects=True),
        cost_estimate=cost(0, blocks),
        name="sum_and_gather",
    )(blocks, pair, terms, block_rows, cell_rows)


def sum_and_gather_by_steps(blocks, pair, terms, block_rows, cell_rows, ndp, orders, quarter, shift):
    seq, dp = lax.axis_index("seq"), lax.axis_index("dp")
    core, xi = seq % 2, seq // 2
    count = blocks.shape[1]
    thirds = []
    for i in range(3):
        sent, kept = blocks[i, count // 2 :], blocks[i, : count // 2]
        for k, (axis, bit) in enumerate(orders[i]):
            got = swap(sent, axis, bit)
            if k + 1 < len(orders[i]):
                sent, kept = halve(kept, got)
        thirds.append(low(kept.astype(F32) + got.astype(F32))[0])
    piece = jnp.concatenate(thirds, 0)
    halves = piece[: 2 * quarter].reshape(2, quarter, -1)
    ours, theirs = pick(halves, core, 0), swap(pick(halves, 1 - core, 0), "seq", 1)
    held = jnp.concatenate(
        [jnp.where(core == 0, ours, theirs), jnp.where(core == 0, theirs, ours), piece[2 * quarter :]], 0)[None]
    bits = [1 << b for b in range(ndp.bit_length() - 1)]
    for bit in bits[::-1]:
        held = jnp.concatenate([held, swap(held, "dp", bit)], 0)
    for axis, bit in [("seq", 1), ("seq", 2)] + [("dp", b) for b in bits]:
        terms = terms + swap(terms, axis, bit)
    nj = ndp // 2
    across = [(d * 4 + t, (d ^ nj) * 4 + t) for d in range(ndp) for t in range(4) if d // nj != t % 2]
    total = pair.astype(F32) + lax.ppermute(pair, ("dp", "seq"), across).astype(F32)
    parts = [
        jnp.where(xi == 0, quarter_of(total, 0, c, quarter, shift), quarter_of(total, 1, c, quarter, shift)) for c in (0, 1)]
    theirs = swap(low(jnp.where(core == 0, parts[1], parts[0])), "seq", 1).astype(F32)
    hidden = jnp.where(core == dp // nj, jnp.where(core == 0, parts[0], parts[1]), theirs)
    return held, terms, hidden, swap(block_rows[1], "seq", 2), swap(cell_rows[1], "seq", 2)


def assemble_kernel(bits, tiles, held_ref, e_ref, qkv_ref, out_ref, q_ref, o_ref):
    ndp, _, wide = held_ref.shape
    quarter, d = out_ref.shape
    heads, head = e_ref.shape
    tall = o_ref.shape[0] // ndp
    dp = lax.axis_index("dp")
    for j in range(ndp):
        rel = dp ^ j
        slot = sum(jnp.where(rel & b != 0, 1 << k, 0) for k, b in enumerate(bits))
        block = held_ref[slot].astype(F32)
        for c in (0, 1):
            q_ref[c, :, j * wide : (j + 1) * wide] = block[c * quarter : (c + 1) * quarter]
        for t, lo in enumerate(range(0, d, wide)):
            hi = min(lo + wide, d)
            at = 2 * quarter + t * tall
            o_ref[j * tall : (j + 1) * tall, lo:hi] = block[at : at + tall, : hi - lo]
    for part in range(3):
        for c in (0, 1):
            row = jnp.concatenate([q_ref[c, :, 128 * t : 128 * t + 128] for t in tiles[part]], 1)
            lo = part * d + c * head
            qkv_ref[:, lo : lo + head] = nn(row.astype(BF), e_ref[...])
    for h in range(o_ref.shape[0] // 64):
        out_ref[h * HD : (h + 1) * HD] = o_ref[h * 64 : h * 64 + HD]


def assemble(held, e, quarter, d, bits, tiles):
    ndp, _, wide = held.shape
    outs = [jax.ShapeDtypeStruct((quarter, 3 * d), F32), jax.ShapeDtypeStruct((quarter, d), F32)]
    return pl.pallas_call(
        functools.partial(assemble_kernel, bits, tiles),
        in_specs=[pl.BlockSpec(memory_space=pltpu.VMEM)] * 2,
        out_specs=[pl.BlockSpec(memory_space=pltpu.VMEM)] * 2,
        out_shape=outs,
        scratch_shapes=[pltpu.VMEM((2, quarter, ndp * wide), F32), pltpu.VMEM((quarter // HD * 64, d), F32)],
        compiler_params=vmem(40),
        cost_estimate=cost(6 * 2 * quarter * e.size, held, e, *outs),
        name="assemble",
    )(held, e)


def low(value):
    return lax.optimization_barrier(value.astype(BF))


def after(value, *first):
    return lax.optimization_barrier((value, *first))[0]


def swap(value, axis, bit):
    return lax.ppermute(value, axis, [(i, i ^ bit) for i in range(lax.axis_size(axis))])


def swap_by_core(value, steps):
    ndp, nseq = lax.axis_size("dp"), lax.axis_size("seq")
    pairs = []
    for d in range(ndp):
        for s in range(nseq):
            axis, bit = steps[s % 2]
            e, t = (d, s ^ bit) if axis == "seq" else (d ^ bit, s)
            pairs.append((d * nseq + s, e * nseq + t))
    return lax.ppermute(value, ("dp", "seq"), pairs)


def pick(array, index, axis):
    return lax.dynamic_index_in_dim(array, index, axis, keepdims=False)


def one_hot(rows, cols, source):
    r = lax.broadcasted_iota(jnp.int32, (rows, cols), 0)
    return (r == source[None, :]).astype(BF)


def halve(kept, got):
    half = kept.shape[0] // 2
    total = kept.astype(F32) + got.astype(F32)
    return low(total[half:]), low(total[:half])


def per_device(
    cells, prefix_len, ln1_gain, ln1_bias, w_qkv, bias_q, bias_v, w_out, bias_out,
    ln2_gain, ln2_bias, w_up, bias_up, w_down, bias_down, cotangent,
):
    seq, ndp = lax.axis_size("seq"), lax.axis_size("dp")
    s, dp = lax.axis_index("seq"), lax.axis_index("dp")
    core, xi = s % 2, s // 2
    assert seq == 4
    pairs, block, D = cells.shape
    C = pairs // 2
    T = block * seq
    HH = H // 2
    WH = HH * 64
    half = D // 2
    quarter = D // 4
    FF = w_up.shape[1]
    nj = ndp // 2
    R = 2 * C * block
    row = lambda v: v.reshape(1, -1)
    place = s.reshape(1).astype(jnp.int32)

    def split_cells(a):
        return lax.dynamic_slice_in_dim(a, xi * C, C, 0), lax.dynamic_slice_in_dim(a, (1 - xi) * C, C, 0)

    x0, x_other = split_cells(cells)
    x1 = swap(x_other, "seq", 2)
    x0_got = swap(x0, "seq", 1)
    prefix = lax.dynamic_slice_in_dim(prefix_len, xi * C, C, 0)

    col = jnp.arange(WH)
    head_col = jnp.where(col % 64 < HD, core * half + (col // 64) * HD + col % 64, -1)
    w_parts = []
    for j in range(3):
        lo = j * D // 128 * 128
        hi = min(-(-(j + 1) * D // 128) * 128, 3 * D)
        e = one_hot(hi - lo, WH, jnp.where(head_col >= 0, head_col + j * D - lo, -1))
        w_parts.append(jnp.dot(w_qkv[:, lo:hi], e, preferred_element_type=F32).astype(BF))
    cut = FIRST * 128
    in_order = lambda parts: [p[..., :cut] for p in parts] + [p[..., cut:] for p in parts]
    w_own = jnp.concatenate(in_order(w_parts), 1)

    def pad_heads(v, ones):
        v = lax.dynamic_slice_in_dim(v, core * half, half, 0).reshape(HH, HD)
        return jnp.concatenate([v, jnp.full((HH, 3), ones, F32), jnp.zeros((HH, 5), F32)], 1).reshape(WH)

    bias_own = jnp.concatenate(in_order([pad_heads(bias_q, 0.0), pad_heads(jnp.zeros_like(bias_q), 1.0), pad_heads(bias_v, 1.0)]))
    wo = w_out.reshape(2, HH, HD, D)
    wo = jnp.concatenate([wo, jnp.zeros((2, HH, 64 - HD, D), BF)], 2).reshape(2, WH, D)
    wo = jnp.where(core == 0, wo, wo[::-1]).reshape(2 * WH, D)

    x1 = after(x1, wo, w_own)
    x1_got = swap(x1, "seq", 1)
    first, qkv = project(place, (x0, x0_got, x1, x1_got), row(ln1_gain), row(ln1_bias), w_own, row(bias_own))
    c0, c_other = split_cells(cotangent)
    c1 = swap(after(c_other, x1), "seq", 2)
    qkv, c1 = lax.optimization_barrier((qkv, c1))
    c_pair = jnp.concatenate([c0, c1], 0)
    c_got = swap(c_pair, "seq", 1)
    att, q_aug = attention_forward(qkv, prefix)
    att_got = swap(att, "seq", 1)
    middle, second = attention_output(place, att, att_got, x0, x1, wo, row(bias_out), row(ln2_gain), row(ln2_bias))
    blocks = lambda v: v.reshape(-1, block, v.shape[-1])
    rows_of = lambda v: v.reshape(-1, v.shape[-1])
    second_got = rows_of(swap(blocks(second), "seq", 1))
    cot, cot_got = rows_of(c_pair), rows_of(c_got)

    act, gpre, out_own, out_send, gs_own, gs_send, bias_up_sum = hidden_layer(
        second, second_got, cot, cot_got, w_up, row(bias_up), w_down.T, block)
    gs_got = rows_of(swap(blocks(gs_send), "seq", 1))
    out_got = rows_of(swap(blocks(out_send), "seq", 1))

    low_bits = [1 << b for b in range(nj.bit_length() - 1)]
    rest = low_bits[2:]

    def order(*names):
        n = {"x": ("seq", 2), "y": ("dp", 1), "z": ("dp", 2)}
        return [n[k] for k in names] + [("dp", b) for b in rest]

    def codes(steps, n):
        return [n if axis == "seq" else bit for axis, bit in steps]

    down_orders = (order("x", "z", "y"), order("y", "x", "z"))
    up_orders = (order("z", "x", "y"), order("y", "z", "x"))
    top = [("dp", nj)]
    q_orders = [order("x", "y", "z") + top, order("y", "z", "x") + top, order("z", "x", "y") + top]

    def send(sent, orders, k):
        return swap_by_core(sent, (orders[0][k], orders[1][k]))

    d_sent, d_kept = hidden_weights(act, cot, cot_got, FF, nj, [codes(o, nj) for o in down_orders])
    d_got = send(d_sent, down_orders, 0)
    u_sent, u_kept = hidden_weights(gpre, second, second_got, FF, nj, [codes(o, nj) for o in up_orders])
    u_got = send(u_sent, up_orders, 0)

    gmiddle, gbranch, gatt, block_rows, sums2 = middle_back(
        after(gs_own, d_sent, u_sent), gs_got, out_own, out_got, middle, cot, wo, row(ln2_gain), row(bias_down), block)
    gatt_got = swap(gatt, "seq", 1)
    o_send, o_keep = output_weights(place, att, att_got, gbranch, block)
    o_got = swap(o_send, "seq", 1)
    g_out = o_keep + o_got[::-1].astype(F32)

    shape = (2, C, block, 2 * WH)
    gatt, gatt_got = gatt.reshape(shape), gatt_got.reshape(shape)
    d_sent, d_kept = halve(d_kept, d_got)
    d_got = send(d_sent, down_orders, 1)
    g_first = attention_backward(qkv, q_aug, after(gatt, d_sent, g_out), gatt_got, att, prefix, 0, FIRST).reshape(C * T, -1)
    d_sent, d_kept = halve(d_kept, after(d_got, g_first))
    d_got = send(d_sent, down_orders, 2)
    u_sent, u_kept = halve(u_kept, after(u_got, d_sent))
    u_got = send(u_sent, up_orders, 1)
    g_rest = attention_backward(
        qkv, q_aug, after(gatt, d_sent, u_sent), gatt_got, att, prefix, FIRST, WH // 128).reshape(C * T, -1)
    u_sent, u_kept = halve(u_kept, after(u_got, g_rest))
    u_got = send(u_sent, up_orders, 2)
    q_blocks = project_weights(
        first.reshape(C * T, D), [g_first, after(g_rest, u_sent)], -(-3 * WH // (128 * 16)) * 128 * 16, g_out, ndp,
        [codes(o, ndp) for o in q_orders])
    for k in range(3, len(down_orders[0])):
        d_sent, d_kept = halve(d_kept, d_got)
        d_got = send(d_sent, down_orders, k)
        u_sent, u_kept = halve(u_kept, u_got)
        u_got = send(u_sent, up_orders, k)
    d_got, u_got, q_blocks = lax.optimization_barrier((d_got, u_got, q_blocks))
    pair = low(jnp.concatenate([d_kept, u_kept], 0).astype(F32) + jnp.concatenate([d_got, u_got], 0).astype(F32))
    gfirst, sums_qkv = project_back(g_first, after(g_rest, pair), w_own, block)
    gfirst_got = rows_of(swap(blocks(gfirst), "seq", 1)).reshape(C, T, D)
    gfirst = gfirst.reshape(C, T, D)
    gcells, sums1 = cells_back(place, gfirst, gfirst_got, x0, x1, gmiddle, row(ln1_gain))

    unpad = lambda v: v.reshape(HH, 64)[:, :HD].reshape(half)
    own_half = lambda v: jnp.where(core == 0, jnp.concatenate([v, jnp.zeros_like(v)]), jnp.concatenate([jnp.zeros_like(v), v]))
    ff_width = bias_up_sum.shape[1]
    pad_up = FF - ff_width
    g_bias_up = jnp.where(core == 0, jnp.pad(bias_up_sum[0], (0, pad_up)), jnp.pad(bias_up_sum[0], (pad_up, 0)))
    rest_cut = 3 * cut
    more = WH - cut
    sums_of = lambda j: jnp.concatenate([
        sums_qkv[0, j * cut : (j + 1) * cut], sums_qkv[0, rest_cut + j * more : rest_cut + (j + 1) * more]])
    terms = [
        sums1[0], sums1[1], own_half(unpad(sums_of(0))), own_half(unpad(sums_of(2))),
        sums2[0], sums2[1], sums2[2], sums2[3], g_bias_up,
    ]
    terms = jnp.concatenate(terms).reshape(-1, 128)

    bits = [1 << b for b in range(ndp.bit_length() - 1)]
    shift = half - (-(-D // 128) * 128 - 640)
    block_rows = block_rows.reshape(2, C, block, D)
    finish = sum_and_gather if ndp <= 8 else sum_and_gather_by_steps
    held, packed, hidden, block_got, cells_got = finish(
        q_blocks, pair, terms, block_rows, gcells, ndp, q_orders, quarter, shift)
    packed = packed.reshape(-1)
    shared = [packed[i * D : (i + 1) * D] for i in range(8)] + [packed[8 * D :]]

    def both_cells(own, got):
        return jnp.concatenate([jnp.where(xi == 0, own, got), jnp.where(xi == 0, got, own)], 0)

    block_out, grad_cells = both_cells(block_rows[0], block_got), both_cells(gcells[0], cells_got)

    head_of = jnp.arange(half)
    e_out = (jnp.arange(WH)[:, None] == (head_of // HD * 64 + head_of % HD)[None, :]).astype(BF)
    n_pairs = WH // 128
    tiles = [[tile_of(part, p, n_pairs) for p in range(n_pairs)] for part in range(3)]
    final_qkv, final_out = assemble(held, e_out, quarter, D, bits[::-1], tiles)

    final_down, final_up = hidden[0], hidden[1].T

    return (
        block_out, grad_cells, shared[0], shared[1], final_qkv, shared[2], shared[3], final_out,
        shared[4], shared[5], shared[6], final_up, shared[8], final_down, shared[7],
    )


def solution(mesh):
    rows = P("dp", "seq", None)
    return jax.shard_map(
        per_device,
        mesh=mesh,
        in_specs=(rows, P("dp")) + (P(),) * 13 + (rows,),
        out_specs=(rows, rows, P(), P(), P("seq", None), P(), P(), P("seq", None), P(), P(), P(), P("seq", "dp"), P(), P("dp", "seq"), P()),
        check_vma=False,
    )
```

```python
import functools
import math
import jax
import jax.numpy as jnp
from jax import lax
from jax.experimental import pallas as pl
from jax.experimental.pallas import tpu as pltpu
from jax.sharding import PartitionSpec as P

H = 20
HD=56
F32=jnp.float32; BF=jnp.bfloat16
LOG2=math.log2(math.e)
NEG=-1e30
def nt(a,b): return lax.dot_general(a,b,(((1,),(1,)),((),())),preferred_element_type=F32)
def nn(a,b): return lax.dot_general(a,b,(((1,),(0,)),((),())),preferred_element_type=F32)
def tn(a,b): return lax.dot_general(a,b,(((0,),(0,)),((),())),preferred_element_type=F32)

def split3(v):
    a=v.astype(BF); r=v-a.astype(F32); b=r.astype(BF); r=r-b.astype(F32)
    return a.astype(F32),b.astype(F32),r

def dup(k):
    low=lax.broadcasted_iota(jnp.int32,k.shape,1)<64
    r=pltpu.roll(k,64,1)
    return jnp.where(low,k,r).astype(BF), jnp.where(low,r,k).astype(BF)

def fwd_kernel(B, prefix_ref, q_ref,k_ref,v_ref,o_ref,qa_ref):
    T=q_ref.shape[1]
    p=prefix_ref[pl.program_id(0)]
    lane=lax.broadcasted_iota(jnp.int32,(T,128),1); low=lane<64
    q=q_ref[0].astype(F32)*(HD**-0.5*LOG2)
    hi=q.astype(BF).astype(F32); res=pltpu.roll(q-hi,64,1)
    qa=[jnp.where(low,hi,res),jnp.where(low,res,hi)]
    qab=[x.astype(BF) for x in qa]
    ka=dup(k_ref[0].astype(F32))
    lane_b=lane[:B]
    v32=v_ref[0].astype(F32)
    vm=[jnp.where(low,v32,0.0).astype(BF),jnp.where(low,0.0,v32).astype(BF)]
    row=lax.broadcasted_iota(jnp.int32,(B,B),0); col=lax.broadcasted_iota(jnp.int32,(B,B),1)
    tri=col<=row
    first=tri|((col<p)&(row<p))
    for i in range(T//B):
        n=(i+1)*B; rows=slice(i*B,n)
        outs=[]
        for h in range(2):
            s=nt(qab[h][rows],ka[h][:n])
            d=jnp.where(first if i==0 else tri,s[:,n-B:],NEG)
            if i: s=jnp.concatenate([s[:,:n-B],d],1)
            else: s=d
            m=jnp.max(s,axis=1,keepdims=True)
            outs.append((jnp.exp2(s-m).astype(BF),m))
        o=nn(jnp.concatenate([outs[0][0],outs[1][0]],1),jnp.concatenate([vm[0][:n],vm[1][:n]],0))
        ls=[o[:,56:57],o[:,120:121]]
        for h in range(2):
            lse=-(outs[h][1]+jnp.log2(ls[h]))
            a,b,c=split3(lse)
            z=64*h+56
            x=jnp.where(lane_b==z,a,jnp.where(lane_b==z+1,b,jnp.where(lane_b==z+2,c,qa[h][rows])))
            qa_ref[0,rows,128*h:128*h+128]=x.astype(BF)
        o_ref[0,rows]=(o*jnp.where(low[:B],1.0/ls[0],1.0/ls[1])).astype(BF)


FIRST=3


def tile_of(part,p,pairs):
    if isinstance(p,int):
        return part*FIRST+p if p<FIRST else 3*FIRST+part*(pairs-FIRST)+p-FIRST
    return jnp.where(p<FIRST,part*FIRST+p,3*FIRST+part*(pairs-FIRST)+p-FIRST)


def attention_forward(qkv,prefix,B=256):
    C,T,W=qkv.shape; NP=W//384
    spec=lambda part: pl.BlockSpec((1,T,128),lambda c,p,pr: (c,0,tile_of(part,p,NP)))
    return pl.pallas_call(functools.partial(fwd_kernel,B),
        grid_spec=pltpu.PrefetchScalarGridSpec(num_scalar_prefetch=1,grid=(C,NP),
            in_specs=[spec(0),spec(1),spec(2)],
            out_specs=[pl.BlockSpec((1,T,128),lambda c,p,pr:(c,0,p)),pl.BlockSpec((1,T,256),lambda c,p,pr:(c,0,p))]),
        out_shape=[jax.ShapeDtypeStruct((C,T,128*NP),BF),jax.ShapeDtypeStruct((C,T,256*NP),BF)],
        compiler_params=pltpu.CompilerParams(vmem_limit_bytes=40<<20),
        cost_estimate=pl.CostEstimate(flops=1,bytes_accessed=1,transcendentals=0),
        name="attention_forward",
    )(prefix,qkv,qkv,qkv)

def bwd_kernel(B, prefix_ref, qa_ref,q_ref,k_ref,v_ref,go_ref,gg_ref,o_ref,out_ref,dk_ref,dv_ref,do_ref):
    T=q_ref.shape[1]; NP=pl.num_programs(1); W=out_ref.shape[2]
    block=T//4
    s=lax.axis_index("seq")
    for k,piece in enumerate((go_ref[0,0],go_ref[1,0],gg_ref[0,0],gg_ref[1,0])):
        place=s^(2*(k%2)+k//2)
        do_ref[pl.ds(pl.multiple_of(place*block,block),block)]=piece
    pr=pl.program_id(1)
    p=prefix_ref[pl.program_id(0)]
    lane=lax.broadcasted_iota(jnp.int32,(T,128),1); low=lane<64
    k32=k_ref[0].astype(F32); q32=q_ref[0].astype(F32); do32=do_ref[...].astype(F32)
    ka=dup(k32)
    zero=jnp.zeros_like(k32)
    km=[jnp.where(low,k32,zero).astype(BF),jnp.where(low,zero,k32).astype(BF)]
    qm=[jnp.where(low,q32,zero).astype(BF),jnp.where(low,zero,q32).astype(BF)]
    dom=[jnp.where(low,do32,zero),jnp.where(low,zero,do32)]
    o32=o_ref[0].astype(F32)
    doa=[]
    for h in range(2):
        dl=-jnp.sum(dom[h]*o32,axis=1,keepdims=True)
        a,b,c=split3(dl); z=64*h+56
        doa.append(jnp.where(lane==z,a,jnp.where(lane==z+1,b,jnp.where(lane==z+2,c,dom[h]))).astype(BF))
    dom=[x.astype(BF) for x in dom]
    key=lax.broadcasted_iota(jnp.int32,(B,B),0); qry=lax.broadcasted_iota(jnp.int32,(B,B),1)
    tri=key<=qry
    first=tri|((key<p)&(qry<p))
    sc=HD**-0.5
    for i in reversed(range(T//B)):
        n=(i+1)*B; rows=slice(i*B,n)
        pbs=[];dss=[]
        for h in range(2):
            s=nt(ka[h][:n],qa_ref[0,rows,128*h:128*h+128])
            d=jnp.where(first if i==0 else tri,s[n-B:],NEG)
            s=jnp.concatenate([s[:n-B],d],0) if i else d
            e=jnp.exp2(s)
            dp=nt(v_ref[0,:n],doa[h][rows])
            dss.append((e*dp).astype(BF)); pbs.append(e.astype(BF))
        dq=tn(jnp.concatenate(dss,0),jnp.concatenate([km[0][:n],km[1][:n]],0))
        out_ref[0,rows,pl.ds(pl.multiple_of(pr*128,128),128)]=(dq*sc).astype(BF)
        dv=nn(pbs[0],dom[0][rows])+nn(pbs[1],dom[1][rows])
        dk=nn(dss[0],qm[0][rows])+nn(dss[1],qm[1][rows])
        if i==T//B-1:
            dv_ref[...]=dv; dk_ref[...]=dk
        else:
            dv_ref[:n]+=dv; dk_ref[:n]+=dk
    out_ref[0,:,pl.ds(pl.multiple_of((NP+pr)*128,128),128)]=(dk_ref[...]*sc).astype(BF)
    out_ref[0,:,pl.ds(pl.multiple_of((2*NP+pr)*128,128),128)]=dv_ref[...].astype(BF)

def attention_backward(qkv,qa,do,do_got,o,prefix,p0,p1,B=256):
    C,T,W=qkv.shape; NP=W//384
    width=384*(p1-p0)
    spec=lambda part: pl.BlockSpec((1,T,128),lambda c,p,pr: (c,0,tile_of(part,p0,NP)+p))
    return pl.pallas_call(functools.partial(bwd_kernel,B),
        grid_spec=pltpu.PrefetchScalarGridSpec(num_scalar_prefetch=1,grid=(C,p1-p0),
            in_specs=[pl.BlockSpec((1,T,256),lambda c,p,pr:(c,0,p0+p)),spec(0),spec(1),spec(2),
                pl.BlockSpec((2,1,T//4,128),lambda c,p,pr:(0,c,0,p0+p)),pl.BlockSpec((2,1,T//4,128),lambda c,p,pr:(0,c,0,NP+p0+p)),
                pl.BlockSpec((1,T,128),lambda c,p,pr:(c,0,p0+p))],
            out_specs=pl.BlockSpec((1,T,width),lambda c,p,pr:(c,0,0)),
            scratch_shapes=[pltpu.VMEM((T,128),F32)]*2+[pltpu.VMEM((T,128),BF)]),
        out_shape=jax.ShapeDtypeStruct((C,T,width),BF),
        compiler_params=pltpu.CompilerParams(vmem_limit_bytes=40<<20),
        cost_estimate=pl.CostEstimate(flops=1,bytes_accessed=1,transcendentals=0),
        name="attention_backward",
    )(prefix,qa,qkv,qkv,qkv,do,do_got,o)


epsilon = 1e-05


def vmem(megabytes):
    return pltpu.CompilerParams(vmem_limit_bytes=megabytes << 20)


def whole(array):
    return pl.BlockSpec(array.shape, lambda *_: (0,) * array.ndim, pipeline_mode=pl.Buffered(1))


def cost(flops, *arrays):
    return pl.CostEstimate(flops=1, bytes_accessed=1, transcendentals=0)


def block_norm(rows):
    width = rows.shape[1]
    mean = jnp.sum(rows, axis=1, keepdims=True) * (1.0 / width)
    centred = rows - mean
    rstd = lax.rsqrt(jnp.sum(centred * centred, axis=1, keepdims=True) * (1.0 / width) + epsilon)
    return centred * rstd, rstd


def block_norm_back(grad, normed, rstd, gain):
    inv = 1.0 / grad.shape[1]
    dn = grad * gain
    a = jnp.sum(dn, axis=1, keepdims=True) * inv
    b = jnp.sum(dn * normed, axis=1, keepdims=True) * inv
    return rstd * (dn - a - normed * b)


def add_sums(ref, start, *rows):
    for k, v in enumerate(rows):
        total = jnp.sum(v, axis=0, keepdims=True)
        ref[k : k + 1] = jnp.where(start, total, ref[k : k + 1] + total)


def project_kernel(s_ref, a_ref, b_ref, c_ref, d_ref, g_ref, h_ref, w_ref, bias_ref, first_ref, out_ref):
    k = pl.program_id(1)
    x = jnp.where(k < 2, jnp.where(k == 0, a_ref[0].astype(F32), b_ref[0].astype(F32)),
                  jnp.where(k == 2, c_ref[0].astype(F32), d_ref[0].astype(F32)))
    n, _ = block_norm(x)
    first = (n * g_ref[...] + h_ref[...]).astype(BF)
    first_ref[0] = first
    width = w_ref.shape[1]
    for lo in range(0, width, 640):
        cols = slice(lo, min(lo + 640, width))
        out_ref[0, :, cols] = (nn(first, w_ref[:, cols]) + bias_ref[:, cols]).astype(BF)


def project(place, pieces, gain, shift, w, bias):
    cells, rows, d = pieces[0].shape
    width = w.shape[1]
    piece = pl.BlockSpec((1, rows, d), lambda c, k, s: (c, 0, 0))
    at = lambda c, k, s: (c, s[0] ^ k, 0)
    ins = (gain, shift, w, bias)
    outs = [jax.ShapeDtypeStruct((cells, 4 * rows, n), BF) for n in (d, width)]
    return pl.pallas_call(
        project_kernel,
        grid_spec=pltpu.PrefetchScalarGridSpec(
            num_scalar_prefetch=1, grid=(cells, 4), in_specs=[piece] * 4 + [whole(a) for a in ins],
            out_specs=[pl.BlockSpec((1, rows, n), at) for n in (d, width)]),
        out_shape=outs,
        compiler_params=vmem(40),
        cost_estimate=cost(8 * cells * rows * w.size, *pieces, *ins, *outs),
        name="norm_project",
    )(place, *pieces, *ins)


def middle_kernel(s_ref, own_ref, got_ref, a_ref, b_ref, w_ref, c_ref, g_ref, h_ref, middle_ref, second_ref):
    half = own_ref.shape[2]
    out = nn(own_ref[0], w_ref[:half]) + nn(got_ref[0], w_ref[half:])
    x = jnp.where(pl.program_id(0) == 0, a_ref[0].astype(F32), b_ref[0].astype(F32))
    middle = x + out + c_ref[...]
    middle_ref[...] = middle
    n, _ = block_norm(middle)
    second_ref[...] = (n * g_ref[...] + h_ref[...]).astype(BF)


def attention_output(place, own, got, x0, x1, w, bias, gain, shift):
    cells, rows, d = x0.shape
    half = own.shape[2]
    at = pl.BlockSpec((1, rows, half), lambda k, c, s: (c, s[0] ^ (2 * k), 0))
    piece = pl.BlockSpec((1, rows, d), lambda k, c, s: (c, 0, 0))
    ins = (w, bias, gain, shift)
    outs = [jax.ShapeDtypeStruct((2 * cells * rows, d), t) for t in (F32, BF)]
    return pl.pallas_call(
        middle_kernel,
        grid_spec=pltpu.PrefetchScalarGridSpec(
            num_scalar_prefetch=1, grid=(2, cells), in_specs=[at, at, piece, piece] + [whole(a) for a in ins],
            out_specs=[pl.BlockSpec((rows, d), lambda k, c, s: (k * cells + c, 0))] * 2),
        out_shape=outs,
        compiler_params=vmem(32),
        cost_estimate=cost(4 * cells * rows * w.size, x0, x0, *ins, *outs),
        name="attention_output",
    )(place, own, got, x0, x1, *ins)


CHUNK = 768


def hidden_window(core, ff):
    width = -(-(ff // 2) // CHUNK) * CHUNK
    return core * (ff - width), width, core * (width - ff // 2)


def hidden_kernel(
    ff, s0_ref, s1_ref, c0_ref, c1_ref, bu_ref, wu_hbm, wd_hbm,
    act_ref, gpre_ref, out0_ref, out1_ref, gs0_ref, gs1_ref, sum_ref, wu_ref, wd_ref, sem,
):
    i, n = pl.program_id(0), pl.num_programs(0) // 2
    core = lax.rem(lax.axis_index("seq"), 2)
    start, width, skip = hidden_window(core, ff)
    chunks = width // CHUNK

    def copies(k):
        at = pl.multiple_of(start + k * CHUNK, 128)
        cols = pl.ds(k * CHUNK, CHUNK)
        return (
            pltpu.make_async_copy(wu_hbm.at[:, pl.ds(at, CHUNK)], wu_ref.at[:, cols], sem.at[2 * k]),
            pltpu.make_async_copy(wd_hbm.at[:, pl.ds(at, CHUNK)], wd_ref.at[:, cols], sem.at[2 * k + 1]),
        )

    @pl.when(i == 0)
    def _():
        for k in range(chunks):
            for c in copies(k):
                c.start()

    second = jnp.where(i < n, s0_ref[...].astype(F32), s1_ref[...].astype(F32)).astype(BF)
    cot = jnp.where(i < n, c0_ref[...].astype(F32), c1_ref[...].astype(F32)).astype(BF)
    out = gsec = None
    a, b = 0.7978845608, 0.044715
    for k in range(chunks):
        cols = slice(k * CHUNK, (k + 1) * CHUNK)

        @pl.when(i == 0)
        def _():
            for c in copies(k):
                c.wait()

        u = nn(second, wu_ref[:, cols]) + bu_ref[:, pl.ds(pl.multiple_of(start + k * CHUNK, 128), CHUNK)]
        gact = nn(cot, wd_ref[:, cols])
        u2 = u * u
        t = jnp.tanh(u * (a + a * b * u2))
        h = 0.5 + 0.5 * t
        act = u * h
        gpre = gact * (h + u * (0.5 - 0.5 * t * t) * (a + 3 * a * b * u2))
        if k in (0, chunks - 1):
            col = lax.broadcasted_iota(jnp.int32, (1, CHUNK), 1) + k * CHUNK
            mine = (col >= skip) & (col < skip + ff // 2)
            act, gpre = jnp.where(mine, act, 0.0), jnp.where(mine, gpre, 0.0)
        act, gpre = act.astype(BF), gpre.astype(BF)
        act_ref[:, cols] = act
        gpre_ref[:, cols] = gpre
        total = jnp.sum(gpre.astype(F32), axis=0, keepdims=True)
        sum_ref[:, cols] = jnp.where(i == 0, total, sum_ref[:, cols] + total)
        o, g = nt(act, wd_ref[:, cols]), nt(gpre, wu_ref[:, cols])
        out, gsec = (o, g) if out is None else (out + o, gsec + g)

    @pl.when(i < n)
    def _():
        out0_ref[...] = out.astype(BF)
        gs0_ref[...] = gsec.astype(BF)

    @pl.when(i >= n)
    def _():
        out1_ref[...] = out.astype(BF)
        gs1_ref[...] = gsec.astype(BF)


def hidden_layer(second, second_got, cot, cot_got, w_up, bias_up, w_down_t, m):
    rows, d = second.shape
    ff = w_up.shape[1]
    n = rows // m
    width = hidden_window(0, ff)[1]
    lo = pl.BlockSpec((m, d), lambda i: (jnp.minimum(i, n - 1), 0))
    hi = pl.BlockSpec((m, d), lambda i: (jnp.maximum(i - n, 0), 0))
    row = pl.BlockSpec((m, width), lambda i: (i, 0))
    hbm = pl.BlockSpec(memory_space=pl.ANY)
    shape = jax.ShapeDtypeStruct
    outs = [shape((2 * rows, width), BF)] * 2 + [shape((rows, d), BF)] * 4 + [shape((1, width), F32)]
    return pl.pallas_call(
        functools.partial(hidden_kernel, ff),
        grid=(2 * n,),
        in_specs=[lo, hi, lo, hi, whole(bias_up), hbm, hbm],
        out_specs=[row, row, lo, hi, lo, hi, pl.BlockSpec((1, width), lambda i: (0, 0))],
        out_shape=outs,
        scratch_shapes=[pltpu.VMEM((d, width), BF), pltpu.VMEM((d, width), BF), pltpu.SemaphoreType.DMA((2 * (width // CHUNK),))],
        compiler_params=vmem(56),
        cost_estimate=cost(16 * rows * d * width, second, second, cot, cot, w_up, *outs),
        name="hidden_layer",
    )(second, second_got, cot, cot_got, bias_up, w_up, w_down_t)


def middle_back_kernel(
    gs_ref, gs_got_ref, o_ref, o_got_ref, middle_ref, cot_ref, w_ref, g_ref, c_ref,
    gm_ref, gb_ref, gatt_ref, block_ref, sum_ref,
):
    middle, gy = middle_ref[...], cot_ref[...].astype(F32)
    gsecond = gs_ref[...].astype(F32) + gs_got_ref[...].astype(F32)
    n, rstd = block_norm(middle)
    gmiddle = gy + block_norm_back(gsecond, n, rstd, g_ref[...])
    gm_ref[...] = gmiddle
    gbranch = gmiddle.astype(BF)
    gb_ref[...] = gbranch
    gatt_ref[...] = nt(gbranch, w_ref[...]).astype(BF)
    block_ref[...] = (middle + (o_ref[...].astype(F32) + o_got_ref[...].astype(F32)) + c_ref[...]).astype(BF)
    add_sums(sum_ref, pl.program_id(0) == 0, gbranch.astype(F32), gsecond * n, gsecond, gy)


def middle_back(gsec, gsec_got, out, out_got, middle, cot, w, gain, bias, m):
    rows, d = middle.shape
    row = lambda n: pl.BlockSpec((m, n), lambda i: (i, 0))
    ins = (gsec, gsec_got, out, out_got, middle, cot, w, gain, bias)
    shape = jax.ShapeDtypeStruct
    heads = w.shape[0]
    outs = [shape((rows, d), F32), shape((rows, d), BF), shape((rows, heads), BF), shape((rows, d), BF), shape((4, d), F32)]
    return pl.pallas_call(
        middle_back_kernel,
        grid=(rows // m,),
        in_specs=[row(d)] * 6 + [whole(a) for a in ins[6:]],
        out_specs=[row(d), row(d), row(heads), row(d), pl.BlockSpec((4, d), lambda i: (0, 0))],
        out_shape=outs,
        compiler_params=vmem(40),
        cost_estimate=cost(2 * rows * w.size, *ins, *outs),
        name="middle_back",
    )(*ins)


def project_back_kernel(a_ref, b_ref, w_ref, out_ref, sum_ref):
    split = a_ref.shape[1]
    out_ref[...] = (nt(a_ref[...], w_ref[:, :split]) + nt(b_ref[...], w_ref[:, split:])).astype(BF)
    start = pl.program_id(0) == 0
    for ref, cols in ((a_ref, slice(0, split)), (b_ref, slice(split, None))):
        total = jnp.sum(ref[...].astype(F32), axis=0, keepdims=True)
        sum_ref[:, cols] = jnp.where(start, total, sum_ref[:, cols] + total)


def project_back(a, b, w, m):
    rows = a.shape[0]
    d, width = w.shape
    outs = [jax.ShapeDtypeStruct((rows, d), BF), jax.ShapeDtypeStruct((1, width), F32)]
    return pl.pallas_call(
        project_back_kernel,
        grid=(rows // m,),
        in_specs=[pl.BlockSpec((m, a.shape[1]), lambda i: (i, 0)), pl.BlockSpec((m, b.shape[1]), lambda i: (i, 0)), whole(w)],
        out_specs=[pl.BlockSpec((m, d), lambda i: (i, 0)), pl.BlockSpec((1, width), lambda i: (0, 0))],
        out_shape=outs,
        compiler_params=vmem(32),
        cost_estimate=cost(2 * rows * w.size, a, b, w, *outs),
        name="project_back",
    )(a, b, w)


def cells_back_kernel(s_ref, g_ref, got_ref, a_ref, b_ref, gm_ref, gain_ref, out_ref, sum_ref):
    k = pl.program_id(0)
    g = g_ref[0].astype(F32) + got_ref[0].astype(F32)
    n, rstd = block_norm(jnp.where(k == 0, a_ref[0].astype(F32), b_ref[0].astype(F32)))
    out_ref[0, 0] = (gm_ref[...] + block_norm_back(g, n, rstd, gain_ref[...])).astype(BF)
    add_sums(sum_ref, (k == 0) & (pl.program_id(1) == 0), g * n, g)


def cells_back(place, g, got, x0, x1, gmiddle, gain):
    cells, rows, d = x0.shape
    at = pl.BlockSpec((1, rows, d), lambda k, c, s: (c, s[0] ^ (2 * k), 0))
    piece = pl.BlockSpec((1, rows, d), lambda k, c, s: (c, 0, 0))
    outs = [jax.ShapeDtypeStruct((2, cells, rows, d), BF), jax.ShapeDtypeStruct((2, d), F32)]
    return pl.pallas_call(
        cells_back_kernel,
        grid_spec=pltpu.PrefetchScalarGridSpec(
            num_scalar_prefetch=1, grid=(2, cells),
            in_specs=[at, at, piece, piece, pl.BlockSpec((rows, d), lambda k, c, s: (k * cells + c, 0)), whole(gain)],
            out_specs=[pl.BlockSpec((1, 1, rows, d), lambda k, c, s: (k, c, 0, 0)), pl.BlockSpec((2, d), lambda k, c, s: (0, 0))]),
        out_shape=outs,
        compiler_params=vmem(32),
        cost_estimate=cost(0, x0, x0, x0, x0, x0, x0, gmiddle, *outs),
        name="cells_back",
    )(place, g, got, x0, x1, gmiddle, gain)


def store_block(orders, rel, value, sent_ref, kept_ref):
    core = lax.rem(lax.axis_index("seq"), 2)
    half = kept_ref.shape[0]
    places = [
        sum(jnp.where(rel & step != 0, half >> k, 0) for k, step in enumerate(steps)) for steps in orders
    ]
    pos = jnp.where(core == 0, places[0], places[1])

    @pl.when(pos >= half)
    def _():
        sent_ref[pos - half] = value

    @pl.when(pos < half)
    def _():
        kept_ref[pos] = value


def hidden_weights_kernel(orders, ff, nj, lhs_ref, own_ref, got_ref, sent_ref, kept_ref, rhs_ref, acc_ref):
    rows, d = own_ref.shape
    pad = rhs_ref.shape[1]
    step, steps = pl.program_id(0), pl.num_programs(0)
    seq, dp = lax.axis_index("seq"), lax.axis_index("dp")
    core, xi = lax.rem(seq, 2), lax.div(seq, 2)
    depth = ff // 2 // nj

    @pl.when(step == 0)
    def _():
        rhs_ref[:rows, :d] = own_ref[...]
        rhs_ref[rows:, :d] = got_ref[...]
        rhs_ref[:, d:] = jnp.zeros((2 * rows, pad - d), BF)

    wide = lhs_ref.shape[1]
    acc_ref[pl.ds(pl.multiple_of(step * wide, wide), wide)] = tn(lhs_ref[...], rhs_ref[...])
    for c in (0, 1):

        @pl.when((core == c) & (step == steps - 1))
        def _():
            for x in (0, 1):
                for j in range(nj):
                    at = hidden_window(c, ff)[2] + j * depth
                    rel = (x ^ xi) * nj + (j ^ lax.rem(dp, nj))
                    value = acc_ref[at : at + depth, x * (pad - 640) : x * (pad - 640) + 640]
                    store_block(orders, rel, value.astype(BF), sent_ref, kept_ref)


def hidden_weights(lhs, own, got, ff, nj, orders):
    rows, d = own.shape
    width = lhs.shape[1]
    pad = -(-d // 128) * 128
    depth = ff // 2 // nj
    outs = [jax.ShapeDtypeStruct((nj, depth, 640), BF)] * 2
    full = lambda: pl.BlockSpec((nj, depth, 640), lambda *_: (0, 0, 0), pipeline_mode=pl.Buffered(1))
    return pl.pallas_call(
        functools.partial(hidden_weights_kernel, orders, ff, nj),
        grid=(width // 256,),
        in_specs=[pl.BlockSpec((2 * rows, 256), lambda i: (0, i)), whole(own), whole(got)],
        out_specs=[full(), full()],
        out_shape=outs,
        scratch_shapes=[pltpu.VMEM((2 * rows, pad), BF), pltpu.VMEM((width, pad), F32)],
        compiler_params=vmem(48),
        cost_estimate=cost(4 * rows * width * pad, lhs, own, got, *outs),
        name="hidden_weights",
    )(lhs, own, got)


def output_weights_kernel(s_ref, own_ref, got_ref, g_ref, send_ref, keep_ref, acc_ref):
    k, c = pl.program_id(0), pl.program_id(1)
    start = (k == 0) & (c == 0)
    for h, ref in enumerate((own_ref, got_ref)):
        total = tn(ref[0], g_ref[...])
        acc_ref[h] = jnp.where(start, total, acc_ref[h] + total)
    core = lax.rem(lax.axis_index("seq"), 2)
    half = keep_ref.shape[1]
    for mine in (0, 1):

        @pl.when((k == 1) & (c == pl.num_programs(1) - 1) & (core == mine))
        def _():
            for h in (0, 1):
                keep_ref[h] = acc_ref[h, mine * half : (mine + 1) * half]
                send_ref[h] = acc_ref[h, (1 - mine) * half : (2 - mine) * half].astype(BF)


def output_weights(place, own, got, g, rows):
    cells, _, width = own.shape
    d = g.shape[1]
    at = pl.BlockSpec((1, rows, width), lambda k, c, s: (c, s[0] ^ (2 * k), 0))
    shape = (2, width // 2, d)
    outs = [jax.ShapeDtypeStruct(shape, BF), jax.ShapeDtypeStruct(shape, F32)]
    return pl.pallas_call(
        output_weights_kernel,
        grid_spec=pltpu.PrefetchScalarGridSpec(
            num_scalar_prefetch=1, grid=(2, cells),
            in_specs=[at, at, pl.BlockSpec((rows, d), lambda k, c, s: (k * cells + c, 0))],
            out_specs=[pl.BlockSpec(shape, lambda *_: (0, 0, 0), pipeline_mode=pl.Buffered(1))] * 2,
            scratch_shapes=[pltpu.VMEM((2, width, d), F32)]),
        out_shape=outs,
        compiler_params=vmem(32),
        cost_estimate=cost(8 * cells * rows * width * d, own, got, g, *outs),
        name="output_weights",
    )(place, own, got, g)


def place_in(steps, rel, count):
    return sum(jnp.where(rel & step != 0, count >> (k + 1), 0) for k, step in enumerate(steps))


def project_weights_kernel(orders, ndp, half, lhs_ref, rhs_refs, out_ref, blocks_ref, acc_ref, block_ref):
    step, steps = pl.program_id(0), pl.num_programs(0)
    seq, dp = lax.axis_index("seq"), lax.axis_index("dp")
    xi, core = lax.div(seq, 2), lax.rem(seq, 2)
    m = lhs_ref.shape[1]
    lo = 0
    rows = pl.ds(pl.multiple_of(step * m, m), m)
    for ref in rhs_refs:
        wide = ref.shape[1]
        acc_ref[rows, lo : lo + wide] = tn(lhs_ref[...], ref[...])
        lo += wide
    acc_ref[rows, lo:] = jnp.zeros((m, acc_ref.shape[1] - lo), F32)

    @pl.when(step == steps - 1)
    def _():
        wide = acc_ref.shape[1] // ndp
        third = block_ref.shape[0] // 3
        block_ref[half:] = jnp.zeros((3 * third - half, wide), F32)
        tall = out_ref.shape[1] // ndp
        for x in (0, 1):
            for j in range(ndp):
                block_ref[:half] = acc_ref[x * half : (x + 1) * half, j * wide : (j + 1) * wide]
                strip = out_ref[x ^ core, j * tall : (j + 1) * tall]
                for t, lo in enumerate(range(0, 2 * half, wide)):
                    hi = min(lo + wide, 2 * half)
                    block_ref[half + t * tall : half + (t + 1) * tall, : hi - lo] = strip[:, lo:hi]
                rel = (x ^ xi) * ndp + (j ^ dp)
                for i in range(3):
                    blocks_ref[i, place_in(orders[i], rel, 2 * ndp)] = block_ref[i * third : (i + 1) * third].astype(BF)


def project_weights(lhs, parts, width, out, ndp, orders):
    rows_in, d = lhs.shape
    m = 256
    steps = -(-d // m)
    wide = width // ndp
    third = -(-(d // 2 + -(-d // wide) * (out.shape[1] // ndp)) // 48) * 16
    block = (3, 2 * ndp, third, wide)
    n = len(parts)

    def kernel(lhs_ref, *refs):
        project_weights_kernel(orders, ndp, d // 2, lhs_ref, refs[:n], *refs[n:])

    return pl.pallas_call(
        kernel,
        grid=(steps,),
        in_specs=[pl.BlockSpec((rows_in, m), lambda i: (0, i))] + [whole(a) for a in (*parts, out)],
        out_specs=pl.BlockSpec(block, lambda *_: (0, 0, 0, 0), pipeline_mode=pl.Buffered(1)),
        out_shape=jax.ShapeDtypeStruct(block, BF),
        scratch_shapes=[pltpu.VMEM((steps * m, width), F32), pltpu.VMEM((3 * third, wide), F32)],
        compiler_params=vmem(48),
        cost_estimate=cost(2 * rows_in * d * width, lhs, out),
        name="project_weights",
    )(lhs, *parts, out)


def flip(index, bit):
    return index + bit - 2 * bit * lax.rem(lax.div(index, bit), 2)


def quarter_of(pair, x, c, quarter, shift):
    lo = x * shift + c * quarter
    return pair[:, :, lo : lo + quarter]


def sum_kernel(
    ndp, orders, quarter, shift, in_ref, pair_ref, sums_ref, gain_ref,
    ga_hbm, gb_hbm, w_hbm, x0_hbm, x1_hbm, gm_hbm, block_ref,
    held_ref, shared_ref, hidden_ref, block_out, cells_out,
    acc, got, piece, core_out, core_in, pair_got, part_out, part_in, sums, sums_got,
    ga, gb, w, xs, gm, gf, gf_got, rows_out, out_sem, in_sem, here_sem,
):
    seq, dp = lax.axis_index("seq"), lax.axis_index("dp")
    core, xi = lax.rem(seq, 2), lax.div(seq, 2)
    count, third = in_ref.shape[1], in_ref.shape[2]
    dims = [1 << b for b in range(ndp.bit_length() - 1)]

    def to(axis, bit):
        return {"dp": flip(dp, bit) if axis == "dp" else dp, "seq": flip(seq, bit) if axis == "seq" else seq}

    partners = [to("seq", 1), to("seq", 2)] + [to("dp", b) for b in dims]
    here = [
        pltpu.make_async_copy(src, dst, here_sem.at[n])
        for n, (src, dst) in enumerate((
            (ga_hbm, ga), (gb_hbm, gb), (w_hbm, w), (x0_hbm, xs.at[0]), (x1_hbm, xs.at[1]), (gm_hbm, gm)))
    ]
    for c in here:
        c.start()
    barrier = pltpu.get_barrier_semaphore()
    for p in partners:
        pl.semaphore_signal(barrier, inc=1, device_id=p, device_id_type=pl.DeviceIdType.MESH)
    pl.semaphore_wait(barrier, len(partners))
    used = []

    def copy(src, dst, target, always=True):
        n = len(used)
        c = pltpu.make_async_remote_copy(
            src_ref=src, dst_ref=dst, send_sem=out_sem.at[n], recv_sem=in_sem.at[n], device_id=target,
            device_id_type=pl.DeviceIdType.MESH)
        used.append((c, always))
        return c

    part = third // 2
    steps = len(orders[0])
    flying = {}

    def start(i, h, k):
        half = count >> (k + 1)
        rows = pl.ds(h * part, part)
        src = (in_ref if k == 0 else acc).at[i, pl.ds(half, half), rows]
        c = copy(src, got.at[i, pl.ds(count - 2 * half, half), rows], to(*orders[i][k]))
        c.start()
        flying[i, h] = c

    def finish(i, h, k):
        flying[i, h].wait_recv()
        half = count >> (k + 1)
        rows = slice(h * part, (h + 1) * part)
        for b in range(half):
            kept = in_ref[i, b, rows] if k == 0 else acc[i, b, rows]
            acc[i, b, rows] = (kept.astype(F32) + got[i, count - 2 * half + b, rows].astype(F32)).astype(BF)
        if k + 1 < steps:
            start(i, h, k + 1)

    for i in range(3):
        start(i, 0, 0)
    mine = core == lax.div(dp, ndp // 2)
    over_dp = copy(pair_ref, pair_got, to("dp", ndp // 2), False)
    over_core = copy(part_out, part_in, to("seq", 1), False)

    @pl.when(jnp.logical_not(mine))
    def _():
        over_dp.start()

    for c in here[:3]:
        c.wait()
    cells, block, d = x0_hbm.shape
    split = ga.shape[1]
    qkv_sums = [0.0, 0.0]
    for r in range(4 * cells):
        rows = slice(r * block, (r + 1) * block)
        a, b = ga[rows], gb[rows]
        gf[rows] = (nt(a, w[:, :split]) + nt(b, w[:, split:])).astype(BF)
        qkv_sums = [t + jnp.sum(v.astype(F32), axis=0, keepdims=True) for t, v in zip(qkv_sums, (a, b))]
    to_core = []
    for k in (1, 3):
        for c in range(cells):
            rows = pl.ds(pl.multiple_of((4 * c + (seq ^ k)) * block, block), block)
            to_core.append(copy(gf.at[rows], gf_got.at[rows], to("seq", 1)))
            to_core[-1].start()

    small = []
    small_order = [("seq", 2)] + [("dp", b) for b in dims] + [("seq", 1)]

    def small_step():
        n = len(small)
        if n:
            small[-1].wait_recv()
            if n < len(small_order):
                sums[n] = sums[n - 1] + sums_got[n - 1]
            else:
                shared_ref[0] = sums[n - 1]
                shared_ref[1] = sums_got[n - 1]
                return
        c = copy(sums.at[n], sums_got.at[n], to(*small_order[n]))
        c.start()
        small.append(c)

    for i in range(3):
        finish(i, 0, 0)
        start(i, 1, 0)
    for c in here[3:]:
        c.wait()
    for c in to_core:
        c.wait_recv()
    norm_sums = [0.0, 0.0]
    for k in (0, 1):
        for c in range(cells):
            rows = pl.ds(pl.multiple_of((4 * c + (seq ^ (2 * k))) * block, block), block)
            g = gf[rows].astype(F32) + gf_got[rows].astype(F32)
            n, rstd = block_norm(xs[k, c].astype(F32))
            mid = gm[(k * cells + c) * block : (k * cells + c + 1) * block]
            rows_out[k, c] = (mid + block_norm_back(g, n, rstd, gain_ref[...])).astype(BF)
            norm_sums = [t + jnp.sum(v, axis=0, keepdims=True) for t, v in zip(norm_sums, (g * n, g))]
    sums[0] = sums_ref[...]
    sums[0, 0:1, :d] = norm_sums[0]
    sums[0, 1:2, :d] = norm_sums[1]
    sums[0, 7:8, :split] = qkv_sums[0]
    sums[0, 7:8, split : w.shape[1]] = qkv_sums[1]
    small_step()
    for k in range(1, steps):
        for h in (0, 1):
            for i in range(3):
                finish(i, h, k - h)
        if k < 4:
            small_step()
    for i in range(3):
        finish(i, 1, steps - 1)

    for i in range(3):
        piece[i * third : (i + 1) * third] = acc[i, 0].astype(F32)
    for c in (0, 1):

        @pl.when(core == c)
        def _():
            core_out[...] = piece[(1 - c) * quarter : (2 - c) * quarter].astype(BF)

    swap_core = copy(core_out, core_in, to("seq", 1))
    swap_core.start()
    mine_cells = pl.ds(xi * cells, cells)
    back = [
        copy(block_ref.at[1], block_out.at[mine_cells], to("seq", 2)),
        copy(rows_out.at[1], cells_out.at[mine_cells], to("seq", 2)),
    ]
    keep = [
        pltpu.make_async_copy(src, dst.at[mine_cells], here_sem.at[len(here) + n])
        for n, (src, dst) in enumerate(((block_ref.at[0], block_out), (rows_out.at[0], cells_out)))
    ]
    for c in back + keep:
        c.start()
    swap_core.wait_recv()
    for c in (0, 1):

        @pl.when(core == c)
        def _():
            piece[(1 - c) * quarter : (2 - c) * quarter] = core_in[...].astype(F32)

    held_ref[0] = piece[...].astype(BF)

    ends = []
    far = dims[::-1]
    parts = 6
    rows_of = [pl.ds(i * (3 * third // parts), 3 * third // parts) for i in range(parts)]

    def share(i, k):
        n = 1 << k
        c = copy(held_ref.at[pl.ds(0, n), rows_of[i]], held_ref.at[pl.ds(n, n), rows_of[i]], to("dp", far[k]))
        c.start()
        return c

    first = share(0, 0)
    for i in range(parts):
        first.wait_recv()
        c = share(i, 1)
        if i + 1 < parts:
            first = share(i + 1, 0)
        for k in range(2, len(far)):
            c.wait_recv()
            c = share(i, k)
        ends.append(c)
        if i == 0:
            small_step()

    for x in (0, 1):
        for c in (0, 1):

            @pl.when(mine & (xi == x) & (core == c))
            def _():
                over_dp.wait_recv()
                total = pair_ref[...].astype(F32) + pair_got[...].astype(F32)
                hidden_ref[...] = quarter_of(total, x, c, quarter, shift)
                part_out[...] = quarter_of(total, x, 1 - c, quarter, shift).astype(BF)

    @pl.when(mine)
    def _():
        over_core.start()
        over_core.wait_send()

    @pl.when(jnp.logical_not(mine))
    def _():
        over_dp.wait_send()
        over_core.wait_recv()
        hidden_ref[...] = part_in[...].astype(F32)

    small_step()
    for c in keep:
        c.wait()
    for c in ends + back:
        c.wait_recv()
    for c, always in used:
        if always:
            c.wait_send()


def sum_and_gather(place, blocks, pair, sums, gain, ga, gb, w, x0, x1, gmiddle, block_rows, ndp, orders, quarter, shift):
    _, count, third, wide = blocks.shape
    _, depth, width = pair.shape
    cells, block, d = x0.shape
    in_vmem, hbm = pl.BlockSpec(memory_space=pltpu.VMEM), pl.BlockSpec(memory_space=pl.ANY)
    dims = ndp.bit_length() - 1
    copies = 6 * len(orders[0]) + 2 + (2 + dims) + 1 + 2 + 6 * dims + 2 * cells
    shape = jax.ShapeDtypeStruct
    both = (2 * cells, block, d)
    outs = [
        shape((ndp, 3 * third, wide), BF), shape((2, *sums.shape), F32), shape((2, depth, quarter), F32),
        shape(both, BF), shape(both, BF)]
    return pl.pallas_call(
        functools.partial(sum_kernel, ndp, orders, quarter, shift),
        in_specs=[in_vmem] * 4 + [hbm] * 7,
        out_specs=[in_vmem] * 3 + [hbm] * 2,
        out_shape=outs,
        scratch_shapes=[
            pltpu.VMEM((3, count // 2, third, wide), BF),
            pltpu.VMEM((3, count - 1, third, wide), BF),
            pltpu.VMEM((3 * third, wide), F32),
            pltpu.VMEM((quarter, wide), BF),
            pltpu.VMEM((quarter, wide), BF),
            pltpu.VMEM((2, depth, width), BF),
            pltpu.VMEM((2, depth, quarter), BF),
            pltpu.VMEM((2, depth, quarter), BF),
            pltpu.VMEM((2 + dims, *sums.shape), F32),
            pltpu.VMEM((2 + dims, *sums.shape), F32),
            pltpu.VMEM(ga.shape, BF),
            pltpu.VMEM(gb.shape, BF),
            pltpu.VMEM(w.shape, BF),
            pltpu.VMEM((2, *x0.shape), BF),
            pltpu.VMEM(gmiddle.shape, F32),
            pltpu.VMEM((4 * cells * block, d), BF),
            pltpu.VMEM((4 * cells * block, d), BF),
            pltpu.VMEM((2, *x0.shape), BF),
            pltpu.SemaphoreType.DMA((copies,)),
            pltpu.SemaphoreType.DMA((copies,)),
            pltpu.SemaphoreType.DMA((8,)),
        ],
        compiler_params=pltpu.CompilerParams(vmem_limit_bytes=60 << 20, collective_id=0, has_side_effects=True),
        cost_estimate=cost(0, blocks),
        name="sum_and_gather",
    )(blocks, pair, sums, gain, ga, gb, w, x0, x1, gmiddle, block_rows)


def sum_and_gather_by_steps(place, blocks, pair, sums, gain, ga, gb, w, x0, x1, gmiddle, block_rows, ndp, orders, quarter, shift):
    seq, dp = lax.axis_index("seq"), lax.axis_index("dp")
    core, xi = seq % 2, seq // 2
    cells, block, d = x0.shape
    gfirst, sums_qkv = project_back(ga, gb, w, block)
    gfirst_got = swap(gfirst.reshape(-1, block, d), "seq", 1).reshape(cells, 4 * block, d)
    cell_rows, sums1 = cells_back(place, gfirst.reshape(cells, 4 * block, d), gfirst_got, x0, x1, gmiddle, gain)
    sums = sums.at[:2, :d].set(sums1).at[7, : w.shape[1]].set(sums_qkv[0])
    count = blocks.shape[1]
    thirds = []
    for i in range(3):
        sent, kept = blocks[i, count // 2 :], blocks[i, : count // 2]
        for k, (axis, bit) in enumerate(orders[i]):
            got = swap(sent, axis, bit)
            if k + 1 < len(orders[i]):
                sent, kept = halve(kept, got)
        thirds.append(low(kept.astype(F32) + got.astype(F32))[0])
    piece = jnp.concatenate(thirds, 0)
    halves = piece[: 2 * quarter].reshape(2, quarter, -1)
    ours, theirs = pick(halves, core, 0), swap(pick(halves, 1 - core, 0), "seq", 1)
    held = jnp.concatenate(
        [jnp.where(core == 0, ours, theirs), jnp.where(core == 0, theirs, ours), piece[2 * quarter :]], 0)[None]
    bits = [1 << b for b in range(ndp.bit_length() - 1)]
    for bit in bits[::-1]:
        held = jnp.concatenate([held, swap(held, "dp", bit)], 0)
    for axis, bit in [("seq", 2)] + [("dp", b) for b in bits]:
        sums = sums + swap(sums, axis, bit)
    nj = ndp // 2
    across = [(d * 4 + t, (d ^ nj) * 4 + t) for d in range(ndp) for t in range(4) if d // nj != t % 2]
    total = pair.astype(F32) + lax.ppermute(pair, ("dp", "seq"), across).astype(F32)
    parts = [
        jnp.where(xi == 0, quarter_of(total, 0, c, quarter, shift), quarter_of(total, 1, c, quarter, shift)) for c in (0, 1)]
    theirs = swap(low(jnp.where(core == 0, parts[1], parts[0])), "seq", 1).astype(F32)
    hidden = jnp.where(core == dp // nj, jnp.where(core == 0, parts[0], parts[1]), theirs)

    def both_cells(rows):
        own, got = rows[0], swap(rows[1], "seq", 2)
        return jnp.concatenate([jnp.where(xi == 0, own, got), jnp.where(xi == 0, got, own)], 0)

    return held, jnp.stack([sums, swap(sums, "seq", 1)]), hidden, both_cells(block_rows), both_cells(cell_rows)


def assemble_kernel(bits, tiles, held_ref, e_ref, qkv_ref, out_ref, q_ref, o_ref):
    ndp, _, wide = held_ref.shape
    quarter, d = out_ref.shape
    heads, head = e_ref.shape
    tall = o_ref.shape[0] // ndp
    dp = lax.axis_index("dp")
    for j in range(ndp):
        rel = dp ^ j
        slot = sum(jnp.where(rel & b != 0, 1 << k, 0) for k, b in enumerate(bits))
        block = held_ref[slot].astype(F32)
        for c in (0, 1):
            q_ref[c, :, j * wide : (j + 1) * wide] = block[c * quarter : (c + 1) * quarter]
        for t, lo in enumerate(range(0, d, wide)):
            hi = min(lo + wide, d)
            at = 2 * quarter + t * tall
            o_ref[j * tall : (j + 1) * tall, lo:hi] = block[at : at + tall, : hi - lo]
    for part in range(3):
        for c in (0, 1):
            row = jnp.concatenate([q_ref[c, :, 128 * t : 128 * t + 128] for t in tiles[part]], 1)
            lo = part * d + c * head
            qkv_ref[:, lo : lo + head] = nn(row.astype(BF), e_ref[...])
    for h in range(o_ref.shape[0] // 64):
        out_ref[h * HD : (h + 1) * HD] = o_ref[h * 64 : h * 64 + HD]


def assemble(held, e, quarter, d, bits, tiles):
    ndp, _, wide = held.shape
    outs = [jax.ShapeDtypeStruct((quarter, 3 * d), F32), jax.ShapeDtypeStruct((quarter, d), F32)]
    return pl.pallas_call(
        functools.partial(assemble_kernel, bits, tiles),
        in_specs=[pl.BlockSpec(memory_space=pltpu.VMEM)] * 2,
        out_specs=[pl.BlockSpec(memory_space=pltpu.VMEM)] * 2,
        out_shape=outs,
        scratch_shapes=[pltpu.VMEM((2, quarter, ndp * wide), F32), pltpu.VMEM((quarter // HD * 64, d), F32)],
        compiler_params=vmem(40),
        cost_estimate=cost(6 * 2 * quarter * e.size, held, e, *outs),
        name="assemble",
    )(held, e)


def low(value):
    return lax.optimization_barrier(value.astype(BF))


def after(value, *first):
    return lax.optimization_barrier((value, *first))[0]


def swap(value, axis, bit):
    return lax.ppermute(value, axis, [(i, i ^ bit) for i in range(lax.axis_size(axis))])


def swap_by_core(value, steps):
    ndp, nseq = lax.axis_size("dp"), lax.axis_size("seq")
    pairs = []
    for d in range(ndp):
        for s in range(nseq):
            axis, bit = steps[s % 2]
            e, t = (d, s ^ bit) if axis == "seq" else (d ^ bit, s)
            pairs.append((d * nseq + s, e * nseq + t))
    return lax.ppermute(value, ("dp", "seq"), pairs)


def pick(array, index, axis):
    return lax.dynamic_index_in_dim(array, index, axis, keepdims=False)


def one_hot(rows, cols, source):
    r = lax.broadcasted_iota(jnp.int32, (rows, cols), 0)
    return (r == source[None, :]).astype(BF)


def halve(kept, got):
    half = kept.shape[0] // 2
    total = kept.astype(F32) + got.astype(F32)
    return low(total[half:]), low(total[:half])


def per_device(
    cells, prefix_len, ln1_gain, ln1_bias, w_qkv, bias_q, bias_v, w_out, bias_out,
    ln2_gain, ln2_bias, w_up, bias_up, w_down, bias_down, cotangent,
):
    seq, ndp = lax.axis_size("seq"), lax.axis_size("dp")
    s, dp = lax.axis_index("seq"), lax.axis_index("dp")
    core, xi = s % 2, s // 2
    assert seq == 4
    pairs, block, D = cells.shape
    C = pairs // 2
    T = block * seq
    HH = H // 2
    WH = HH * 64
    half = D // 2
    quarter = D // 4
    FF = w_up.shape[1]
    nj = ndp // 2
    R = 2 * C * block
    row = lambda v: v.reshape(1, -1)
    place = s.reshape(1).astype(jnp.int32)

    def split_cells(a):
        return lax.dynamic_slice_in_dim(a, xi * C, C, 0), lax.dynamic_slice_in_dim(a, (1 - xi) * C, C, 0)

    x0, x_other = split_cells(cells)
    x1 = swap(x_other, "seq", 2)
    x0_got = swap(x0, "seq", 1)
    prefix = lax.dynamic_slice_in_dim(prefix_len, xi * C, C, 0)

    col = jnp.arange(WH)
    head_col = jnp.where(col % 64 < HD, core * half + (col // 64) * HD + col % 64, -1)
    w_parts = []
    for j in range(3):
        lo = j * D // 128 * 128
        hi = min(-(-(j + 1) * D // 128) * 128, 3 * D)
        e = one_hot(hi - lo, WH, jnp.where(head_col >= 0, head_col + j * D - lo, -1))
        w_parts.append(jnp.dot(w_qkv[:, lo:hi], e, preferred_element_type=F32).astype(BF))
    cut = FIRST * 128
    in_order = lambda parts: [p[..., :cut] for p in parts] + [p[..., cut:] for p in parts]
    w_own = jnp.concatenate(in_order(w_parts), 1)

    def pad_heads(v, ones):
        v = lax.dynamic_slice_in_dim(v, core * half, half, 0).reshape(HH, HD)
        return jnp.concatenate([v, jnp.full((HH, 3), ones, F32), jnp.zeros((HH, 5), F32)], 1).reshape(WH)

    bias_own = jnp.concatenate(in_order([pad_heads(bias_q, 0.0), pad_heads(jnp.zeros_like(bias_q), 1.0), pad_heads(bias_v, 1.0)]))
    wo = w_out.reshape(2, HH, HD, D)
    wo = jnp.concatenate([wo, jnp.zeros((2, HH, 64 - HD, D), BF)], 2).reshape(2, WH, D)
    wo = jnp.where(core == 0, wo, wo[::-1]).reshape(2 * WH, D)

    x1 = after(x1, wo, w_own)
    x1_got = swap(x1, "seq", 1)
    first, qkv = project(place, (x0, x0_got, x1, x1_got), row(ln1_gain), row(ln1_bias), w_own, row(bias_own))
    c0, c_other = split_cells(cotangent)
    c1 = swap(after(c_other, x1), "seq", 2)
    qkv, c1 = lax.optimization_barrier((qkv, c1))
    c_pair = jnp.concatenate([c0, c1], 0)
    c_got = swap(c_pair, "seq", 1)
    att, q_aug = attention_forward(qkv, prefix)
    att_got = swap(att, "seq", 1)
    middle, second = attention_output(place, att, att_got, x0, x1, wo, row(bias_out), row(ln2_gain), row(ln2_bias))
    blocks = lambda v: v.reshape(-1, block, v.shape[-1])
    rows_of = lambda v: v.reshape(-1, v.shape[-1])
    second_got = rows_of(swap(blocks(second), "seq", 1))
    cot, cot_got = rows_of(c_pair), rows_of(c_got)

    act, gpre, out_own, out_send, gs_own, gs_send, bias_up_sum = hidden_layer(
        second, second_got, cot, cot_got, w_up, row(bias_up), w_down.T, block)
    gs_got = rows_of(swap(blocks(gs_send), "seq", 1))
    out_got = rows_of(swap(blocks(out_send), "seq", 1))

    low_bits = [1 << b for b in range(nj.bit_length() - 1)]
    rest = low_bits[2:]

    def order(*names):
        n = {"x": ("seq", 2), "y": ("dp", 1), "z": ("dp", 2)}
        return [n[k] for k in names] + [("dp", b) for b in rest]

    def codes(steps, n):
        return [n if axis == "seq" else bit for axis, bit in steps]

    down_orders = (order("x", "z", "y"), order("y", "x", "z"))
    up_orders = (order("z", "x", "y"), order("y", "z", "x"))
    top = [("dp", nj)]
    q_orders = [order("x", "y", "z") + top, order("y", "z", "x") + top, order("z", "x", "y") + top]

    def send(sent, orders, k):
        return swap_by_core(sent, (orders[0][k], orders[1][k]))

    d_sent, d_kept = hidden_weights(act, cot, cot_got, FF, nj, [codes(o, nj) for o in down_orders])
    d_got = send(d_sent, down_orders, 0)
    u_sent, u_kept = hidden_weights(gpre, second, second_got, FF, nj, [codes(o, nj) for o in up_orders])
    u_got = send(u_sent, up_orders, 0)

    gmiddle, gbranch, gatt, block_rows, sums2 = middle_back(
        after(gs_own, d_sent, u_sent), gs_got, out_own, out_got, middle, cot, wo, row(ln2_gain), row(bias_down), block)
    gatt_got = swap(gatt, "seq", 1)
    o_send, o_keep = output_weights(place, att, att_got, gbranch, block)
    o_got = swap(o_send, "seq", 1)
    g_out = o_keep + o_got[::-1].astype(F32)

    shape = (2, C, block, 2 * WH)
    gatt, gatt_got = gatt.reshape(shape), gatt_got.reshape(shape)
    d_sent, d_kept = halve(d_kept, d_got)
    d_got = send(d_sent, down_orders, 1)
    g_first = attention_backward(qkv, q_aug, after(gatt, d_sent, g_out), gatt_got, att, prefix, 0, FIRST).reshape(C * T, -1)
    d_sent, d_kept = halve(d_kept, after(d_got, g_first))
    d_got = send(d_sent, down_orders, 2)
    u_sent, u_kept = halve(u_kept, after(u_got, d_sent))
    u_got = send(u_sent, up_orders, 1)
    g_rest = attention_backward(
        qkv, q_aug, after(gatt, d_sent, u_sent), gatt_got, att, prefix, FIRST, WH // 128).reshape(C * T, -1)
    u_sent, u_kept = halve(u_kept, after(u_got, g_rest))
    u_got = send(u_sent, up_orders, 2)
    q_blocks = project_weights(
        first.reshape(C * T, D), [g_first, after(g_rest, u_sent)], -(-3 * WH // (128 * 16)) * 128 * 16, g_out, ndp,
        [codes(o, ndp) for o in q_orders])
    for k in range(3, len(down_orders[0])):
        d_sent, d_kept = halve(d_kept, d_got)
        d_got = send(d_sent, down_orders, k)
        u_sent, u_kept = halve(u_kept, u_got)
        u_got = send(u_sent, up_orders, k)
    d_got, u_got, q_blocks = lax.optimization_barrier((d_got, u_got, q_blocks))
    pair = low(jnp.concatenate([d_kept, u_kept], 0).astype(F32) + jnp.concatenate([d_got, u_got], 0).astype(F32))
    ff_width = bias_up_sum.shape[1]
    sums = jnp.concatenate(
        [jnp.zeros((2, ff_width), F32), jnp.pad(sums2, ((0, 0), (0, ff_width - D))), bias_up_sum, jnp.zeros((1, ff_width), F32)], 0)

    bits = [1 << b for b in range(ndp.bit_length() - 1)]
    shift = half - (-(-D // 128) * 128 - 640)
    block_rows = block_rows.reshape(2, C, block, D)
    finish = sum_and_gather if ndp <= 8 else sum_and_gather_by_steps
    held, sums, hidden, block_out, grad_cells = finish(
        place, q_blocks, pair, sums, row(ln1_gain), g_first, g_rest, w_own, x0, x1, gmiddle, block_rows, ndp, q_orders,
        quarter, shift)
    total = sums[0, :6, :D] + sums[1, :6, :D]
    by_core = jnp.where(core == 0, sums[:, 6:], sums[::-1, 6:])
    pad_up = FF - ff_width
    g_bias_up = jnp.pad(by_core[0, 0], (0, pad_up)) + jnp.pad(by_core[1, 0], (pad_up, 0))
    more = WH - cut

    def column_sums(j):
        v = jnp.concatenate(
            [by_core[:, 1, j * cut : (j + 1) * cut], by_core[:, 1, 3 * cut + j * more : 3 * cut + (j + 1) * more]], 1)
        return v.reshape(2 * HH, 64)[:, :HD].reshape(D)

    shared = [total[0], total[1], column_sums(0), column_sums(2), total[2], total[3], total[4], total[5], g_bias_up]

    head_of = jnp.arange(half)
    e_out = (jnp.arange(WH)[:, None] == (head_of // HD * 64 + head_of % HD)[None, :]).astype(BF)
    n_pairs = WH // 128
    tiles = [[tile_of(part, p, n_pairs) for p in range(n_pairs)] for part in range(3)]
    final_qkv, final_out = assemble(held, e_out, quarter, D, bits[::-1], tiles)

    final_down, final_up = hidden[0], hidden[1].T

    return (
        block_out, grad_cells, shared[0], shared[1], final_qkv, shared[2], shared[3], final_out,
        shared[4], shared[5], shared[6], final_up, shared[8], final_down, shared[7],
    )


def solution(mesh):
    rows = P("dp", "seq", None)
    return jax.shard_map(
        per_device,
        mesh=mesh,
        in_specs=(rows, P("dp")) + (P(),) * 13 + (rows,),
        out_specs=(rows, rows, P(), P(), P("seq", None), P(), P(), P("seq", None), P(), P(), P(), P("seq", "dp"), P(), P("dp", "seq"), P()),
        check_vma=False,
    )
```

```python
import functools
import math
import jax
import jax.numpy as jnp
from jax import lax
from jax.experimental import pallas as pl
from jax.experimental.pallas import tpu as pltpu
from jax.sharding import PartitionSpec as P

H = 20
HD=56
F32=jnp.float32; BF=jnp.bfloat16
LOG2=math.log2(math.e)
NEG=-1e30
def nt(a,b): return lax.dot_general(a,b,(((1,),(1,)),((),())),preferred_element_type=F32)
def nn(a,b): return lax.dot_general(a,b,(((1,),(0,)),((),())),preferred_element_type=F32)
def tn(a,b): return lax.dot_general(a,b,(((0,),(0,)),((),())),preferred_element_type=F32)

def split3(v):
    a=v.astype(BF); r=v-a.astype(F32); b=r.astype(BF); r=r-b.astype(F32)
    return a.astype(F32),b.astype(F32),r

def dup(k):
    low=lax.broadcasted_iota(jnp.int32,k.shape,1)<64
    r=pltpu.roll(k,64,1)
    return jnp.where(low,k,r).astype(BF), jnp.where(low,r,k).astype(BF)

def fwd_kernel(B, prefix_ref, q_ref,k_ref,v_ref,o_ref,qa_ref):
    T=q_ref.shape[1]
    p=prefix_ref[pl.program_id(0)]
    lane=lax.broadcasted_iota(jnp.int32,(T,128),1); low=lane<64
    q=q_ref[0].astype(F32)*(HD**-0.5*LOG2)
    hi=q.astype(BF).astype(F32); res=pltpu.roll(q-hi,64,1)
    qa=[jnp.where(low,hi,res),jnp.where(low,res,hi)]
    qab=[x.astype(BF) for x in qa]
    ka=dup(k_ref[0].astype(F32))
    lane_b=lane[:B]
    v32=v_ref[0].astype(F32)
    vm=[jnp.where(low,v32,0.0).astype(BF),jnp.where(low,0.0,v32).astype(BF)]
    row=lax.broadcasted_iota(jnp.int32,(B,B),0); col=lax.broadcasted_iota(jnp.int32,(B,B),1)
    tri=col<=row
    first=tri|((col<p)&(row<p))
    for i in range(T//B):
        n=(i+1)*B; rows=slice(i*B,n)
        outs=[]
        for h in range(2):
            s=nt(qab[h][rows],ka[h][:n])
            d=jnp.where(first if i==0 else tri,s[:,n-B:],NEG)
            if i: s=jnp.concatenate([s[:,:n-B],d],1)
            else: s=d
            m=jnp.max(s,axis=1,keepdims=True)
            outs.append((jnp.exp2(s-m).astype(BF),m))
        o=nn(jnp.concatenate([outs[0][0],outs[1][0]],1),jnp.concatenate([vm[0][:n],vm[1][:n]],0))
        ls=[o[:,56:57],o[:,120:121]]
        for h in range(2):
            lse=-(outs[h][1]+jnp.log2(ls[h]))
            a,b,c=split3(lse)
            z=64*h+56
            x=jnp.where(lane_b==z,a,jnp.where(lane_b==z+1,b,jnp.where(lane_b==z+2,c,qa[h][rows])))
            qa_ref[0,rows,128*h:128*h+128]=x.astype(BF)
        o_ref[0,rows]=(o*jnp.where(low[:B],1.0/ls[0],1.0/ls[1])).astype(BF)


FIRST=3


def tile_of(part,p,pairs):
    if isinstance(p,int):
        return part*FIRST+p if p<FIRST else 3*FIRST+part*(pairs-FIRST)+p-FIRST
    return jnp.where(p<FIRST,part*FIRST+p,3*FIRST+part*(pairs-FIRST)+p-FIRST)


def attention_forward(qkv,prefix,B=256):
    C,T,W=qkv.shape; NP=W//384
    spec=lambda part: pl.BlockSpec((1,T,128),lambda c,p,pr: (c,0,tile_of(part,p,NP)))
    return pl.pallas_call(functools.partial(fwd_kernel,B),
        grid_spec=pltpu.PrefetchScalarGridSpec(num_scalar_prefetch=1,grid=(C,NP),
            in_specs=[spec(0),spec(1),spec(2)],
            out_specs=[pl.BlockSpec((1,T,128),lambda c,p,pr:(c,0,p)),pl.BlockSpec((1,T,256),lambda c,p,pr:(c,0,p))]),
        out_shape=[jax.ShapeDtypeStruct((C,T,128*NP),BF),jax.ShapeDtypeStruct((C,T,256*NP),BF)],
        compiler_params=pltpu.CompilerParams(vmem_limit_bytes=40<<20),
        cost_estimate=pl.CostEstimate(flops=1,bytes_accessed=1,transcendentals=0),
        name="attention_forward",
    )(prefix,qkv,qkv,qkv)

def bwd_kernel(B, prefix_ref, qa_ref,q_ref,k_ref,v_ref,go_ref,gg_ref,o_ref,out_ref,dk_ref,dv_ref,do_ref):
    T=q_ref.shape[1]; NP=pl.num_programs(1); W=out_ref.shape[2]
    block=T//4
    s=lax.axis_index("seq")
    for k,piece in enumerate((go_ref[0,0],go_ref[1,0],gg_ref[0,0],gg_ref[1,0])):
        place=s^(2*(k%2)+k//2)
        do_ref[pl.ds(pl.multiple_of(place*block,block),block)]=piece
    pr=pl.program_id(1)
    p=prefix_ref[pl.program_id(0)]
    lane=lax.broadcasted_iota(jnp.int32,(T,128),1); low=lane<64
    k32=k_ref[0].astype(F32); q32=q_ref[0].astype(F32); do32=do_ref[...].astype(F32)
    ka=dup(k32)
    zero=jnp.zeros_like(k32)
    km=[jnp.where(low,k32,zero).astype(BF),jnp.where(low,zero,k32).astype(BF)]
    qm=[jnp.where(low,q32,zero).astype(BF),jnp.where(low,zero,q32).astype(BF)]
    dom=[jnp.where(low,do32,zero),jnp.where(low,zero,do32)]
    o32=o_ref[0].astype(F32)
    doa=[]
    for h in range(2):
        dl=-jnp.sum(dom[h]*o32,axis=1,keepdims=True)
        a,b,c=split3(dl); z=64*h+56
        doa.append(jnp.where(lane==z,a,jnp.where(lane==z+1,b,jnp.where(lane==z+2,c,dom[h]))).astype(BF))
    dom=[x.astype(BF) for x in dom]
    key=lax.broadcasted_iota(jnp.int32,(B,B),0); qry=lax.broadcasted_iota(jnp.int32,(B,B),1)
    tri=key<=qry
    first=tri|((key<p)&(qry<p))
    sc=HD**-0.5
    for i in reversed(range(T//B)):
        n=(i+1)*B; rows=slice(i*B,n)
        pbs=[];dss=[]
        for h in range(2):
            s=nt(ka[h][:n],qa_ref[0,rows,128*h:128*h+128])
            d=jnp.where(first if i==0 else tri,s[n-B:],NEG)
            s=jnp.concatenate([s[:n-B],d],0) if i else d
            e=jnp.exp2(s)
            dp=nt(v_ref[0,:n],doa[h][rows])
            dss.append((e*dp).astype(BF)); pbs.append(e.astype(BF))
        dq=tn(jnp.concatenate(dss,0),jnp.concatenate([km[0][:n],km[1][:n]],0))
        out_ref[0,rows,pl.ds(pl.multiple_of(pr*128,128),128)]=(dq*sc).astype(BF)
        dv=nn(pbs[0],dom[0][rows])+nn(pbs[1],dom[1][rows])
        dk=nn(dss[0],qm[0][rows])+nn(dss[1],qm[1][rows])
        if i==T//B-1:
            dv_ref[...]=dv; dk_ref[...]=dk
        else:
            dv_ref[:n]+=dv; dk_ref[:n]+=dk
    out_ref[0,:,pl.ds(pl.multiple_of((NP+pr)*128,128),128)]=(dk_ref[...]*sc).astype(BF)
    out_ref[0,:,pl.ds(pl.multiple_of((2*NP+pr)*128,128),128)]=dv_ref[...].astype(BF)

def attention_backward(qkv,qa,do,do_got,o,prefix,p0,p1,B=256):
    C,T,W=qkv.shape; NP=W//384
    width=384*(p1-p0)
    spec=lambda part: pl.BlockSpec((1,T,128),lambda c,p,pr: (c,0,tile_of(part,p0,NP)+p))
    return pl.pallas_call(functools.partial(bwd_kernel,B),
        grid_spec=pltpu.PrefetchScalarGridSpec(num_scalar_prefetch=1,grid=(C,p1-p0),
            in_specs=[pl.BlockSpec((1,T,256),lambda c,p,pr:(c,0,p0+p)),spec(0),spec(1),spec(2),
                pl.BlockSpec((2,1,T//4,128),lambda c,p,pr:(0,c,0,p0+p)),pl.BlockSpec((2,1,T//4,128),lambda c,p,pr:(0,c,0,NP+p0+p)),
                pl.BlockSpec((1,T,128),lambda c,p,pr:(c,0,p0+p))],
            out_specs=pl.BlockSpec((1,T,width),lambda c,p,pr:(c,0,0)),
            scratch_shapes=[pltpu.VMEM((T,128),F32)]*2+[pltpu.VMEM((T,128),BF)]),
        out_shape=jax.ShapeDtypeStruct((C,T,width),BF),
        compiler_params=pltpu.CompilerParams(vmem_limit_bytes=40<<20),
        cost_estimate=pl.CostEstimate(flops=1,bytes_accessed=1,transcendentals=0),
        name="attention_backward",
    )(prefix,qa,qkv,qkv,qkv,do,do_got,o)


epsilon = 1e-05


def vmem(megabytes):
    return pltpu.CompilerParams(vmem_limit_bytes=megabytes << 20)


def whole(array):
    return pl.BlockSpec(array.shape, lambda *_: (0,) * array.ndim, pipeline_mode=pl.Buffered(1))


def cost(flops, *arrays):
    return pl.CostEstimate(flops=1, bytes_accessed=1, transcendentals=0)


def block_norm(rows):
    width = rows.shape[1]
    mean = jnp.sum(rows, axis=1, keepdims=True) * (1.0 / width)
    centred = rows - mean
    rstd = lax.rsqrt(jnp.sum(centred * centred, axis=1, keepdims=True) * (1.0 / width) + epsilon)
    return centred * rstd, rstd


def block_norm_back(grad, normed, rstd, gain):
    inv = 1.0 / grad.shape[1]
    dn = grad * gain
    a = jnp.sum(dn, axis=1, keepdims=True) * inv
    b = jnp.sum(dn * normed, axis=1, keepdims=True) * inv
    return rstd * (dn - a - normed * b)


def add_sums(ref, start, *rows):
    for k, v in enumerate(rows):
        total = jnp.sum(v, axis=0, keepdims=True)
        ref[k : k + 1] = jnp.where(start, total, ref[k : k + 1] + total)


def project_kernel(s_ref, a_ref, b_ref, c_ref, d_ref, g_ref, h_ref, w_ref, bias_ref, first_ref, out_ref):
    k = pl.program_id(1)
    x = jnp.where(k < 2, jnp.where(k == 0, a_ref[0].astype(F32), b_ref[0].astype(F32)),
                  jnp.where(k == 2, c_ref[0].astype(F32), d_ref[0].astype(F32)))
    n, _ = block_norm(x)
    first = (n * g_ref[...] + h_ref[...]).astype(BF)
    first_ref[0] = first
    width = w_ref.shape[1]
    for lo in range(0, width, 640):
        cols = slice(lo, min(lo + 640, width))
        out_ref[0, :, cols] = (nn(first, w_ref[:, cols]) + bias_ref[:, cols]).astype(BF)


def project(place, pieces, gain, shift, w, bias):
    cells, rows, d = pieces[0].shape
    width = w.shape[1]
    piece = pl.BlockSpec((1, rows, d), lambda c, k, s: (c, 0, 0))
    at = lambda c, k, s: (c, s[0] ^ k, 0)
    ins = (gain, shift, w, bias)
    outs = [jax.ShapeDtypeStruct((cells, 4 * rows, n), BF) for n in (d, width)]
    return pl.pallas_call(
        project_kernel,
        grid_spec=pltpu.PrefetchScalarGridSpec(
            num_scalar_prefetch=1, grid=(cells, 4), in_specs=[piece] * 4 + [whole(a) for a in ins],
            out_specs=[pl.BlockSpec((1, rows, n), at) for n in (d, width)]),
        out_shape=outs,
        compiler_params=vmem(40),
        cost_estimate=cost(8 * cells * rows * w.size, *pieces, *ins, *outs),
        name="norm_project",
    )(place, *pieces, *ins)


def middle_kernel(s_ref, own_ref, got_ref, a_ref, b_ref, w_ref, c_ref, g_ref, h_ref, middle_ref, second_ref):
    half = own_ref.shape[2]
    out = nn(own_ref[0], w_ref[:half]) + nn(got_ref[0], w_ref[half:])
    x = jnp.where(pl.program_id(0) == 0, a_ref[0].astype(F32), b_ref[0].astype(F32))
    middle = x + out + c_ref[...]
    middle_ref[...] = middle
    n, _ = block_norm(middle)
    second_ref[...] = (n * g_ref[...] + h_ref[...]).astype(BF)


def attention_output(place, own, got, x0, x1, w, bias, gain, shift):
    cells, rows, d = x0.shape
    half = own.shape[2]
    at = pl.BlockSpec((1, rows, half), lambda k, c, s: (c, s[0] ^ (2 * k), 0))
    piece = pl.BlockSpec((1, rows, d), lambda k, c, s: (c, 0, 0))
    ins = (w, bias, gain, shift)
    outs = [jax.ShapeDtypeStruct((2 * cells * rows, d), t) for t in (F32, BF)]
    return pl.pallas_call(
        middle_kernel,
        grid_spec=pltpu.PrefetchScalarGridSpec(
            num_scalar_prefetch=1, grid=(2, cells), in_specs=[at, at, piece, piece] + [whole(a) for a in ins],
            out_specs=[pl.BlockSpec((rows, d), lambda k, c, s: (k * cells + c, 0))] * 2),
        out_shape=outs,
        compiler_params=vmem(32),
        cost_estimate=cost(4 * cells * rows * w.size, x0, x0, *ins, *outs),
        name="attention_output",
    )(place, own, got, x0, x1, *ins)


CHUNK = 768


def hidden_window(core, ff):
    width = -(-(ff // 2) // CHUNK) * CHUNK
    return core * (ff - width), width, core * (width - ff // 2)


def hidden_kernel(
    ff, s0_ref, s1_ref, c0_ref, c1_ref, bu_ref, wu_hbm, wd_hbm,
    act_ref, gpre_ref, out0_ref, out1_ref, gs0_ref, gs1_ref, sum_ref, wu_ref, wd_ref, sem,
):
    i, n = pl.program_id(0), pl.num_programs(0) // 2
    core = lax.rem(lax.axis_index("seq"), 2)
    start, width, skip = hidden_window(core, ff)
    chunks = width // CHUNK

    def copies(k):
        at = pl.multiple_of(start + k * CHUNK, 128)
        cols = pl.ds(k * CHUNK, CHUNK)
        return (
            pltpu.make_async_copy(wu_hbm.at[:, pl.ds(at, CHUNK)], wu_ref.at[:, cols], sem.at[2 * k]),
            pltpu.make_async_copy(wd_hbm.at[:, pl.ds(at, CHUNK)], wd_ref.at[:, cols], sem.at[2 * k + 1]),
        )

    @pl.when(i == 0)
    def _():
        for k in range(chunks):
            for c in copies(k):
                c.start()

    second = jnp.where(i < n, s0_ref[...].astype(F32), s1_ref[...].astype(F32)).astype(BF)
    cot = jnp.where(i < n, c0_ref[...].astype(F32), c1_ref[...].astype(F32)).astype(BF)
    out = gsec = None
    a, b = 0.7978845608, 0.044715
    for k in range(chunks):
        cols = slice(k * CHUNK, (k + 1) * CHUNK)

        @pl.when(i == 0)
        def _():
            for c in copies(k):
                c.wait()

        u = nn(second, wu_ref[:, cols]) + bu_ref[:, pl.ds(pl.multiple_of(start + k * CHUNK, 128), CHUNK)]
        gact = nn(cot, wd_ref[:, cols])
        u2 = u * u
        t = jnp.tanh(u * (a + a * b * u2))
        h = 0.5 + 0.5 * t
        act = u * h
        gpre = gact * (h + u * (0.5 - 0.5 * t * t) * (a + 3 * a * b * u2))
        if k in (0, chunks - 1):
            col = lax.broadcasted_iota(jnp.int32, (1, CHUNK), 1) + k * CHUNK
            mine = (col >= skip) & (col < skip + ff // 2)
            act, gpre = jnp.where(mine, act, 0.0), jnp.where(mine, gpre, 0.0)
        act, gpre = act.astype(BF), gpre.astype(BF)
        act_ref[:, cols] = act
        gpre_ref[:, cols] = gpre
        total = jnp.sum(gpre.astype(F32), axis=0, keepdims=True)
        sum_ref[:, cols] = jnp.where(i == 0, total, sum_ref[:, cols] + total)
        o, g = nt(act, wd_ref[:, cols]), nt(gpre, wu_ref[:, cols])
        out, gsec = (o, g) if out is None else (out + o, gsec + g)

    @pl.when(i < n)
    def _():
        out0_ref[...] = out.astype(BF)
        gs0_ref[...] = gsec.astype(BF)

    @pl.when(i >= n)
    def _():
        out1_ref[...] = out.astype(BF)
        gs1_ref[...] = gsec.astype(BF)


def hidden_layer(second, second_got, cot, cot_got, w_up, bias_up, w_down_t, m):
    rows, d = second.shape
    ff = w_up.shape[1]
    n = rows // m
    width = hidden_window(0, ff)[1]
    lo = pl.BlockSpec((m, d), lambda i: (jnp.minimum(i, n - 1), 0))
    hi = pl.BlockSpec((m, d), lambda i: (jnp.maximum(i - n, 0), 0))
    row = pl.BlockSpec((m, width), lambda i: (i, 0))
    hbm = pl.BlockSpec(memory_space=pl.ANY)
    shape = jax.ShapeDtypeStruct
    outs = [shape((2 * rows, width), BF)] * 2 + [shape((rows, d), BF)] * 4 + [shape((1, width), F32)]
    return pl.pallas_call(
        functools.partial(hidden_kernel, ff),
        grid=(2 * n,),
        in_specs=[lo, hi, lo, hi, whole(bias_up), hbm, hbm],
        out_specs=[row, row, lo, hi, lo, hi, pl.BlockSpec((1, width), lambda i: (0, 0))],
        out_shape=outs,
        scratch_shapes=[pltpu.VMEM((d, width), BF), pltpu.VMEM((d, width), BF), pltpu.SemaphoreType.DMA((2 * (width // CHUNK),))],
        compiler_params=vmem(56),
        cost_estimate=cost(16 * rows * d * width, second, second, cot, cot, w_up, *outs),
        name="hidden_layer",
    )(second, second_got, cot, cot_got, bias_up, w_up, w_down_t)


def middle_back_kernel(
    gs_ref, gs_got_ref, o_ref, o_got_ref, middle_ref, cot_ref, w_ref, g_ref, c_ref,
    gm_ref, gb_ref, gatt_ref, block_ref, sum_ref,
):
    middle, gy = middle_ref[...], cot_ref[...].astype(F32)
    gsecond = gs_ref[...].astype(F32) + gs_got_ref[...].astype(F32)
    n, rstd = block_norm(middle)
    gmiddle = gy + block_norm_back(gsecond, n, rstd, g_ref[...])
    gm_ref[...] = gmiddle
    gbranch = gmiddle.astype(BF)
    gb_ref[...] = gbranch
    gatt_ref[...] = nt(gbranch, w_ref[...]).astype(BF)
    block_ref[...] = (middle + (o_ref[...].astype(F32) + o_got_ref[...].astype(F32)) + c_ref[...]).astype(BF)
    add_sums(sum_ref, pl.program_id(0) == 0, gbranch.astype(F32), gsecond * n, gsecond, gy)


def middle_back(gsec, gsec_got, out, out_got, middle, cot, w, gain, bias, m):
    rows, d = middle.shape
    row = lambda n: pl.BlockSpec((m, n), lambda i: (i, 0))
    ins = (gsec, gsec_got, out, out_got, middle, cot, w, gain, bias)
    shape = jax.ShapeDtypeStruct
    heads = w.shape[0]
    outs = [shape((rows, d), F32), shape((rows, d), BF), shape((rows, heads), BF), shape((rows, d), BF), shape((4, d), F32)]
    return pl.pallas_call(
        middle_back_kernel,
        grid=(rows // m,),
        in_specs=[row(d)] * 6 + [whole(a) for a in ins[6:]],
        out_specs=[row(d), row(d), row(heads), row(d), pl.BlockSpec((4, d), lambda i: (0, 0))],
        out_shape=outs,
        compiler_params=vmem(40),
        cost_estimate=cost(2 * rows * w.size, *ins, *outs),
        name="middle_back",
    )(*ins)


def project_back_kernel(a_ref, b_ref, w_ref, out_ref, sum_ref):
    split = a_ref.shape[1]
    out_ref[...] = (nt(a_ref[...], w_ref[:, :split]) + nt(b_ref[...], w_ref[:, split:])).astype(BF)
    start = pl.program_id(0) == 0
    for ref, cols in ((a_ref, slice(0, split)), (b_ref, slice(split, None))):
        total = jnp.sum(ref[...].astype(F32), axis=0, keepdims=True)
        sum_ref[:, cols] = jnp.where(start, total, sum_ref[:, cols] + total)


def project_back(a, b, w, m):
    rows = a.shape[0]
    d, width = w.shape
    outs = [jax.ShapeDtypeStruct((rows, d), BF), jax.ShapeDtypeStruct((1, width), F32)]
    return pl.pallas_call(
        project_back_kernel,
        grid=(rows // m,),
        in_specs=[pl.BlockSpec((m, a.shape[1]), lambda i: (i, 0)), pl.BlockSpec((m, b.shape[1]), lambda i: (i, 0)), whole(w)],
        out_specs=[pl.BlockSpec((m, d), lambda i: (i, 0)), pl.BlockSpec((1, width), lambda i: (0, 0))],
        out_shape=outs,
        compiler_params=vmem(32),
        cost_estimate=cost(2 * rows * w.size, a, b, w, *outs),
        name="project_back",
    )(a, b, w)


def cells_back_kernel(s_ref, g_ref, got_ref, a_ref, b_ref, gm_ref, gain_ref, out_ref, sum_ref):
    k = pl.program_id(0)
    g = g_ref[0].astype(F32) + got_ref[0].astype(F32)
    n, rstd = block_norm(jnp.where(k == 0, a_ref[0].astype(F32), b_ref[0].astype(F32)))
    out_ref[0, 0] = (gm_ref[...] + block_norm_back(g, n, rstd, gain_ref[...])).astype(BF)
    add_sums(sum_ref, (k == 0) & (pl.program_id(1) == 0), g * n, g)


def cells_back(place, g, got, x0, x1, gmiddle, gain):
    cells, rows, d = x0.shape
    at = pl.BlockSpec((1, rows, d), lambda k, c, s: (c, s[0] ^ (2 * k), 0))
    piece = pl.BlockSpec((1, rows, d), lambda k, c, s: (c, 0, 0))
    outs = [jax.ShapeDtypeStruct((2, cells, rows, d), BF), jax.ShapeDtypeStruct((2, d), F32)]
    return pl.pallas_call(
        cells_back_kernel,
        grid_spec=pltpu.PrefetchScalarGridSpec(
            num_scalar_prefetch=1, grid=(2, cells),
            in_specs=[at, at, piece, piece, pl.BlockSpec((rows, d), lambda k, c, s: (k * cells + c, 0)), whole(gain)],
            out_specs=[pl.BlockSpec((1, 1, rows, d), lambda k, c, s: (k, c, 0, 0)), pl.BlockSpec((2, d), lambda k, c, s: (0, 0))]),
        out_shape=outs,
        compiler_params=vmem(32),
        cost_estimate=cost(0, x0, x0, x0, x0, x0, x0, gmiddle, *outs),
        name="cells_back",
    )(place, g, got, x0, x1, gmiddle, gain)


def store_block(orders, rel, value, sent_ref, kept_ref):
    core = lax.rem(lax.axis_index("seq"), 2)
    half = kept_ref.shape[0]
    places = [
        sum(jnp.where(rel & step != 0, half >> k, 0) for k, step in enumerate(steps)) for steps in orders
    ]
    pos = jnp.where(core == 0, places[0], places[1])

    @pl.when(pos >= half)
    def _():
        sent_ref[pos - half] = value

    @pl.when(pos < half)
    def _():
        kept_ref[pos] = value


def hidden_weights_kernel(orders, ff, nj, lhs_ref, own_ref, got_ref, sent_ref, kept_ref, rhs_ref, acc_ref):
    rows, d = own_ref.shape
    pad = rhs_ref.shape[1]
    step, steps = pl.program_id(0), pl.num_programs(0)
    seq, dp = lax.axis_index("seq"), lax.axis_index("dp")
    core, xi = lax.rem(seq, 2), lax.div(seq, 2)
    depth = ff // 2 // nj

    @pl.when(step == 0)
    def _():
        rhs_ref[:rows, :d] = own_ref[...]
        rhs_ref[rows:, :d] = got_ref[...]
        rhs_ref[:, d:] = jnp.zeros((2 * rows, pad - d), BF)

    wide = lhs_ref.shape[1]
    acc_ref[pl.ds(pl.multiple_of(step * wide, wide), wide)] = tn(lhs_ref[...], rhs_ref[...])
    for c in (0, 1):

        @pl.when((core == c) & (step == steps - 1))
        def _():
            for x in (0, 1):
                for j in range(nj):
                    at = hidden_window(c, ff)[2] + j * depth
                    rel = (x ^ xi) * nj + (j ^ lax.rem(dp, nj))
                    value = acc_ref[at : at + depth, x * (pad - 640) : x * (pad - 640) + 640]
                    store_block(orders, rel, value.astype(BF), sent_ref, kept_ref)


def hidden_weights(lhs, own, got, ff, nj, orders):
    rows, d = own.shape
    width = lhs.shape[1]
    pad = -(-d // 128) * 128
    depth = ff // 2 // nj
    outs = [jax.ShapeDtypeStruct((nj, depth, 640), BF)] * 2
    full = lambda: pl.BlockSpec((nj, depth, 640), lambda *_: (0, 0, 0), pipeline_mode=pl.Buffered(1))
    return pl.pallas_call(
        functools.partial(hidden_weights_kernel, orders, ff, nj),
        grid=(width // 256,),
        in_specs=[pl.BlockSpec((2 * rows, 256), lambda i: (0, i)), whole(own), whole(got)],
        out_specs=[full(), full()],
        out_shape=outs,
        scratch_shapes=[pltpu.VMEM((2 * rows, pad), BF), pltpu.VMEM((width, pad), F32)],
        compiler_params=vmem(48),
        cost_estimate=cost(4 * rows * width * pad, lhs, own, got, *outs),
        name="hidden_weights",
    )(lhs, own, got)


def output_weights_kernel(s_ref, own_ref, got_ref, g_ref, send_ref, keep_ref, acc_ref):
    k, c = pl.program_id(0), pl.program_id(1)
    start = (k == 0) & (c == 0)
    for h, ref in enumerate((own_ref, got_ref)):
        total = tn(ref[0], g_ref[...])
        acc_ref[h] = jnp.where(start, total, acc_ref[h] + total)
    core = lax.rem(lax.axis_index("seq"), 2)
    half = keep_ref.shape[1]
    for mine in (0, 1):

        @pl.when((k == 1) & (c == pl.num_programs(1) - 1) & (core == mine))
        def _():
            for h in (0, 1):
                keep_ref[h] = acc_ref[h, mine * half : (mine + 1) * half]
                send_ref[h] = acc_ref[h, (1 - mine) * half : (2 - mine) * half].astype(BF)


def output_weights(place, own, got, g, rows):
    cells, _, width = own.shape
    d = g.shape[1]
    at = pl.BlockSpec((1, rows, width), lambda k, c, s: (c, s[0] ^ (2 * k), 0))
    shape = (2, width // 2, d)
    outs = [jax.ShapeDtypeStruct(shape, BF), jax.ShapeDtypeStruct(shape, F32)]
    return pl.pallas_call(
        output_weights_kernel,
        grid_spec=pltpu.PrefetchScalarGridSpec(
            num_scalar_prefetch=1, grid=(2, cells),
            in_specs=[at, at, pl.BlockSpec((rows, d), lambda k, c, s: (k * cells + c, 0))],
            out_specs=[pl.BlockSpec(shape, lambda *_: (0, 0, 0), pipeline_mode=pl.Buffered(1))] * 2,
            scratch_shapes=[pltpu.VMEM((2, width, d), F32)]),
        out_shape=outs,
        compiler_params=vmem(32),
        cost_estimate=cost(8 * cells * rows * width * d, own, got, g, *outs),
        name="output_weights",
    )(place, own, got, g)


def place_in(steps, rel, count):
    return sum(jnp.where(rel & step != 0, count >> (k + 1), 0) for k, step in enumerate(steps))


def project_weights_kernel(orders, ndp, half, lhs_ref, rhs_refs, out_ref, blocks_ref, acc_ref, block_ref):
    step, steps = pl.program_id(0), pl.num_programs(0)
    seq, dp = lax.axis_index("seq"), lax.axis_index("dp")
    xi, core = lax.div(seq, 2), lax.rem(seq, 2)
    m = lhs_ref.shape[1]
    lo = 0
    rows = pl.ds(pl.multiple_of(step * m, m), m)
    for ref in rhs_refs:
        wide = ref.shape[1]
        acc_ref[rows, lo : lo + wide] = tn(lhs_ref[...], ref[...])
        lo += wide
    acc_ref[rows, lo:] = jnp.zeros((m, acc_ref.shape[1] - lo), F32)

    @pl.when(step == steps - 1)
    def _():
        wide = acc_ref.shape[1] // ndp
        part = blocks_ref.shape[2] // 2
        full = half // part
        rest = half - full * part
        block_ref[rest:] = jnp.zeros((block_ref.shape[0] - rest, wide), F32)
        tall = out_ref.shape[1] // ndp
        for x in (0, 1):
            for j in range(ndp):
                cols = slice(j * wide, (j + 1) * wide)
                block_ref[:rest] = acc_ref[x * half + full * part : (x + 1) * half, cols]
                strip = out_ref[x ^ core, j * tall : (j + 1) * tall]
                for t, lo in enumerate(range(0, 2 * half, wide)):
                    hi = min(lo + wide, 2 * half)
                    block_ref[rest + t * tall : rest + (t + 1) * tall, : hi - lo] = strip[:, lo:hi]
                rel = (x ^ xi) * ndp + (j ^ dp)
                for n, steps_of in enumerate(orders):
                    if n < full:
                        value = acc_ref[x * half + n * part : x * half + (n + 1) * part, cols]
                    else:
                        value = block_ref[(n - full) * part : (n - full + 1) * part]
                    place = place_in(steps_of, rel, 2 * ndp)
                    blocks_ref[n // 2, place, n % 2 * part : (n % 2 + 1) * part] = value.astype(BF)


def project_weights(lhs, parts, width, out, ndp, orders):
    rows_in, d = lhs.shape
    m = 256
    steps = -(-d // m)
    wide = width // ndp
    third = -(-(d // 2 + -(-d // wide) * (out.shape[1] // ndp)) // 48) * 16
    block = (3, 2 * ndp, third, wide)
    n = len(parts)

    def kernel(lhs_ref, *refs):
        project_weights_kernel(orders, ndp, d // 2, lhs_ref, refs[:n], *refs[n:])

    return pl.pallas_call(
        kernel,
        grid=(steps,),
        in_specs=[pl.BlockSpec((rows_in, m), lambda i: (0, i))] + [whole(a) for a in (*parts, out)],
        out_specs=pl.BlockSpec(block, lambda *_: (0, 0, 0, 0), pipeline_mode=pl.Buffered(1)),
        out_shape=jax.ShapeDtypeStruct(block, BF),
        scratch_shapes=[
            pltpu.VMEM((steps * m, width), F32),
            pltpu.VMEM((3 * third - d // 2 // (third // 2) * (third // 2), wide), F32)],
        compiler_params=vmem(48),
        cost_estimate=cost(2 * rows_in * d * width, lhs, out),
        name="project_weights",
    )(lhs, *parts, out)


def flip(index, bit):
    return index + bit - 2 * bit * lax.rem(lax.div(index, bit), 2)


def quarter_of(pair, x, c, quarter, shift):
    lo = x * shift + c * quarter
    return pair[:, :, lo : lo + quarter]


def sum_kernel(
    ndp, orders, quarter, shift, in_ref, pair_ref, sums_ref, gain_ref,
    ga_hbm, gb_hbm, w_hbm, x0_hbm, x1_hbm, gm_hbm, block_ref,
    held_ref, shared_ref, hidden_ref, block_out, cells_out,
    acc, got, piece, core_out, core_in, pair_got, part_out, part_in, sums, sums_got,
    ga, gb, w, xs, gm, gf, gf_got, rows_out, out_sem, in_sem, here_sem,
):
    seq, dp = lax.axis_index("seq"), lax.axis_index("dp")
    core, xi = lax.rem(seq, 2), lax.div(seq, 2)
    count, third = in_ref.shape[1], in_ref.shape[2]
    dims = [1 << b for b in range(ndp.bit_length() - 1)]

    def to(axis, bit):
        return {"dp": flip(dp, bit) if axis == "dp" else dp, "seq": flip(seq, bit) if axis == "seq" else seq}

    partners = [to("seq", 1), to("seq", 2)] + [to("dp", b) for b in dims]
    here = [
        pltpu.make_async_copy(src, dst, here_sem.at[n])
        for n, (src, dst) in enumerate((
            (ga_hbm, ga), (gb_hbm, gb), (w_hbm, w), (x0_hbm, xs.at[0]), (x1_hbm, xs.at[1]), (gm_hbm, gm)))
    ]
    for c in here:
        c.start()
    barrier = pltpu.get_barrier_semaphore()
    for p in partners:
        pl.semaphore_signal(barrier, inc=1, device_id=p, device_id_type=pl.DeviceIdType.MESH)
    pl.semaphore_wait(barrier, len(partners))
    used = []

    def copy(src, dst, target, always=True):
        n = len(used)
        c = pltpu.make_async_remote_copy(
            src_ref=src, dst_ref=dst, send_sem=out_sem.at[n], recv_sem=in_sem.at[n], device_id=target,
            device_id_type=pl.DeviceIdType.MESH)
        used.append((c, always))
        return c

    part = third // 2
    steps = len(orders[0])
    flying = {}

    def start(i, h, k):
        half = count >> (k + 1)
        rows = pl.ds(h * part, part)
        src = (in_ref if k == 0 else acc).at[i, pl.ds(half, half), rows]
        c = copy(src, got.at[i, pl.ds(count - 2 * half, half), rows], to(*orders[2 * i + h][k]))
        c.start()
        flying[i, h] = c

    def finish(i, h, k):
        flying[i, h].wait_recv()
        half = count >> (k + 1)
        rows = slice(h * part, (h + 1) * part)
        for b in range(half):
            kept = in_ref[i, b, rows] if k == 0 else acc[i, b, rows]
            acc[i, b, rows] = (kept.astype(F32) + got[i, count - 2 * half + b, rows].astype(F32)).astype(BF)
        if k + 1 < steps:
            start(i, h, k + 1)

    for i in range(3):
        start(i, 0, 0)
    mine = core == lax.div(dp, ndp // 2)
    over_dp = copy(pair_ref, pair_got, to("dp", ndp // 2), False)
    over_core = copy(part_out, part_in, to("seq", 1), False)

    @pl.when(jnp.logical_not(mine))
    def _():
        over_dp.start()

    for c in here[:3]:
        c.wait()
    cells, block, d = x0_hbm.shape
    split = ga.shape[1]
    qkv_sums = [0.0, 0.0]
    for r in range(4 * cells):
        rows = slice(r * block, (r + 1) * block)
        a, b = ga[rows], gb[rows]
        gf[rows] = (nt(a, w[:, :split]) + nt(b, w[:, split:])).astype(BF)
        qkv_sums = [t + jnp.sum(v.astype(F32), axis=0, keepdims=True) for t, v in zip(qkv_sums, (a, b))]
    to_core = []
    for k in (1, 3):
        for c in range(cells):
            rows = pl.ds(pl.multiple_of((4 * c + (seq ^ k)) * block, block), block)
            to_core.append(copy(gf.at[rows], gf_got.at[rows], to("seq", 1)))
            to_core[-1].start()

    small = []
    small_order = [("seq", 2)] + [("dp", b) for b in dims] + [("seq", 1)]

    def small_step():
        n = len(small)
        if n:
            small[-1].wait_recv()
            if n < len(small_order):
                sums[n] = sums[n - 1] + sums_got[n - 1]
            else:
                shared_ref[0] = sums[n - 1]
                shared_ref[1] = sums_got[n - 1]
                return
        c = copy(sums.at[n], sums_got.at[n], to(*small_order[n]))
        c.start()
        small.append(c)

    for i in range(3):
        finish(i, 0, 0)
        start(i, 1, 0)
    for c in here[3:]:
        c.wait()
    for c in to_core:
        c.wait_recv()
    norm_sums = [0.0, 0.0]
    for k in (0, 1):
        for c in range(cells):
            rows = pl.ds(pl.multiple_of((4 * c + (seq ^ (2 * k))) * block, block), block)
            g = gf[rows].astype(F32) + gf_got[rows].astype(F32)
            n, rstd = block_norm(xs[k, c].astype(F32))
            mid = gm[(k * cells + c) * block : (k * cells + c + 1) * block]
            rows_out[k, c] = (mid + block_norm_back(g, n, rstd, gain_ref[...])).astype(BF)
            norm_sums = [t + jnp.sum(v, axis=0, keepdims=True) for t, v in zip(norm_sums, (g * n, g))]
    sums[0] = sums_ref[...]
    sums[0, 0:1, :d] = norm_sums[0]
    sums[0, 1:2, :d] = norm_sums[1]
    sums[0, 7:8, :split] = qkv_sums[0]
    sums[0, 7:8, split : w.shape[1]] = qkv_sums[1]
    small_step()
    for k in range(1, steps):
        for h in (0, 1):
            for i in range(3):
                finish(i, h, k - h)
        if k < 4:
            small_step()
    for i in range(3):
        finish(i, 1, steps - 1)

    for i in range(3):
        piece[i * third : (i + 1) * third] = acc[i, 0].astype(F32)
    for c in (0, 1):

        @pl.when(core == c)
        def _():
            core_out[...] = piece[(1 - c) * quarter : (2 - c) * quarter].astype(BF)

    swap_core = copy(core_out, core_in, to("seq", 1))
    swap_core.start()
    mine_cells = pl.ds(xi * cells, cells)
    back = [
        copy(block_ref.at[1], block_out.at[mine_cells], to("seq", 2)),
        copy(rows_out.at[1], cells_out.at[mine_cells], to("seq", 2)),
    ]
    keep = [
        pltpu.make_async_copy(src, dst.at[mine_cells], here_sem.at[len(here) + n])
        for n, (src, dst) in enumerate(((block_ref.at[0], block_out), (rows_out.at[0], cells_out)))
    ]
    for c in back + keep:
        c.start()
    swap_core.wait_recv()
    for c in (0, 1):

        @pl.when(core == c)
        def _():
            piece[(1 - c) * quarter : (2 - c) * quarter] = core_in[...].astype(F32)

    held_ref[0] = piece[...].astype(BF)

    ends = []
    far = dims[::-1]
    parts = 6
    rows_of = [pl.ds(i * (3 * third // parts), 3 * third // parts) for i in range(parts)]

    def share(i, k):
        n = 1 << k
        c = copy(held_ref.at[pl.ds(0, n), rows_of[i]], held_ref.at[pl.ds(n, n), rows_of[i]], to("dp", far[k]))
        c.start()
        return c

    first = share(0, 0)
    for i in range(parts):
        first.wait_recv()
        c = share(i, 1)
        if i + 1 < parts:
            first = share(i + 1, 0)
        for k in range(2, len(far)):
            c.wait_recv()
            c = share(i, k)
        ends.append(c)
        if i == 0:
            small_step()

    for x in (0, 1):
        for c in (0, 1):

            @pl.when(mine & (xi == x) & (core == c))
            def _():
                over_dp.wait_recv()
                total = pair_ref[...].astype(F32) + pair_got[...].astype(F32)
                hidden_ref[...] = quarter_of(total, x, c, quarter, shift)
                part_out[...] = quarter_of(total, x, 1 - c, quarter, shift).astype(BF)

    @pl.when(mine)
    def _():
        over_core.start()
        over_core.wait_send()

    @pl.when(jnp.logical_not(mine))
    def _():
        over_dp.wait_send()
        over_core.wait_recv()
        hidden_ref[...] = part_in[...].astype(F32)

    small_step()
    for c in keep:
        c.wait()
    for c in ends + back:
        c.wait_recv()
    for c, always in used:
        if always:
            c.wait_send()


def sum_and_gather(place, blocks, pair, sums, gain, ga, gb, w, x0, x1, gmiddle, block_rows, ndp, orders, quarter, shift):
    _, count, third, wide = blocks.shape
    _, depth, width = pair.shape
    cells, block, d = x0.shape
    in_vmem, hbm = pl.BlockSpec(memory_space=pltpu.VMEM), pl.BlockSpec(memory_space=pl.ANY)
    dims = ndp.bit_length() - 1
    copies = 6 * len(orders[0]) + 2 + (2 + dims) + 1 + 2 + 6 * dims + 2 * cells
    shape = jax.ShapeDtypeStruct
    both = (2 * cells, block, d)
    outs = [
        shape((ndp, 3 * third, wide), BF), shape((2, *sums.shape), F32), shape((2, depth, quarter), F32),
        shape(both, BF), shape(both, BF)]
    return pl.pallas_call(
        functools.partial(sum_kernel, ndp, orders, quarter, shift),
        in_specs=[in_vmem] * 4 + [hbm] * 7,
        out_specs=[in_vmem] * 3 + [hbm] * 2,
        out_shape=outs,
        scratch_shapes=[
            pltpu.VMEM((3, count // 2, third, wide), BF),
            pltpu.VMEM((3, count - 1, third, wide), BF),
            pltpu.VMEM((3 * third, wide), F32),
            pltpu.VMEM((quarter, wide), BF),
            pltpu.VMEM((quarter, wide), BF),
            pltpu.VMEM((2, depth, width), BF),
            pltpu.VMEM((2, depth, quarter), BF),
            pltpu.VMEM((2, depth, quarter), BF),
            pltpu.VMEM((2 + dims, *sums.shape), F32),
            pltpu.VMEM((2 + dims, *sums.shape), F32),
            pltpu.VMEM(ga.shape, BF),
            pltpu.VMEM(gb.shape, BF),
            pltpu.VMEM(w.shape, BF),
            pltpu.VMEM((2, *x0.shape), BF),
            pltpu.VMEM(gmiddle.shape, F32),
            pltpu.VMEM((4 * cells * block, d), BF),
            pltpu.VMEM((4 * cells * block, d), BF),
            pltpu.VMEM((2, *x0.shape), BF),
            pltpu.SemaphoreType.DMA((copies,)),
            pltpu.SemaphoreType.DMA((copies,)),
            pltpu.SemaphoreType.DMA((8,)),
        ],
        compiler_params=pltpu.CompilerParams(vmem_limit_bytes=60 << 20, collective_id=0, has_side_effects=True),
        cost_estimate=cost(0, blocks),
        name="sum_and_gather",
    )(blocks, pair, sums, gain, ga, gb, w, x0, x1, gmiddle, block_rows)


def sum_and_gather_by_steps(place, blocks, pair, sums, gain, ga, gb, w, x0, x1, gmiddle, block_rows, ndp, orders, quarter, shift):
    seq, dp = lax.axis_index("seq"), lax.axis_index("dp")
    core, xi = seq % 2, seq // 2
    cells, block, d = x0.shape
    gfirst, sums_qkv = project_back(ga, gb, w, block)
    gfirst_got = swap(gfirst.reshape(-1, block, d), "seq", 1).reshape(cells, 4 * block, d)
    cell_rows, sums1 = cells_back(place, gfirst.reshape(cells, 4 * block, d), gfirst_got, x0, x1, gmiddle, gain)
    sums = sums.at[:2, :d].set(sums1).at[7, : w.shape[1]].set(sums_qkv[0])
    count = blocks.shape[1]
    parts = []
    part = blocks.shape[2] // 2
    for n, steps in enumerate(orders):
        rows = blocks[n // 2, :, n % 2 * part : (n % 2 + 1) * part]
        sent, kept = rows[count // 2 :], rows[: count // 2]
        for k, (axis, bit) in enumerate(steps):
            got = swap(sent, axis, bit)
            if k + 1 < len(steps):
                sent, kept = halve(kept, got)
        parts.append(low(kept.astype(F32) + got.astype(F32))[0])
    piece = jnp.concatenate(parts, 0)
    halves = piece[: 2 * quarter].reshape(2, quarter, -1)
    ours, theirs = pick(halves, core, 0), swap(pick(halves, 1 - core, 0), "seq", 1)
    held = jnp.concatenate(
        [jnp.where(core == 0, ours, theirs), jnp.where(core == 0, theirs, ours), piece[2 * quarter :]], 0)[None]
    bits = [1 << b for b in range(ndp.bit_length() - 1)]
    for bit in bits[::-1]:
        held = jnp.concatenate([held, swap(held, "dp", bit)], 0)
    for axis, bit in [("seq", 2)] + [("dp", b) for b in bits]:
        sums = sums + swap(sums, axis, bit)
    nj = ndp // 2
    across = [(d * 4 + t, (d ^ nj) * 4 + t) for d in range(ndp) for t in range(4) if d // nj != t % 2]
    total = pair.astype(F32) + lax.ppermute(pair, ("dp", "seq"), across).astype(F32)
    parts = [
        jnp.where(xi == 0, quarter_of(total, 0, c, quarter, shift), quarter_of(total, 1, c, quarter, shift)) for c in (0, 1)]
    theirs = swap(low(jnp.where(core == 0, parts[1], parts[0])), "seq", 1).astype(F32)
    hidden = jnp.where(core == dp // nj, jnp.where(core == 0, parts[0], parts[1]), theirs)

    def both_cells(rows):
        own, got = rows[0], swap(rows[1], "seq", 2)
        return jnp.concatenate([jnp.where(xi == 0, own, got), jnp.where(xi == 0, got, own)], 0)

    return held, jnp.stack([sums, swap(sums, "seq", 1)]), hidden, both_cells(block_rows), both_cells(cell_rows)


def assemble_kernel(bits, tiles, held_ref, e_ref, qkv_ref, out_ref, q_ref, o_ref):
    ndp, _, wide = held_ref.shape
    quarter, d = out_ref.shape
    heads, head = e_ref.shape
    tall = o_ref.shape[0] // ndp
    dp = lax.axis_index("dp")
    for j in range(ndp):
        rel = dp ^ j
        slot = sum(jnp.where(rel & b != 0, 1 << k, 0) for k, b in enumerate(bits))
        block = held_ref[slot].astype(F32)
        for c in (0, 1):
            q_ref[c, :, j * wide : (j + 1) * wide] = block[c * quarter : (c + 1) * quarter]
        for t, lo in enumerate(range(0, d, wide)):
            hi = min(lo + wide, d)
            at = 2 * quarter + t * tall
            o_ref[j * tall : (j + 1) * tall, lo:hi] = block[at : at + tall, : hi - lo]
    for part in range(3):
        for c in (0, 1):
            row = jnp.concatenate([q_ref[c, :, 128 * t : 128 * t + 128] for t in tiles[part]], 1)
            lo = part * d + c * head
            qkv_ref[:, lo : lo + head] = nn(row.astype(BF), e_ref[...])
    for h in range(o_ref.shape[0] // 64):
        out_ref[h * HD : (h + 1) * HD] = o_ref[h * 64 : h * 64 + HD]


def assemble(held, e, quarter, d, bits, tiles):
    ndp, _, wide = held.shape
    outs = [jax.ShapeDtypeStruct((quarter, 3 * d), F32), jax.ShapeDtypeStruct((quarter, d), F32)]
    return pl.pallas_call(
        functools.partial(assemble_kernel, bits, tiles),
        in_specs=[pl.BlockSpec(memory_space=pltpu.VMEM)] * 2,
        out_specs=[pl.BlockSpec(memory_space=pltpu.VMEM)] * 2,
        out_shape=outs,
        scratch_shapes=[pltpu.VMEM((2, quarter, ndp * wide), F32), pltpu.VMEM((quarter // HD * 64, d), F32)],
        compiler_params=vmem(40),
        cost_estimate=cost(6 * 2 * quarter * e.size, held, e, *outs),
        name="assemble",
    )(held, e)


def low(value):
    return lax.optimization_barrier(value.astype(BF))


def after(value, *first):
    return lax.optimization_barrier((value, *first))[0]


def swap(value, axis, bit):
    return lax.ppermute(value, axis, [(i, i ^ bit) for i in range(lax.axis_size(axis))])


def swap_by_core(value, steps):
    ndp, nseq = lax.axis_size("dp"), lax.axis_size("seq")
    pairs = []
    for d in range(ndp):
        for s in range(nseq):
            axis, bit = steps[s % 2]
            e, t = (d, s ^ bit) if axis == "seq" else (d ^ bit, s)
            pairs.append((d * nseq + s, e * nseq + t))
    return lax.ppermute(value, ("dp", "seq"), pairs)


def pick(array, index, axis):
    return lax.dynamic_index_in_dim(array, index, axis, keepdims=False)


def one_hot(rows, cols, source):
    r = lax.broadcasted_iota(jnp.int32, (rows, cols), 0)
    return (r == source[None, :]).astype(BF)


def halve(kept, got):
    half = kept.shape[0] // 2
    total = kept.astype(F32) + got.astype(F32)
    return low(total[half:]), low(total[:half])


def per_device(
    cells, prefix_len, ln1_gain, ln1_bias, w_qkv, bias_q, bias_v, w_out, bias_out,
    ln2_gain, ln2_bias, w_up, bias_up, w_down, bias_down, cotangent,
):
    seq, ndp = lax.axis_size("seq"), lax.axis_size("dp")
    s, dp = lax.axis_index("seq"), lax.axis_index("dp")
    core, xi = s % 2, s // 2
    assert seq == 4
    pairs, block, D = cells.shape
    C = pairs // 2
    T = block * seq
    HH = H // 2
    WH = HH * 64
    half = D // 2
    quarter = D // 4
    FF = w_up.shape[1]
    nj = ndp // 2
    R = 2 * C * block
    row = lambda v: v.reshape(1, -1)
    place = s.reshape(1).astype(jnp.int32)

    def split_cells(a):
        return lax.dynamic_slice_in_dim(a, xi * C, C, 0), lax.dynamic_slice_in_dim(a, (1 - xi) * C, C, 0)

    x0, x_other = split_cells(cells)
    x1 = swap(x_other, "seq", 2)
    x0_got = swap(x0, "seq", 1)
    prefix = lax.dynamic_slice_in_dim(prefix_len, xi * C, C, 0)

    col = jnp.arange(WH)
    head_col = jnp.where(col % 64 < HD, core * half + (col // 64) * HD + col % 64, -1)
    w_parts = []
    for j in range(3):
        lo = j * D // 128 * 128
        hi = min(-(-(j + 1) * D // 128) * 128, 3 * D)
        e = one_hot(hi - lo, WH, jnp.where(head_col >= 0, head_col + j * D - lo, -1))
        w_parts.append(jnp.dot(w_qkv[:, lo:hi], e, preferred_element_type=F32).astype(BF))
    cut = FIRST * 128
    in_order = lambda parts: [p[..., :cut] for p in parts] + [p[..., cut:] for p in parts]
    w_own = jnp.concatenate(in_order(w_parts), 1)

    def pad_heads(v, ones):
        v = lax.dynamic_slice_in_dim(v, core * half, half, 0).reshape(HH, HD)
        return jnp.concatenate([v, jnp.full((HH, 3), ones, F32), jnp.zeros((HH, 5), F32)], 1).reshape(WH)

    bias_own = jnp.concatenate(in_order([pad_heads(bias_q, 0.0), pad_heads(jnp.zeros_like(bias_q), 1.0), pad_heads(bias_v, 1.0)]))
    wo = w_out.reshape(2, HH, HD, D)
    wo = jnp.concatenate([wo, jnp.zeros((2, HH, 64 - HD, D), BF)], 2).reshape(2, WH, D)
    wo = jnp.where(core == 0, wo, wo[::-1]).reshape(2 * WH, D)

    x1 = after(x1, wo, w_own)
    x1_got = swap(x1, "seq", 1)
    first, qkv = project(place, (x0, x0_got, x1, x1_got), row(ln1_gain), row(ln1_bias), w_own, row(bias_own))
    c0, c_other = split_cells(cotangent)
    c1 = swap(after(c_other, x1), "seq", 2)
    qkv, c1 = lax.optimization_barrier((qkv, c1))
    c_pair = jnp.concatenate([c0, c1], 0)
    c_got = swap(c_pair, "seq", 1)
    att, q_aug = attention_forward(qkv, prefix)
    att_got = swap(att, "seq", 1)
    middle, second = attention_output(place, att, att_got, x0, x1, wo, row(bias_out), row(ln2_gain), row(ln2_bias))
    blocks = lambda v: v.reshape(-1, block, v.shape[-1])
    rows_of = lambda v: v.reshape(-1, v.shape[-1])
    second_got = rows_of(swap(blocks(second), "seq", 1))
    cot, cot_got = rows_of(c_pair), rows_of(c_got)

    act, gpre, out_own, out_send, gs_own, gs_send, bias_up_sum = hidden_layer(
        second, second_got, cot, cot_got, w_up, row(bias_up), w_down.T, block)
    gs_got = rows_of(swap(blocks(gs_send), "seq", 1))
    out_got = rows_of(swap(blocks(out_send), "seq", 1))

    low_bits = [1 << b for b in range(nj.bit_length() - 1)]
    rest = low_bits[2:]

    def order(*names):
        n = {"x": ("seq", 2), "y": ("dp", 1), "z": ("dp", 2)}
        return [n[k] for k in names] + [("dp", b) for b in rest]

    def codes(steps, n):
        return [n if axis == "seq" else bit for axis, bit in steps]

    down_orders = (order("x", "z", "y"), order("y", "x", "z"))
    up_orders = (order("z", "x", "y"), order("y", "z", "x"))
    top = [("dp", nj)]
    q_orders = [order(*names) + top for names in ("xyz", "xyz", "yxz", "yxz", "zxy", "zyx")]

    def send(sent, orders, k):
        return swap_by_core(sent, (orders[0][k], orders[1][k]))

    d_sent, d_kept = hidden_weights(act, cot, cot_got, FF, nj, [codes(o, nj) for o in down_orders])
    d_got = send(d_sent, down_orders, 0)
    u_sent, u_kept = hidden_weights(gpre, second, second_got, FF, nj, [codes(o, nj) for o in up_orders])
    u_got = send(u_sent, up_orders, 0)

    gmiddle, gbranch, gatt, block_rows, sums2 = middle_back(
        after(gs_own, d_sent, u_sent), gs_got, out_own, out_got, middle, cot, wo, row(ln2_gain), row(bias_down), block)
    gatt_got = swap(gatt, "seq", 1)
    o_send, o_keep = output_weights(place, att, att_got, gbranch, block)
    o_got = swap(o_send, "seq", 1)
    g_out = o_keep + o_got[::-1].astype(F32)

    shape = (2, C, block, 2 * WH)
    gatt, gatt_got = gatt.reshape(shape), gatt_got.reshape(shape)
    d_sent, d_kept = halve(d_kept, d_got)
    d_got = send(d_sent, down_orders, 1)
    g_first = attention_backward(qkv, q_aug, after(gatt, d_sent, g_out), gatt_got, att, prefix, 0, FIRST).reshape(C * T, -1)
    d_sent, d_kept = halve(d_kept, after(d_got, g_first))
    d_got = send(d_sent, down_orders, 2)
    u_sent, u_kept = halve(u_kept, after(u_got, d_sent))
    u_got = send(u_sent, up_orders, 1)
    g_rest = attention_backward(
        qkv, q_aug, after(gatt, d_sent, u_sent), gatt_got, att, prefix, FIRST, WH // 128).reshape(C * T, -1)
    u_sent, u_kept = halve(u_kept, after(u_got, g_rest))
    u_got = send(u_sent, up_orders, 2)
    q_blocks = project_weights(
        first.reshape(C * T, D), [g_first, after(g_rest, u_sent)], -(-3 * WH // (128 * 16)) * 128 * 16, g_out, ndp,
        [codes(o, ndp) for o in q_orders])
    for k in range(3, len(down_orders[0])):
        d_sent, d_kept = halve(d_kept, d_got)
        d_got = send(d_sent, down_orders, k)
        u_sent, u_kept = halve(u_kept, u_got)
        u_got = send(u_sent, up_orders, k)
    d_got, u_got, q_blocks = lax.optimization_barrier((d_got, u_got, q_blocks))
    pair = low(jnp.concatenate([d_kept, u_kept], 0).astype(F32) + jnp.concatenate([d_got, u_got], 0).astype(F32))
    ff_width = bias_up_sum.shape[1]
    sums = jnp.concatenate(
        [jnp.zeros((2, ff_width), F32), jnp.pad(sums2, ((0, 0), (0, ff_width - D))), bias_up_sum, jnp.zeros((1, ff_width), F32)], 0)

    bits = [1 << b for b in range(ndp.bit_length() - 1)]
    shift = half - (-(-D // 128) * 128 - 640)
    block_rows = block_rows.reshape(2, C, block, D)
    finish = sum_and_gather if ndp <= 8 else sum_and_gather_by_steps
    held, sums, hidden, block_out, grad_cells = finish(
        place, q_blocks, pair, sums, row(ln1_gain), g_first, g_rest, w_own, x0, x1, gmiddle, block_rows, ndp, q_orders,
        quarter, shift)
    total = sums[0, :6, :D] + sums[1, :6, :D]
    by_core = jnp.where(core == 0, sums[:, 6:], sums[::-1, 6:])
    pad_up = FF - ff_width
    g_bias_up = jnp.pad(by_core[0, 0], (0, pad_up)) + jnp.pad(by_core[1, 0], (pad_up, 0))
    more = WH - cut

    def column_sums(j):
        v = jnp.concatenate(
            [by_core[:, 1, j * cut : (j + 1) * cut], by_core[:, 1, 3 * cut + j * more : 3 * cut + (j + 1) * more]], 1)
        return v.reshape(2 * HH, 64)[:, :HD].reshape(D)

    shared = [total[0], total[1], column_sums(0), column_sums(2), total[2], total[3], total[4], total[5], g_bias_up]

    head_of = jnp.arange(half)
    e_out = (jnp.arange(WH)[:, None] == (head_of // HD * 64 + head_of % HD)[None, :]).astype(BF)
    n_pairs = WH // 128
    tiles = [[tile_of(part, p, n_pairs) for p in range(n_pairs)] for part in range(3)]
    final_qkv, final_out = assemble(held, e_out, quarter, D, bits[::-1], tiles)

    final_down, final_up = hidden[0], hidden[1].T

    return (
        block_out, grad_cells, shared[0], shared[1], final_qkv, shared[2], shared[3], final_out,
        shared[4], shared[5], shared[6], final_up, shared[8], final_down, shared[7],
    )


def solution(mesh):
    rows = P("dp", "seq", None)
    return jax.shard_map(
        per_device,
        mesh=mesh,
        in_specs=(rows, P("dp")) + (P(),) * 13 + (rows,),
        out_specs=(rows, rows, P(), P(), P("seq", None), P(), P(), P("seq", None), P(), P(), P(), P("seq", "dp"), P(), P("dp", "seq"), P()),
        check_vma=False,
    )
```

```python
import functools
import math
import jax
import jax.numpy as jnp
from jax import lax
from jax.experimental import pallas as pl
from jax.experimental.pallas import tpu as pltpu
from jax.sharding import PartitionSpec as P

H = 20
HD=56
F32=jnp.float32; BF=jnp.bfloat16
LOG2=math.log2(math.e)
NEG=-1e30
def nt(a,b): return lax.dot_general(a,b,(((1,),(1,)),((),())),preferred_element_type=F32)
def nn(a,b): return lax.dot_general(a,b,(((1,),(0,)),((),())),preferred_element_type=F32)
def tn(a,b): return lax.dot_general(a,b,(((0,),(0,)),((),())),preferred_element_type=F32)

def split3(v):
    a=v.astype(BF); r=v-a.astype(F32); b=r.astype(BF); r=r-b.astype(F32)
    return a.astype(F32),b.astype(F32),r

def dup(k):
    low=lax.broadcasted_iota(jnp.int32,k.shape,1)<64
    r=pltpu.roll(k,64,1)
    return jnp.where(low,k,r).astype(BF), jnp.where(low,r,k).astype(BF)

def fwd_kernel(B, prefix_ref, q_ref,k_ref,v_ref,o_ref,qa_ref):
    T=q_ref.shape[1]
    p=prefix_ref[pl.program_id(0)]
    lane=lax.broadcasted_iota(jnp.int32,(T,128),1); low=lane<64
    q=q_ref[0].astype(F32)*(HD**-0.5*LOG2)
    hi=q.astype(BF).astype(F32); res=pltpu.roll(q-hi,64,1)
    qa=[jnp.where(low,hi,res),jnp.where(low,res,hi)]
    qab=[x.astype(BF) for x in qa]
    ka=dup(k_ref[0].astype(F32))
    lane_b=lane[:B]
    v32=v_ref[0].astype(F32)
    vm=[jnp.where(low,v32,0.0).astype(BF),jnp.where(low,0.0,v32).astype(BF)]
    row=lax.broadcasted_iota(jnp.int32,(B,B),0); col=lax.broadcasted_iota(jnp.int32,(B,B),1)
    tri=col<=row
    first=tri|((col<p)&(row<p))
    for i in range(T//B):
        n=(i+1)*B; rows=slice(i*B,n)
        outs=[]
        for h in range(2):
            s=nt(qab[h][rows],ka[h][:n])
            d=jnp.where(first if i==0 else tri,s[:,n-B:],NEG)
            if i: s=jnp.concatenate([s[:,:n-B],d],1)
            else: s=d
            m=jnp.max(s,axis=1,keepdims=True)
            outs.append((jnp.exp2(s-m).astype(BF),m))
        o=nn(jnp.concatenate([outs[0][0],outs[1][0]],1),jnp.concatenate([vm[0][:n],vm[1][:n]],0))
        ls=[o[:,56:57],o[:,120:121]]
        for h in range(2):
            lse=-(outs[h][1]+jnp.log2(ls[h]))
            a,b,c=split3(lse)
            z=64*h+56
            x=jnp.where(lane_b==z,a,jnp.where(lane_b==z+1,b,jnp.where(lane_b==z+2,c,qa[h][rows])))
            qa_ref[0,rows,128*h:128*h+128]=x.astype(BF)
        o_ref[0,rows]=(o*jnp.where(low[:B],1.0/ls[0],1.0/ls[1])).astype(BF)


FIRST=3


def tile_of(part,p,pairs):
    if isinstance(p,int):
        return part*FIRST+p if p<FIRST else 3*FIRST+part*(pairs-FIRST)+p-FIRST
    return jnp.where(p<FIRST,part*FIRST+p,3*FIRST+part*(pairs-FIRST)+p-FIRST)


def attention_forward(qkv,prefix,B=256):
    C,T,W=qkv.shape; NP=W//384
    spec=lambda part: pl.BlockSpec((1,T,128),lambda c,p,pr: (c,0,tile_of(part,p,NP)))
    return pl.pallas_call(functools.partial(fwd_kernel,B),
        grid_spec=pltpu.PrefetchScalarGridSpec(num_scalar_prefetch=1,grid=(C,NP),
            in_specs=[spec(0),spec(1),spec(2)],
            out_specs=[pl.BlockSpec((1,T,128),lambda c,p,pr:(c,0,p)),pl.BlockSpec((1,T,256),lambda c,p,pr:(c,0,p))]),
        out_shape=[jax.ShapeDtypeStruct((C,T,128*NP),BF),jax.ShapeDtypeStruct((C,T,256*NP),BF)],
        compiler_params=pltpu.CompilerParams(vmem_limit_bytes=40<<20),
        cost_estimate=pl.CostEstimate(flops=1,bytes_accessed=1,transcendentals=0),
        name="attention_forward",
    )(prefix,qkv,qkv,qkv)

def bwd_kernel(B, prefix_ref, qa_ref,q_ref,k_ref,v_ref,go_ref,gg_ref,o_ref,out_ref,dk_ref,dv_ref,do_ref):
    T=q_ref.shape[1]; NP=pl.num_programs(1); W=out_ref.shape[2]
    block=T//4
    s=lax.axis_index("seq")
    for k,piece in enumerate((go_ref[0,0],go_ref[1,0],gg_ref[0,0],gg_ref[1,0])):
        place=s^(2*(k%2)+k//2)
        do_ref[pl.ds(pl.multiple_of(place*block,block),block)]=piece
    pr=pl.program_id(1)
    p=prefix_ref[pl.program_id(0)]
    lane=lax.broadcasted_iota(jnp.int32,(T,128),1); low=lane<64
    k32=k_ref[0].astype(F32); q32=q_ref[0].astype(F32); do32=do_ref[...].astype(F32)
    ka=dup(k32)
    zero=jnp.zeros_like(k32)
    km=[jnp.where(low,k32,zero).astype(BF),jnp.where(low,zero,k32).astype(BF)]
    qm=[jnp.where(low,q32,zero).astype(BF),jnp.where(low,zero,q32).astype(BF)]
    dom=[jnp.where(low,do32,zero),jnp.where(low,zero,do32)]
    o32=o_ref[0].astype(F32)
    doa=[]
    for h in range(2):
        dl=-jnp.sum(dom[h]*o32,axis=1,keepdims=True)
        a,b,c=split3(dl); z=64*h+56
        doa.append(jnp.where(lane==z,a,jnp.where(lane==z+1,b,jnp.where(lane==z+2,c,dom[h]))).astype(BF))
    dom=[x.astype(BF) for x in dom]
    key=lax.broadcasted_iota(jnp.int32,(B,B),0); qry=lax.broadcasted_iota(jnp.int32,(B,B),1)
    tri=key<=qry
    first=tri|((key<p)&(qry<p))
    sc=HD**-0.5
    for i in reversed(range(T//B)):
        n=(i+1)*B; rows=slice(i*B,n)
        pbs=[];dss=[]
        for h in range(2):
            s=nt(ka[h][:n],qa_ref[0,rows,128*h:128*h+128])
            d=jnp.where(first if i==0 else tri,s[n-B:],NEG)
            s=jnp.concatenate([s[:n-B],d],0) if i else d
            e=jnp.exp2(s)
            dp=nt(v_ref[0,:n],doa[h][rows])
            dss.append((e*dp).astype(BF)); pbs.append(e.astype(BF))
        dq=tn(jnp.concatenate(dss,0),jnp.concatenate([km[0][:n],km[1][:n]],0))
        out_ref[0,rows,pl.ds(pl.multiple_of(pr*128,128),128)]=(dq*sc).astype(BF)
        dv=nn(pbs[0],dom[0][rows])+nn(pbs[1],dom[1][rows])
        dk=nn(dss[0],qm[0][rows])+nn(dss[1],qm[1][rows])
        if i==T//B-1:
            dv_ref[...]=dv; dk_ref[...]=dk
        else:
            dv_ref[:n]+=dv; dk_ref[:n]+=dk
    out_ref[0,:,pl.ds(pl.multiple_of((NP+pr)*128,128),128)]=(dk_ref[...]*sc).astype(BF)
    out_ref[0,:,pl.ds(pl.multiple_of((2*NP+pr)*128,128),128)]=dv_ref[...].astype(BF)

def attention_backward(qkv,qa,do,do_got,o,prefix,p0,p1,B=256):
    C,T,W=qkv.shape; NP=W//384
    width=384*(p1-p0)
    spec=lambda part: pl.BlockSpec((1,T,128),lambda c,p,pr: (c,0,tile_of(part,p0,NP)+p))
    return pl.pallas_call(functools.partial(bwd_kernel,B),
        grid_spec=pltpu.PrefetchScalarGridSpec(num_scalar_prefetch=1,grid=(C,p1-p0),
            in_specs=[pl.BlockSpec((1,T,256),lambda c,p,pr:(c,0,p0+p)),spec(0),spec(1),spec(2),
                pl.BlockSpec((2,1,T//4,128),lambda c,p,pr:(0,c,0,p0+p)),pl.BlockSpec((2,1,T//4,128),lambda c,p,pr:(0,c,0,NP+p0+p)),
                pl.BlockSpec((1,T,128),lambda c,p,pr:(c,0,p0+p))],
            out_specs=pl.BlockSpec((1,T,width),lambda c,p,pr:(c,0,0)),
            scratch_shapes=[pltpu.VMEM((T,128),F32)]*2+[pltpu.VMEM((T,128),BF)]),
        out_shape=jax.ShapeDtypeStruct((C,T,width),BF),
        compiler_params=pltpu.CompilerParams(vmem_limit_bytes=40<<20),
        cost_estimate=pl.CostEstimate(flops=1,bytes_accessed=1,transcendentals=0),
        name="attention_backward",
    )(prefix,qa,qkv,qkv,qkv,do,do_got,o)


epsilon = 1e-05


def vmem(megabytes):
    return pltpu.CompilerParams(vmem_limit_bytes=megabytes << 20)


def whole(array):
    return pl.BlockSpec(array.shape, lambda *_: (0,) * array.ndim, pipeline_mode=pl.Buffered(1))


def cost(flops, *arrays):
    return pl.CostEstimate(flops=1, bytes_accessed=1, transcendentals=0)


def block_norm(rows):
    width = rows.shape[1]
    mean = jnp.sum(rows, axis=1, keepdims=True) * (1.0 / width)
    centred = rows - mean
    rstd = lax.rsqrt(jnp.sum(centred * centred, axis=1, keepdims=True) * (1.0 / width) + epsilon)
    return centred * rstd, rstd


def block_norm_back(grad, normed, rstd, gain):
    inv = 1.0 / grad.shape[1]
    dn = grad * gain
    a = jnp.sum(dn, axis=1, keepdims=True) * inv
    b = jnp.sum(dn * normed, axis=1, keepdims=True) * inv
    return rstd * (dn - a - normed * b)


def add_sums(ref, start, *rows):
    for k, v in enumerate(rows):
        total = jnp.sum(v, axis=0, keepdims=True)
        ref[k : k + 1] = jnp.where(start, total, ref[k : k + 1] + total)


def project_kernel(s_ref, a_ref, b_ref, c_ref, d_ref, g_ref, h_ref, w_ref, bias_ref, first_ref, out_ref):
    k = pl.program_id(1)
    x = jnp.where(k < 2, jnp.where(k == 0, a_ref[0].astype(F32), b_ref[0].astype(F32)),
                  jnp.where(k == 2, c_ref[0].astype(F32), d_ref[0].astype(F32)))
    n, _ = block_norm(x)
    first = (n * g_ref[...] + h_ref[...]).astype(BF)
    first_ref[0] = first
    width = w_ref.shape[1]
    for lo in range(0, width, 640):
        cols = slice(lo, min(lo + 640, width))
        out_ref[0, :, cols] = (nn(first, w_ref[:, cols]) + bias_ref[:, cols]).astype(BF)


def project(place, pieces, gain, shift, w, bias):
    cells, rows, d = pieces[0].shape
    width = w.shape[1]
    piece = pl.BlockSpec((1, rows, d), lambda c, k, s: (c, 0, 0))
    at = lambda c, k, s: (c, s[0] ^ k, 0)
    ins = (gain, shift, w, bias)
    outs = [jax.ShapeDtypeStruct((cells, 4 * rows, n), BF) for n in (d, width)]
    return pl.pallas_call(
        project_kernel,
        grid_spec=pltpu.PrefetchScalarGridSpec(
            num_scalar_prefetch=1, grid=(cells, 4), in_specs=[piece] * 4 + [whole(a) for a in ins],
            out_specs=[pl.BlockSpec((1, rows, n), at) for n in (d, width)]),
        out_shape=outs,
        compiler_params=vmem(40),
        cost_estimate=cost(8 * cells * rows * w.size, *pieces, *ins, *outs),
        name="norm_project",
    )(place, *pieces, *ins)


def middle_kernel(s_ref, own_ref, got_ref, a_ref, b_ref, w_ref, c_ref, g_ref, h_ref, middle_ref, second_ref):
    half = own_ref.shape[2]
    out = nn(own_ref[0], w_ref[:half]) + nn(got_ref[0], w_ref[half:])
    x = jnp.where(pl.program_id(0) == 0, a_ref[0].astype(F32), b_ref[0].astype(F32))
    middle = x + out + c_ref[...]
    middle_ref[...] = middle
    n, _ = block_norm(middle)
    second_ref[...] = (n * g_ref[...] + h_ref[...]).astype(BF)


def attention_output(place, own, got, x0, x1, w, bias, gain, shift):
    cells, rows, d = x0.shape
    half = own.shape[2]
    at = pl.BlockSpec((1, rows, half), lambda k, c, s: (c, s[0] ^ (2 * k), 0))
    piece = pl.BlockSpec((1, rows, d), lambda k, c, s: (c, 0, 0))
    ins = (w, bias, gain, shift)
    outs = [jax.ShapeDtypeStruct((2 * cells * rows, d), t) for t in (F32, BF)]
    return pl.pallas_call(
        middle_kernel,
        grid_spec=pltpu.PrefetchScalarGridSpec(
            num_scalar_prefetch=1, grid=(2, cells), in_specs=[at, at, piece, piece] + [whole(a) for a in ins],
            out_specs=[pl.BlockSpec((rows, d), lambda k, c, s: (k * cells + c, 0))] * 2),
        out_shape=outs,
        compiler_params=vmem(32),
        cost_estimate=cost(4 * cells * rows * w.size, x0, x0, *ins, *outs),
        name="attention_output",
    )(place, own, got, x0, x1, *ins)


CHUNK = 768


def hidden_window(core, ff):
    width = -(-(ff // 2) // CHUNK) * CHUNK
    return core * (ff - width), width, core * (width - ff // 2)


def hidden_kernel(
    ff, s0_ref, s1_ref, c0_ref, c1_ref, bu_ref, wu_hbm, wd_hbm,
    act_ref, gpre_ref, out0_ref, out1_ref, gs0_ref, gs1_ref, sum_ref, wu_ref, wd_ref, sem,
):
    i, n = pl.program_id(0), pl.num_programs(0) // 2
    core = lax.rem(lax.axis_index("seq"), 2)
    start, width, skip = hidden_window(core, ff)
    chunks = width // CHUNK

    def copies(k):
        at = pl.multiple_of(start + k * CHUNK, 128)
        cols = pl.ds(k * CHUNK, CHUNK)
        return (
            pltpu.make_async_copy(wu_hbm.at[:, pl.ds(at, CHUNK)], wu_ref.at[:, cols], sem.at[2 * k]),
            pltpu.make_async_copy(wd_hbm.at[:, pl.ds(at, CHUNK)], wd_ref.at[:, cols], sem.at[2 * k + 1]),
        )

    @pl.when(i == 0)
    def _():
        for k in range(chunks):
            for c in copies(k):
                c.start()

    second = jnp.where(i < n, s0_ref[...].astype(F32), s1_ref[...].astype(F32)).astype(BF)
    cot = jnp.where(i < n, c0_ref[...].astype(F32), c1_ref[...].astype(F32)).astype(BF)
    out = gsec = None
    a, b = 0.7978845608, 0.044715
    for k in range(chunks):
        cols = slice(k * CHUNK, (k + 1) * CHUNK)

        @pl.when(i == 0)
        def _():
            for c in copies(k):
                c.wait()

        u = nn(second, wu_ref[:, cols]) + bu_ref[:, pl.ds(pl.multiple_of(start + k * CHUNK, 128), CHUNK)]
        gact = nn(cot, wd_ref[:, cols])
        u2 = u * u
        t = jnp.tanh(u * (a + a * b * u2))
        h = 0.5 + 0.5 * t
        act = u * h
        gpre = gact * (h + u * (0.5 - 0.5 * t * t) * (a + 3 * a * b * u2))
        if k in (0, chunks - 1):
            col = lax.broadcasted_iota(jnp.int32, (1, CHUNK), 1) + k * CHUNK
            mine = (col >= skip) & (col < skip + ff // 2)
            act, gpre = jnp.where(mine, act, 0.0), jnp.where(mine, gpre, 0.0)
        act, gpre = act.astype(BF), gpre.astype(BF)
        act_ref[:, cols] = act
        gpre_ref[:, cols] = gpre
        total = jnp.sum(gpre.astype(F32), axis=0, keepdims=True)
        sum_ref[:, cols] = jnp.where(i == 0, total, sum_ref[:, cols] + total)
        o, g = nt(act, wd_ref[:, cols]), nt(gpre, wu_ref[:, cols])
        out, gsec = (o, g) if out is None else (out + o, gsec + g)

    @pl.when(i < n)
    def _():
        out0_ref[...] = out.astype(BF)
        gs0_ref[...] = gsec.astype(BF)

    @pl.when(i >= n)
    def _():
        out1_ref[...] = out.astype(BF)
        gs1_ref[...] = gsec.astype(BF)


def hidden_layer(second, second_got, cot, cot_got, w_up, bias_up, w_down_t, m):
    rows, d = second.shape
    ff = w_up.shape[1]
    n = rows // m
    width = hidden_window(0, ff)[1]
    lo = pl.BlockSpec((m, d), lambda i: (jnp.minimum(i, n - 1), 0))
    hi = pl.BlockSpec((m, d), lambda i: (jnp.maximum(i - n, 0), 0))
    row = pl.BlockSpec((m, width), lambda i: (i, 0))
    hbm = pl.BlockSpec(memory_space=pl.ANY)
    shape = jax.ShapeDtypeStruct
    outs = [shape((2 * rows, width), BF)] * 2 + [shape((rows, d), BF)] * 4 + [shape((1, width), F32)]
    return pl.pallas_call(
        functools.partial(hidden_kernel, ff),
        grid=(2 * n,),
        in_specs=[lo, hi, lo, hi, whole(bias_up), hbm, hbm],
        out_specs=[row, row, lo, hi, lo, hi, pl.BlockSpec((1, width), lambda i: (0, 0))],
        out_shape=outs,
        scratch_shapes=[pltpu.VMEM((d, width), BF), pltpu.VMEM((d, width), BF), pltpu.SemaphoreType.DMA((2 * (width // CHUNK),))],
        compiler_params=vmem(56),
        cost_estimate=cost(16 * rows * d * width, second, second, cot, cot, w_up, *outs),
        name="hidden_layer",
    )(second, second_got, cot, cot_got, bias_up, w_up, w_down_t)


def middle_back_kernel(
    gs_ref, gs_got_ref, o_ref, o_got_ref, middle_ref, cot_ref, w_ref, g_ref, c_ref,
    gm_ref, gb_ref, gatt_ref, block_ref, sum_ref,
):
    middle, gy = middle_ref[...], cot_ref[...].astype(F32)
    gsecond = gs_ref[...].astype(F32) + gs_got_ref[...].astype(F32)
    n, rstd = block_norm(middle)
    gmiddle = gy + block_norm_back(gsecond, n, rstd, g_ref[...])
    gm_ref[...] = gmiddle
    gbranch = gmiddle.astype(BF)
    gb_ref[...] = gbranch
    gatt_ref[...] = nt(gbranch, w_ref[...]).astype(BF)
    block_ref[...] = (middle + (o_ref[...].astype(F32) + o_got_ref[...].astype(F32)) + c_ref[...]).astype(BF)
    add_sums(sum_ref, pl.program_id(0) == 0, gbranch.astype(F32), gsecond * n, gsecond, gy)


def middle_back(gsec, gsec_got, out, out_got, middle, cot, w, gain, bias, m):
    rows, d = middle.shape
    row = lambda n: pl.BlockSpec((m, n), lambda i: (i, 0))
    ins = (gsec, gsec_got, out, out_got, middle, cot, w, gain, bias)
    shape = jax.ShapeDtypeStruct
    heads = w.shape[0]
    outs = [shape((rows, d), F32), shape((rows, d), BF), shape((rows, heads), BF), shape((rows, d), BF), shape((4, d), F32)]
    return pl.pallas_call(
        middle_back_kernel,
        grid=(rows // m,),
        in_specs=[row(d)] * 6 + [whole(a) for a in ins[6:]],
        out_specs=[row(d), row(d), row(heads), row(d), pl.BlockSpec((4, d), lambda i: (0, 0))],
        out_shape=outs,
        compiler_params=vmem(40),
        cost_estimate=cost(2 * rows * w.size, *ins, *outs),
        name="middle_back",
    )(*ins)


def project_back_kernel(a_ref, b_ref, w_ref, out_ref, sum_ref):
    split = a_ref.shape[1]
    out_ref[...] = (nt(a_ref[...], w_ref[:, :split]) + nt(b_ref[...], w_ref[:, split:])).astype(BF)
    start = pl.program_id(0) == 0
    for ref, cols in ((a_ref, slice(0, split)), (b_ref, slice(split, None))):
        total = jnp.sum(ref[...].astype(F32), axis=0, keepdims=True)
        sum_ref[:, cols] = jnp.where(start, total, sum_ref[:, cols] + total)


def project_back(a, b, w, m):
    rows = a.shape[0]
    d, width = w.shape
    outs = [jax.ShapeDtypeStruct((rows, d), BF), jax.ShapeDtypeStruct((1, width), F32)]
    return pl.pallas_call(
        project_back_kernel,
        grid=(rows // m,),
        in_specs=[pl.BlockSpec((m, a.shape[1]), lambda i: (i, 0)), pl.BlockSpec((m, b.shape[1]), lambda i: (i, 0)), whole(w)],
        out_specs=[pl.BlockSpec((m, d), lambda i: (i, 0)), pl.BlockSpec((1, width), lambda i: (0, 0))],
        out_shape=outs,
        compiler_params=vmem(32),
        cost_estimate=cost(2 * rows * w.size, a, b, w, *outs),
        name="project_back",
    )(a, b, w)


def cells_back_kernel(s_ref, g_ref, got_ref, a_ref, b_ref, gm_ref, gain_ref, out_ref, sum_ref):
    k = pl.program_id(0)
    g = g_ref[0].astype(F32) + got_ref[0].astype(F32)
    n, rstd = block_norm(jnp.where(k == 0, a_ref[0].astype(F32), b_ref[0].astype(F32)))
    out_ref[0, 0] = (gm_ref[...] + block_norm_back(g, n, rstd, gain_ref[...])).astype(BF)
    add_sums(sum_ref, (k == 0) & (pl.program_id(1) == 0), g * n, g)


def cells_back(place, g, got, x0, x1, gmiddle, gain):
    cells, rows, d = x0.shape
    at = pl.BlockSpec((1, rows, d), lambda k, c, s: (c, s[0] ^ (2 * k), 0))
    piece = pl.BlockSpec((1, rows, d), lambda k, c, s: (c, 0, 0))
    outs = [jax.ShapeDtypeStruct((2, cells, rows, d), BF), jax.ShapeDtypeStruct((2, d), F32)]
    return pl.pallas_call(
        cells_back_kernel,
        grid_spec=pltpu.PrefetchScalarGridSpec(
            num_scalar_prefetch=1, grid=(2, cells),
            in_specs=[at, at, piece, piece, pl.BlockSpec((rows, d), lambda k, c, s: (k * cells + c, 0)), whole(gain)],
            out_specs=[pl.BlockSpec((1, 1, rows, d), lambda k, c, s: (k, c, 0, 0)), pl.BlockSpec((2, d), lambda k, c, s: (0, 0))]),
        out_shape=outs,
        compiler_params=vmem(32),
        cost_estimate=cost(0, x0, x0, x0, x0, x0, x0, gmiddle, *outs),
        name="cells_back",
    )(place, g, got, x0, x1, gmiddle, gain)


def store_block(orders, rel, value, sent_ref, kept_ref):
    core = lax.rem(lax.axis_index("seq"), 2)
    half = kept_ref.shape[0]
    places = [
        sum(jnp.where(rel & step != 0, half >> k, 0) for k, step in enumerate(steps)) for steps in orders
    ]
    pos = jnp.where(core == 0, places[0], places[1])

    @pl.when(pos >= half)
    def _():
        sent_ref[pos - half] = value

    @pl.when(pos < half)
    def _():
        kept_ref[pos] = value


def hidden_weights_kernel(orders, ff, nj, lhs_ref, own_ref, got_ref, sent_ref, kept_ref, rhs_ref, acc_ref):
    rows, d = own_ref.shape
    pad = rhs_ref.shape[1]
    step, steps = pl.program_id(0), pl.num_programs(0)
    seq, dp = lax.axis_index("seq"), lax.axis_index("dp")
    core, xi = lax.rem(seq, 2), lax.div(seq, 2)
    depth = ff // 2 // nj

    @pl.when(step == 0)
    def _():
        rhs_ref[:rows, :d] = own_ref[...]
        rhs_ref[rows:, :d] = got_ref[...]
        rhs_ref[:, d:] = jnp.zeros((2 * rows, pad - d), BF)

    wide = lhs_ref.shape[1]
    acc_ref[pl.ds(pl.multiple_of(step * wide, wide), wide)] = tn(lhs_ref[...], rhs_ref[...])
    for c in (0, 1):

        @pl.when((core == c) & (step == steps - 1))
        def _():
            for x in (0, 1):
                for j in range(nj):
                    at = hidden_window(c, ff)[2] + j * depth
                    rel = (x ^ xi) * nj + (j ^ lax.rem(dp, nj))
                    value = acc_ref[at : at + depth, x * (pad - 640) : x * (pad - 640) + 640]
                    store_block(orders, rel, value.astype(BF), sent_ref, kept_ref)


def hidden_weights(lhs, own, got, ff, nj, orders):
    rows, d = own.shape
    width = lhs.shape[1]
    pad = -(-d // 128) * 128
    depth = ff // 2 // nj
    outs = [jax.ShapeDtypeStruct((nj, depth, 640), BF)] * 2
    full = lambda: pl.BlockSpec((nj, depth, 640), lambda *_: (0, 0, 0), pipeline_mode=pl.Buffered(1))
    return pl.pallas_call(
        functools.partial(hidden_weights_kernel, orders, ff, nj),
        grid=(width // CHUNK,),
        in_specs=[pl.BlockSpec((2 * rows, CHUNK), lambda i: (0, i)), whole(own), whole(got)],
        out_specs=[full(), full()],
        out_shape=outs,
        scratch_shapes=[pltpu.VMEM((2 * rows, pad), BF), pltpu.VMEM((width, pad), F32)],
        compiler_params=vmem(48),
        cost_estimate=cost(4 * rows * width * pad, lhs, own, got, *outs),
        name="hidden_weights",
    )(lhs, own, got)


def output_weights_kernel(s_ref, own_ref, got_ref, g_ref, send_ref, keep_ref, acc_ref):
    k, c = pl.program_id(0), pl.program_id(1)
    start = (k == 0) & (c == 0)
    for h, ref in enumerate((own_ref, got_ref)):
        total = tn(ref[0], g_ref[...])
        acc_ref[h] = jnp.where(start, total, acc_ref[h] + total)
    core = lax.rem(lax.axis_index("seq"), 2)
    half = keep_ref.shape[1]
    for mine in (0, 1):

        @pl.when((k == 1) & (c == pl.num_programs(1) - 1) & (core == mine))
        def _():
            for h in (0, 1):
                keep_ref[h] = acc_ref[h, mine * half : (mine + 1) * half]
                send_ref[h] = acc_ref[h, (1 - mine) * half : (2 - mine) * half].astype(BF)


def output_weights(place, own, got, g, rows):
    cells, _, width = own.shape
    d = g.shape[1]
    at = pl.BlockSpec((1, rows, width), lambda k, c, s: (c, s[0] ^ (2 * k), 0))
    shape = (2, width // 2, d)
    outs = [jax.ShapeDtypeStruct(shape, BF), jax.ShapeDtypeStruct(shape, F32)]
    return pl.pallas_call(
        output_weights_kernel,
        grid_spec=pltpu.PrefetchScalarGridSpec(
            num_scalar_prefetch=1, grid=(2, cells),
            in_specs=[at, at, pl.BlockSpec((rows, d), lambda k, c, s: (k * cells + c, 0))],
            out_specs=[pl.BlockSpec(shape, lambda *_: (0, 0, 0), pipeline_mode=pl.Buffered(1))] * 2,
            scratch_shapes=[pltpu.VMEM((2, width, d), F32)]),
        out_shape=outs,
        compiler_params=vmem(32),
        cost_estimate=cost(8 * cells * rows * width * d, own, got, g, *outs),
        name="output_weights",
    )(place, own, got, g)


def place_in(steps, rel, count):
    return sum(jnp.where(rel & step != 0, count >> (k + 1), 0) for k, step in enumerate(steps))


def project_weights_kernel(orders, ndp, half, lhs_ref, rhs_refs, out_ref, blocks_ref, acc_ref, block_ref):
    step, steps = pl.program_id(0), pl.num_programs(0)
    seq, dp = lax.axis_index("seq"), lax.axis_index("dp")
    xi, core = lax.div(seq, 2), lax.rem(seq, 2)
    m = lhs_ref.shape[1]
    lo = 0
    rows = pl.ds(pl.multiple_of(step * m, m), m)
    for ref in rhs_refs:
        wide = ref.shape[1]
        acc_ref[rows, lo : lo + wide] = tn(lhs_ref[...], ref[...])
        lo += wide
    acc_ref[rows, lo:] = jnp.zeros((m, acc_ref.shape[1] - lo), F32)

    @pl.when(step == steps - 1)
    def _():
        wide = acc_ref.shape[1] // ndp
        part = blocks_ref.shape[2] // 2
        full = half // part
        rest = half - full * part
        block_ref[rest:] = jnp.zeros((block_ref.shape[0] - rest, wide), F32)
        tall = out_ref.shape[1] // ndp
        for x in (0, 1):
            for j in range(ndp):
                cols = slice(j * wide, (j + 1) * wide)
                block_ref[:rest] = acc_ref[x * half + full * part : (x + 1) * half, cols]
                strip = out_ref[x ^ core, j * tall : (j + 1) * tall]
                for t, lo in enumerate(range(0, 2 * half, wide)):
                    hi = min(lo + wide, 2 * half)
                    block_ref[rest + t * tall : rest + (t + 1) * tall, : hi - lo] = strip[:, lo:hi]
                rel = (x ^ xi) * ndp + (j ^ dp)
                for n, steps_of in enumerate(orders):
                    if n < full:
                        value = acc_ref[x * half + n * part : x * half + (n + 1) * part, cols]
                    else:
                        value = block_ref[(n - full) * part : (n - full + 1) * part]
                    place = place_in(steps_of, rel, 2 * ndp)
                    blocks_ref[n // 2, place, n % 2 * part : (n % 2 + 1) * part] = value.astype(BF)


def project_weights(lhs, parts, width, out, ndp, orders):
    rows_in, d = lhs.shape
    m = 256
    steps = -(-d // m)
    wide = width // ndp
    third = -(-(d // 2 + -(-d // wide) * (out.shape[1] // ndp)) // 48) * 16
    block = (3, 2 * ndp, third, wide)
    n = len(parts)

    def kernel(lhs_ref, *refs):
        project_weights_kernel(orders, ndp, d // 2, lhs_ref, refs[:n], *refs[n:])

    return pl.pallas_call(
        kernel,
        grid=(steps,),
        in_specs=[pl.BlockSpec((rows_in, m), lambda i: (0, i))] + [whole(a) for a in (*parts, out)],
        out_specs=pl.BlockSpec(block, lambda *_: (0, 0, 0, 0), pipeline_mode=pl.Buffered(1)),
        out_shape=jax.ShapeDtypeStruct(block, BF),
        scratch_shapes=[
            pltpu.VMEM((steps * m, width), F32),
            pltpu.VMEM((3 * third - d // 2 // (third // 2) * (third // 2), wide), F32)],
        compiler_params=vmem(48),
        cost_estimate=cost(2 * rows_in * d * width, lhs, out),
        name="project_weights",
    )(lhs, *parts, out)


def flip(index, bit):
    return index + bit - 2 * bit * lax.rem(lax.div(index, bit), 2)


def quarter_of(pair, x, c, quarter, shift):
    lo = x * shift + c * quarter
    return pair[:, :, lo : lo + quarter]


def sum_kernel(
    ndp, orders, quarter, shift, in_ref, pair_ref, sums_ref, gain_ref,
    ga_hbm, gb_hbm, w_hbm, x0_hbm, x1_hbm, gm_hbm, block_ref,
    held_ref, shared_ref, hidden_ref, block_out, cells_out,
    acc, got, piece, core_out, core_in, pair_got, part_out, part_in, sums, sums_got,
    ga, gb, w, xs, gm, gf, gf_got, rows_out, out_sem, in_sem, here_sem,
):
    seq, dp = lax.axis_index("seq"), lax.axis_index("dp")
    core, xi = lax.rem(seq, 2), lax.div(seq, 2)
    count, third = in_ref.shape[1], in_ref.shape[2]
    dims = [1 << b for b in range(ndp.bit_length() - 1)]

    def to(axis, bit):
        return {"dp": flip(dp, bit) if axis == "dp" else dp, "seq": flip(seq, bit) if axis == "seq" else seq}

    partners = [to("seq", 1), to("seq", 2)] + [to("dp", b) for b in dims]
    here = [
        pltpu.make_async_copy(src, dst, here_sem.at[n])
        for n, (src, dst) in enumerate((
            (ga_hbm, ga), (gb_hbm, gb), (w_hbm, w), (x0_hbm, xs.at[0]), (x1_hbm, xs.at[1]), (gm_hbm, gm)))
    ]
    for c in here:
        c.start()
    barrier = pltpu.get_barrier_semaphore()
    for p in partners:
        pl.semaphore_signal(barrier, inc=1, device_id=p, device_id_type=pl.DeviceIdType.MESH)
    pl.semaphore_wait(barrier, len(partners))
    used = []

    def copy(src, dst, target, always=True):
        n = len(used)
        c = pltpu.make_async_remote_copy(
            src_ref=src, dst_ref=dst, send_sem=out_sem.at[n], recv_sem=in_sem.at[n], device_id=target,
            device_id_type=pl.DeviceIdType.MESH)
        used.append((c, always))
        return c

    part = third // 2
    steps = len(orders[0])
    flying = {}

    def start(i, h, k):
        half = count >> (k + 1)
        rows = pl.ds(h * part, part)
        src = (in_ref if k == 0 else acc).at[i, pl.ds(half, half), rows]
        c = copy(src, got.at[i, pl.ds(count - 2 * half, half), rows], to(*orders[2 * i + h][k]))
        c.start()
        flying[i, h] = c

    def finish(i, h, k):
        flying[i, h].wait_recv()
        half = count >> (k + 1)
        rows = slice(h * part, (h + 1) * part)
        for b in range(half):
            kept = in_ref[i, b, rows] if k == 0 else acc[i, b, rows]
            acc[i, b, rows] = (kept.astype(F32) + got[i, count - 2 * half + b, rows].astype(F32)).astype(BF)
        if k + 1 < steps:
            start(i, h, k + 1)

    for i in range(3):
        start(i, 0, 0)
    mine = core == lax.div(dp, ndp // 2)
    over_dp = copy(pair_ref, pair_got, to("dp", ndp // 2), False)
    over_core = copy(part_out, part_in, to("seq", 1), False)

    @pl.when(jnp.logical_not(mine))
    def _():
        over_dp.start()

    for c in here[:3]:
        c.wait()
    cells, block, d = x0_hbm.shape
    split = ga.shape[1]
    qkv_sums = [0.0, 0.0]
    for r in range(4 * cells):
        rows = slice(r * block, (r + 1) * block)
        a, b = ga[rows], gb[rows]
        gf[rows] = (nt(a, w[:, :split]) + nt(b, w[:, split:])).astype(BF)
        qkv_sums = [t + jnp.sum(v.astype(F32), axis=0, keepdims=True) for t, v in zip(qkv_sums, (a, b))]
    to_core = []
    for k in (1, 3):
        for c in range(cells):
            rows = pl.ds(pl.multiple_of((4 * c + (seq ^ k)) * block, block), block)
            to_core.append(copy(gf.at[rows], gf_got.at[rows], to("seq", 1)))
            to_core[-1].start()

    small = []
    small_order = [("seq", 2)] + [("dp", b) for b in dims] + [("seq", 1)]

    def small_step():
        n = len(small)
        if n:
            small[-1].wait_recv()
            if n < len(small_order):
                sums[n] = sums[n - 1] + sums_got[n - 1]
            else:
                shared_ref[0] = sums[n - 1]
                shared_ref[1] = sums_got[n - 1]
                return
        c = copy(sums.at[n], sums_got.at[n], to(*small_order[n]))
        c.start()
        small.append(c)

    for i in range(3):
        finish(i, 0, 0)
        start(i, 1, 0)
    for c in here[3:]:
        c.wait()
    for c in to_core:
        c.wait_recv()
    norm_sums = [0.0, 0.0]
    for k in (0, 1):
        for c in range(cells):
            rows = pl.ds(pl.multiple_of((4 * c + (seq ^ (2 * k))) * block, block), block)
            g = gf[rows].astype(F32) + gf_got[rows].astype(F32)
            n, rstd = block_norm(xs[k, c].astype(F32))
            mid = gm[(k * cells + c) * block : (k * cells + c + 1) * block]
            rows_out[k, c] = (mid + block_norm_back(g, n, rstd, gain_ref[...])).astype(BF)
            norm_sums = [t + jnp.sum(v, axis=0, keepdims=True) for t, v in zip(norm_sums, (g * n, g))]
    sums[0] = sums_ref[...]
    sums[0, 0:1, :d] = norm_sums[0]
    sums[0, 1:2, :d] = norm_sums[1]
    sums[0, 7:8, :split] = qkv_sums[0]
    sums[0, 7:8, split : w.shape[1]] = qkv_sums[1]
    small_step()
    for k in range(1, steps):
        for h in (0, 1):
            for i in range(3):
                finish(i, h, k - h)
        if k < 4:
            small_step()
    for i in range(3):
        finish(i, 1, steps - 1)

    for i in range(3):
        piece[i * third : (i + 1) * third] = acc[i, 0].astype(F32)
    for c in (0, 1):

        @pl.when(core == c)
        def _():
            core_out[...] = piece[(1 - c) * quarter : (2 - c) * quarter].astype(BF)

    swap_core = copy(core_out, core_in, to("seq", 1))
    swap_core.start()
    mine_cells = pl.ds(xi * cells, cells)
    back = [
        copy(block_ref.at[1], block_out.at[mine_cells], to("seq", 2)),
        copy(rows_out.at[1], cells_out.at[mine_cells], to("seq", 2)),
    ]
    keep = [
        pltpu.make_async_copy(src, dst.at[mine_cells], here_sem.at[len(here) + n])
        for n, (src, dst) in enumerate(((block_ref.at[0], block_out), (rows_out.at[0], cells_out)))
    ]
    for c in back + keep:
        c.start()
    swap_core.wait_recv()
    for c in (0, 1):

        @pl.when(core == c)
        def _():
            piece[(1 - c) * quarter : (2 - c) * quarter] = core_in[...].astype(F32)

    held_ref[0] = piece[...].astype(BF)

    ends = []
    far = dims[::-1]
    parts = 6
    rows_of = [pl.ds(i * (3 * third // parts), 3 * third // parts) for i in range(parts)]

    def share(i, k):
        n = 1 << k
        c = copy(held_ref.at[pl.ds(0, n), rows_of[i]], held_ref.at[pl.ds(n, n), rows_of[i]], to("dp", far[k]))
        c.start()
        return c

    first = share(0, 0)
    for i in range(parts):
        first.wait_recv()
        c = share(i, 1)
        if i + 1 < parts:
            first = share(i + 1, 0)
        for k in range(2, len(far)):
            c.wait_recv()
            c = share(i, k)
        ends.append(c)
        if i == 0:
            small_step()

    for x in (0, 1):
        for c in (0, 1):

            @pl.when(mine & (xi == x) & (core == c))
            def _():
                over_dp.wait_recv()
                total = pair_ref[...].astype(F32) + pair_got[...].astype(F32)
                hidden_ref[...] = quarter_of(total, x, c, quarter, shift)
                part_out[...] = quarter_of(total, x, 1 - c, quarter, shift).astype(BF)

    @pl.when(mine)
    def _():
        over_core.start()
        over_core.wait_send()

    @pl.when(jnp.logical_not(mine))
    def _():
        over_dp.wait_send()
        over_core.wait_recv()
        hidden_ref[...] = part_in[...].astype(F32)

    small_step()
    for c in keep:
        c.wait()
    for c in ends + back:
        c.wait_recv()
    for c, always in used:
        if always:
            c.wait_send()


def sum_and_gather(place, blocks, pair, sums, gain, ga, gb, w, x0, x1, gmiddle, block_rows, ndp, orders, quarter, shift):
    _, count, third, wide = blocks.shape
    _, depth, width = pair.shape
    cells, block, d = x0.shape
    in_vmem, hbm = pl.BlockSpec(memory_space=pltpu.VMEM), pl.BlockSpec(memory_space=pl.ANY)
    dims = ndp.bit_length() - 1
    copies = 6 * len(orders[0]) + 2 + (2 + dims) + 1 + 2 + 6 * dims + 2 * cells
    shape = jax.ShapeDtypeStruct
    both = (2 * cells, block, d)
    outs = [
        shape((ndp, 3 * third, wide), BF), shape((2, *sums.shape), F32), shape((2, depth, quarter), F32),
        shape(both, BF), shape(both, BF)]
    return pl.pallas_call(
        functools.partial(sum_kernel, ndp, orders, quarter, shift),
        in_specs=[in_vmem] * 4 + [hbm] * 7,
        out_specs=[in_vmem] * 3 + [hbm] * 2,
        out_shape=outs,
        scratch_shapes=[
            pltpu.VMEM((3, count // 2, third, wide), BF),
            pltpu.VMEM((3, count - 1, third, wide), BF),
            pltpu.VMEM((3 * third, wide), F32),
            pltpu.VMEM((quarter, wide), BF),
            pltpu.VMEM((quarter, wide), BF),
            pltpu.VMEM((2, depth, width), BF),
            pltpu.VMEM((2, depth, quarter), BF),
            pltpu.VMEM((2, depth, quarter), BF),
            pltpu.VMEM((2 + dims, *sums.shape), F32),
            pltpu.VMEM((2 + dims, *sums.shape), F32),
            pltpu.VMEM(ga.shape, BF),
            pltpu.VMEM(gb.shape, BF),
            pltpu.VMEM(w.shape, BF),
            pltpu.VMEM((2, *x0.shape), BF),
            pltpu.VMEM(gmiddle.shape, F32),
            pltpu.VMEM((4 * cells * block, d), BF),
            pltpu.VMEM((4 * cells * block, d), BF),
            pltpu.VMEM((2, *x0.shape), BF),
            pltpu.SemaphoreType.DMA((copies,)),
            pltpu.SemaphoreType.DMA((copies,)),
            pltpu.SemaphoreType.DMA((8,)),
        ],
        compiler_params=pltpu.CompilerParams(vmem_limit_bytes=60 << 20, collective_id=0, has_side_effects=True),
        cost_estimate=cost(0, blocks),
        name="sum_and_gather",
    )(blocks, pair, sums, gain, ga, gb, w, x0, x1, gmiddle, block_rows)


def sum_and_gather_by_steps(place, blocks, pair, sums, gain, ga, gb, w, x0, x1, gmiddle, block_rows, ndp, orders, quarter, shift):
    seq, dp = lax.axis_index("seq"), lax.axis_index("dp")
    core, xi = seq % 2, seq // 2
    cells, block, d = x0.shape
    gfirst, sums_qkv = project_back(ga, gb, w, block)
    gfirst_got = swap(gfirst.reshape(-1, block, d), "seq", 1).reshape(cells, 4 * block, d)
    cell_rows, sums1 = cells_back(place, gfirst.reshape(cells, 4 * block, d), gfirst_got, x0, x1, gmiddle, gain)
    sums = sums.at[:2, :d].set(sums1).at[7, : w.shape[1]].set(sums_qkv[0])
    count = blocks.shape[1]
    parts = []
    part = blocks.shape[2] // 2
    for n, steps in enumerate(orders):
        rows = blocks[n // 2, :, n % 2 * part : (n % 2 + 1) * part]
        sent, kept = rows[count // 2 :], rows[: count // 2]
        for k, (axis, bit) in enumerate(steps):
            got = swap(sent, axis, bit)
            if k + 1 < len(steps):
                sent, kept = halve(kept, got)
        parts.append(low(kept.astype(F32) + got.astype(F32))[0])
    piece = jnp.concatenate(parts, 0)
    halves = piece[: 2 * quarter].reshape(2, quarter, -1)
    ours, theirs = pick(halves, core, 0), swap(pick(halves, 1 - core, 0), "seq", 1)
    held = jnp.concatenate(
        [jnp.where(core == 0, ours, theirs), jnp.where(core == 0, theirs, ours), piece[2 * quarter :]], 0)[None]
    bits = [1 << b for b in range(ndp.bit_length() - 1)]
    for bit in bits[::-1]:
        held = jnp.concatenate([held, swap(held, "dp", bit)], 0)
    for axis, bit in [("seq", 2)] + [("dp", b) for b in bits]:
        sums = sums + swap(sums, axis, bit)
    nj = ndp // 2
    across = [(d * 4 + t, (d ^ nj) * 4 + t) for d in range(ndp) for t in range(4) if d // nj != t % 2]
    total = pair.astype(F32) + lax.ppermute(pair, ("dp", "seq"), across).astype(F32)
    parts = [
        jnp.where(xi == 0, quarter_of(total, 0, c, quarter, shift), quarter_of(total, 1, c, quarter, shift)) for c in (0, 1)]
    theirs = swap(low(jnp.where(core == 0, parts[1], parts[0])), "seq", 1).astype(F32)
    hidden = jnp.where(core == dp // nj, jnp.where(core == 0, parts[0], parts[1]), theirs)

    def both_cells(rows):
        own, got = rows[0], swap(rows[1], "seq", 2)
        return jnp.concatenate([jnp.where(xi == 0, own, got), jnp.where(xi == 0, got, own)], 0)

    return held, jnp.stack([sums, swap(sums, "seq", 1)]), hidden, both_cells(block_rows), both_cells(cell_rows)


def assemble_kernel(bits, tiles, held_ref, e_ref, qkv_ref, out_ref, q_ref, o_ref):
    ndp, _, wide = held_ref.shape
    quarter, d = out_ref.shape
    heads, head = e_ref.shape
    tall = o_ref.shape[0] // ndp
    dp = lax.axis_index("dp")
    for j in range(ndp):
        rel = dp ^ j
        slot = sum(jnp.where(rel & b != 0, 1 << k, 0) for k, b in enumerate(bits))
        block = held_ref[slot].astype(F32)
        for c in (0, 1):
            q_ref[c, :, j * wide : (j + 1) * wide] = block[c * quarter : (c + 1) * quarter]
        for t, lo in enumerate(range(0, d, wide)):
            hi = min(lo + wide, d)
            at = 2 * quarter + t * tall
            o_ref[j * tall : (j + 1) * tall, lo:hi] = block[at : at + tall, : hi - lo]
    for part in range(3):
        for c in (0, 1):
            row = jnp.concatenate([q_ref[c, :, 128 * t : 128 * t + 128] for t in tiles[part]], 1)
            lo = part * d + c * head
            qkv_ref[:, lo : lo + head] = nn(row.astype(BF), e_ref[...])
    for h in range(o_ref.shape[0] // 64):
        out_ref[h * HD : (h + 1) * HD] = o_ref[h * 64 : h * 64 + HD]


def assemble(held, e, quarter, d, bits, tiles):
    ndp, _, wide = held.shape
    outs = [jax.ShapeDtypeStruct((quarter, 3 * d), F32), jax.ShapeDtypeStruct((quarter, d), F32)]
    return pl.pallas_call(
        functools.partial(assemble_kernel, bits, tiles),
        in_specs=[pl.BlockSpec(memory_space=pltpu.VMEM)] * 2,
        out_specs=[pl.BlockSpec(memory_space=pltpu.VMEM)] * 2,
        out_shape=outs,
        scratch_shapes=[pltpu.VMEM((2, quarter, ndp * wide), F32), pltpu.VMEM((quarter // HD * 64, d), F32)],
        compiler_params=vmem(40),
        cost_estimate=cost(6 * 2 * quarter * e.size, held, e, *outs),
        name="assemble",
    )(held, e)


def low(value):
    return lax.optimization_barrier(value.astype(BF))


def after(value, *first):
    return lax.optimization_barrier((value, *first))[0]


def swap(value, axis, bit):
    return lax.ppermute(value, axis, [(i, i ^ bit) for i in range(lax.axis_size(axis))])


def swap_by_core(value, steps):
    ndp, nseq = lax.axis_size("dp"), lax.axis_size("seq")
    pairs = []
    for d in range(ndp):
        for s in range(nseq):
            axis, bit = steps[s % 2]
            e, t = (d, s ^ bit) if axis == "seq" else (d ^ bit, s)
            pairs.append((d * nseq + s, e * nseq + t))
    return lax.ppermute(value, ("dp", "seq"), pairs)


def pick(array, index, axis):
    return lax.dynamic_index_in_dim(array, index, axis, keepdims=False)


def one_hot(rows, cols, source):
    r = lax.broadcasted_iota(jnp.int32, (rows, cols), 0)
    return (r == source[None, :]).astype(BF)


def halve(kept, got):
    half = kept.shape[0] // 2
    total = kept.astype(F32) + got.astype(F32)
    return low(total[half:]), low(total[:half])


def per_device(
    cells, prefix_len, ln1_gain, ln1_bias, w_qkv, bias_q, bias_v, w_out, bias_out,
    ln2_gain, ln2_bias, w_up, bias_up, w_down, bias_down, cotangent,
):
    seq, ndp = lax.axis_size("seq"), lax.axis_size("dp")
    s, dp = lax.axis_index("seq"), lax.axis_index("dp")
    core, xi = s % 2, s // 2
    assert seq == 4
    pairs, block, D = cells.shape
    C = pairs // 2
    T = block * seq
    HH = H // 2
    WH = HH * 64
    half = D // 2
    quarter = D // 4
    FF = w_up.shape[1]
    nj = ndp // 2
    R = 2 * C * block
    row = lambda v: v.reshape(1, -1)
    place = s.reshape(1).astype(jnp.int32)

    def split_cells(a):
        return lax.dynamic_slice_in_dim(a, xi * C, C, 0), lax.dynamic_slice_in_dim(a, (1 - xi) * C, C, 0)

    x0, x_other = split_cells(cells)
    x1 = swap(x_other, "seq", 2)
    x0_got = swap(x0, "seq", 1)
    prefix = lax.dynamic_slice_in_dim(prefix_len, xi * C, C, 0)

    col = jnp.arange(WH)
    head_col = jnp.where(col % 64 < HD, core * half + (col // 64) * HD + col % 64, -1)
    w_parts = []
    for j in range(3):
        lo = j * D // 128 * 128
        hi = min(-(-(j + 1) * D // 128) * 128, 3 * D)
        e = one_hot(hi - lo, WH, jnp.where(head_col >= 0, head_col + j * D - lo, -1))
        w_parts.append(jnp.dot(w_qkv[:, lo:hi], e, preferred_element_type=F32).astype(BF))
    cut = FIRST * 128
    in_order = lambda parts: [p[..., :cut] for p in parts] + [p[..., cut:] for p in parts]
    w_own = jnp.concatenate(in_order(w_parts), 1)

    def pad_heads(v, ones):
        v = lax.dynamic_slice_in_dim(v, core * half, half, 0).reshape(HH, HD)
        return jnp.concatenate([v, jnp.full((HH, 3), ones, F32), jnp.zeros((HH, 5), F32)], 1).reshape(WH)

    bias_own = jnp.concatenate(in_order([pad_heads(bias_q, 0.0), pad_heads(jnp.zeros_like(bias_q), 1.0), pad_heads(bias_v, 1.0)]))
    wo = w_out.reshape(2, HH, HD, D)
    wo = jnp.concatenate([wo, jnp.zeros((2, HH, 64 - HD, D), BF)], 2).reshape(2, WH, D)
    wo = jnp.where(core == 0, wo, wo[::-1]).reshape(2 * WH, D)

    x1 = after(x1, wo, w_own)
    x1_got = swap(x1, "seq", 1)
    first, qkv = project(place, (x0, x0_got, x1, x1_got), row(ln1_gain), row(ln1_bias), w_own, row(bias_own))
    c0, c_other = split_cells(cotangent)
    c1 = swap(after(c_other, x1), "seq", 2)
    qkv, c1 = lax.optimization_barrier((qkv, c1))
    c_pair = jnp.concatenate([c0, c1], 0)
    c_got = swap(c_pair, "seq", 1)
    att, q_aug = attention_forward(qkv, prefix)
    att_got = swap(att, "seq", 1)
    middle, second = attention_output(place, att, att_got, x0, x1, wo, row(bias_out), row(ln2_gain), row(ln2_bias))
    blocks = lambda v: v.reshape(-1, block, v.shape[-1])
    rows_of = lambda v: v.reshape(-1, v.shape[-1])
    second_got = rows_of(swap(blocks(second), "seq", 1))
    cot, cot_got = rows_of(c_pair), rows_of(c_got)

    act, gpre, out_own, out_send, gs_own, gs_send, bias_up_sum = hidden_layer(
        second, second_got, cot, cot_got, w_up, row(bias_up), w_down.T, block)
    gs_got = rows_of(swap(blocks(gs_send), "seq", 1))
    out_got = rows_of(swap(blocks(out_send), "seq", 1))

    low_bits = [1 << b for b in range(nj.bit_length() - 1)]
    rest = low_bits[2:]

    def order(*names):
        n = {"x": ("seq", 2), "y": ("dp", 1), "z": ("dp", 2)}
        return [n[k] for k in names] + [("dp", b) for b in rest]

    def codes(steps, n):
        return [n if axis == "seq" else bit for axis, bit in steps]

    down_orders = (order("x", "z", "y"), order("y", "x", "z"))
    up_orders = (order("z", "x", "y"), order("y", "z", "x"))
    top = [("dp", nj)]
    q_orders = [order(*names) + top for names in ("xyz", "xyz", "yxz", "yxz", "zxy", "zyx")]

    def send(sent, orders, k):
        return swap_by_core(sent, (orders[0][k], orders[1][k]))

    d_sent, d_kept = hidden_weights(act, cot, cot_got, FF, nj, [codes(o, nj) for o in down_orders])
    d_got = send(d_sent, down_orders, 0)
    u_sent, u_kept = hidden_weights(gpre, second, second_got, FF, nj, [codes(o, nj) for o in up_orders])
    u_got = send(u_sent, up_orders, 0)

    gmiddle, gbranch, gatt, block_rows, sums2 = middle_back(
        after(gs_own, d_sent, u_sent), gs_got, out_own, out_got, middle, cot, wo, row(ln2_gain), row(bias_down), block // 2)
    gatt_got = swap(gatt, "seq", 1)
    o_send, o_keep = output_weights(place, att, att_got, gbranch, block)
    o_got = swap(o_send, "seq", 1)
    g_out = o_keep + o_got[::-1].astype(F32)

    shape = (2, C, block, 2 * WH)
    gatt, gatt_got = gatt.reshape(shape), gatt_got.reshape(shape)
    d_sent, d_kept = halve(d_kept, d_got)
    d_got = send(d_sent, down_orders, 1)
    g_first = attention_backward(qkv, q_aug, after(gatt, d_sent, g_out), gatt_got, att, prefix, 0, FIRST).reshape(C * T, -1)
    d_sent, d_kept = halve(d_kept, after(d_got, g_first))
    d_got = send(d_sent, down_orders, 2)
    u_sent, u_kept = halve(u_kept, after(u_got, d_sent))
    u_got = send(u_sent, up_orders, 1)
    g_rest = attention_backward(
        qkv, q_aug, after(gatt, d_sent, u_sent), gatt_got, att, prefix, FIRST, WH // 128).reshape(C * T, -1)
    u_sent, u_kept = halve(u_kept, after(u_got, g_rest))
    u_got = send(u_sent, up_orders, 2)
    q_blocks = project_weights(
        first.reshape(C * T, D), [g_first, after(g_rest, u_sent)], -(-3 * WH // (128 * 16)) * 128 * 16, g_out, ndp,
        [codes(o, ndp) for o in q_orders])
    for k in range(3, len(down_orders[0])):
        d_sent, d_kept = halve(d_kept, d_got)
        d_got = send(d_sent, down_orders, k)
        u_sent, u_kept = halve(u_kept, u_got)
        u_got = send(u_sent, up_orders, k)
    d_got, u_got, q_blocks = lax.optimization_barrier((d_got, u_got, q_blocks))
    pair = low(jnp.concatenate([d_kept, u_kept], 0).astype(F32) + jnp.concatenate([d_got, u_got], 0).astype(F32))
    ff_width = bias_up_sum.shape[1]
    sums = jnp.concatenate(
        [jnp.zeros((2, ff_width), F32), jnp.pad(sums2, ((0, 0), (0, ff_width - D))), bias_up_sum, jnp.zeros((1, ff_width), F32)], 0)

    bits = [1 << b for b in range(ndp.bit_length() - 1)]
    shift = half - (-(-D // 128) * 128 - 640)
    block_rows = block_rows.reshape(2, C, block, D)
    finish = sum_and_gather if ndp <= 8 else sum_and_gather_by_steps
    held, sums, hidden, block_out, grad_cells = finish(
        place, q_blocks, pair, sums, row(ln1_gain), g_first, g_rest, w_own, x0, x1, gmiddle, block_rows, ndp, q_orders,
        quarter, shift)
    total = sums[0, :6, :D] + sums[1, :6, :D]
    by_core = jnp.where(core == 0, sums[:, 6:], sums[::-1, 6:])
    pad_up = FF - ff_width
    g_bias_up = jnp.pad(by_core[0, 0], (0, pad_up)) + jnp.pad(by_core[1, 0], (pad_up, 0))
    more = WH - cut

    def column_sums(j):
        v = jnp.concatenate(
            [by_core[:, 1, j * cut : (j + 1) * cut], by_core[:, 1, 3 * cut + j * more : 3 * cut + (j + 1) * more]], 1)
        return v.reshape(2 * HH, 64)[:, :HD].reshape(D)

    shared = [total[0], total[1], column_sums(0), column_sums(2), total[2], total[3], total[4], total[5], g_bias_up]

    head_of = jnp.arange(half)
    e_out = (jnp.arange(WH)[:, None] == (head_of // HD * 64 + head_of % HD)[None, :]).astype(BF)
    n_pairs = WH // 128
    tiles = [[tile_of(part, p, n_pairs) for p in range(n_pairs)] for part in range(3)]
    final_qkv, final_out = assemble(held, e_out, quarter, D, bits[::-1], tiles)

    final_down, final_up = hidden[0], hidden[1].T

    return (
        block_out, grad_cells, shared[0], shared[1], final_qkv, shared[2], shared[3], final_out,
        shared[4], shared[5], shared[6], final_up, shared[8], final_down, shared[7],
    )


def solution(mesh):
    rows = P("dp", "seq", None)
    return jax.shard_map(
        per_device,
        mesh=mesh,
        in_specs=(rows, P("dp")) + (P(),) * 13 + (rows,),
        out_specs=(rows, rows, P(), P(), P("seq", None), P(), P(), P("seq", None), P(), P(), P(), P("seq", "dp"), P(), P("dp", "seq"), P()),
        check_vma=False,
    )
```
